128 devices in a mesh: seq: 32 (over z_hi, x, y), fsdp: 4 (over z_lo, core).
Axes of the slice: x: 4, y: 4, z: 4 (z_hi: 2, z_lo: 2; z = z_hi * 2 + z_lo), core: 2. Of those that a mesh axis runs over, the one named last changes fastest.
Arguments:
- hidden_in: bfloat16 [4, 16384, 640], P('fsdp', 'seq'), may hold values from -6 to 6
- cotangent: bfloat16 [4, 16384, 640], P('fsdp', 'seq'), may hold values from -6 to 6
- positions: int32 [4, 16384], P('fsdp', 'seq'), may hold values from 0 to 15871, as said below
- query_weight: bfloat16 [640, 1024], P('fsdp'), may hold values from -0.25 to 0.25
- key_weight: bfloat16 [640, 256], P('fsdp'), may hold values from -0.25 to 0.25
- value_weight: bfloat16 [640, 256], P('fsdp'), may hold values from -0.25 to 0.25
- output_weight: bfloat16 [1024, 640], P('fsdp'), may hold values from -0.1875 to 0.1875
- gate_weight: bfloat16 [640, 2048], P('fsdp'), may hold values from -0.25 to 0.25
- up_weight: bfloat16 [640, 2048], P('fsdp'), may hold values from -0.25 to 0.25
- down_weight: bfloat16 [2048, 640], P('fsdp'), may hold values from -0.125 to 0.125
- norm_in: bfloat16 [640], P('fsdp'), may hold values from 0.5 to 1.5
- norm_attn: bfloat16 [640], P('fsdp'), may hold values from 0.5 to 1.5
- norm_ffn_in: bfloat16 [640], P('fsdp'), may hold values from 0.5 to 1.5
- norm_ffn_out: bfloat16 [640], P('fsdp'), may hold values from 0.5 to 1.5
- norm_query: bfloat16 [256], P('fsdp'), may hold values from 0.25 to 1.75
- norm_key: bfloat16 [256], P('fsdp'), may hold values from 0.25 to 1.75
Outputs:
- layer_out: bfloat16 [4, 16384, 640], P('fsdp', 'seq')
- grad_in: bfloat16 [4, 16384, 640], P('fsdp', 'seq')
- grad_query: float32 [640, 1024], P('fsdp')
- grad_key: float32 [640, 256], P('fsdp')
- grad_value: float32 [640, 256], P('fsdp')
- grad_output: float32 [1024, 640], P('fsdp')
- grad_gate: float32 [640, 2048], P('fsdp')
- grad_up: float32 [640, 2048], P('fsdp')
- grad_down: float32 [2048, 640], P('fsdp')
- grad_norm_in: float32 [640], P('fsdp')
- grad_norm_attn: float32 [640], P('fsdp')
- grad_norm_ffn_in: float32 [640], P('fsdp')
- grad_norm_ffn_out: float32 [640], P('fsdp')
- grad_norm_query: float32 [256], P('fsdp')
- grad_norm_key: float32 [256], P('fsdp')
The draws below stay inside these ranges and needn't reach their ends.
Inputs may be any that keep to these rules, and one draw needn't show every extreme that they name: `positions`: within each sequence the offsets rise by one from token to token and restart at 0 where a document begins (token 0 begins one); one document begins within the first 512 tokens and spans exactly 15872 tokens.
All inputs are finite; a program needn't handle non-finite values.
Results may differ from the reference program's by a relative error of at most 0.03.
Values may be sent and summed in bfloat16 or wider, within the bound.
No kernel may reach another device: no remote copies, remote signals or barrier semaphores. Data moves between devices by JAX's collectives and lax.ppermute only.
A program may use at most 128 MiB of HBM per device.

```python
import jax
import jax.numpy as jnp
from jax import lax

D = 640
FF = 2048
H = 4
HD = 256
WINDOW = 512
TOK_DEV = 512
SEQS = 4
LENGTH = 16384


def draw_positions(key, part):
    key = jax.random.fold_in(key, 7)

    def draw_row(row_index):
        row_key = jax.random.fold_in(key, row_index)
        open_key, extra_key = jax.random.split(row_key, 2)
        token_index = jnp.arange(LENGTH, dtype=jnp.int32)
        opening = jax.random.randint(open_key, (), 1, TOK_DEV)
        closing = opening + LENGTH - TOK_DEV
        extra = jax.random.randint(extra_key, (LENGTH,), 0, 8) == 0
        outside = (token_index < opening) | (token_index > closing)
        edges = (token_index == opening) | (token_index == closing) | extra & outside
        edges = edges & (token_index > 0)
        starts = lax.cummax(jnp.where(edges, token_index, 0), axis=0)
        return token_index - starts
    return jax.vmap(draw_row)(jnp.arange(SEQS, dtype=jnp.int32))


def shard_levels(key, extent, shards, low, high):
    loudness = 1.0
    for position, parts in shards:
        heights = jax.random.uniform(jax.random.fold_in(jax.random.fold_in(key, 6), position), (parts,), jnp.float32, low / len(shards), high / len(shards))
        loudness = loudness * jnp.repeat(jnp.exp(heights), extent[position] // parts).reshape((-1,) + (1,) * (len(extent) - 1 - position))
    return loudness


def noise(key, extent, scale, limit, shards=(), held_as=jnp.bfloat16):
    values = scale * jax.random.normal(key, extent, jnp.float32)
    if shards:
        values = values * shard_levels(key, extent, shards, -0.22, 0.18)
    return jnp.clip(values, -limit, limit).astype(held_as)


def setup_inputs(seed: int = 0) -> dict:
    arg_keys = jax.random.split(jax.random.key(seed), 17)
    return {
        "hidden_in": noise(arg_keys[0], (SEQS, LENGTH, D), 1.0, 6.0, ((0, 4), (1, 32))),
        "cotangent": noise(arg_keys[1], (SEQS, LENGTH, D), 1.0, 6.0, ((0, 4), (1, 32))),
        "positions": draw_positions(jax.random.fold_in(arg_keys[16], 71), 0),
        "query_weight": noise(arg_keys[3], (D, H * HD), D ** -0.5, 0.25, ((0, 4),)),
        "key_weight": noise(arg_keys[4], (D, HD), D ** -0.5, 0.25, ((0, 4),)),
        "value_weight": noise(arg_keys[5], (D, HD), D ** -0.5, 0.25, ((0, 4),)),
        "output_weight": noise(arg_keys[6], (H * HD, D), (H * HD) ** -0.5, 0.1875, ((0, 4),)),
        "gate_weight": noise(arg_keys[7], (D, FF), D ** -0.5, 0.25, ((0, 4),)),
        "up_weight": noise(arg_keys[8], (D, FF), D ** -0.5, 0.25, ((0, 4),)),
        "down_weight": noise(arg_keys[9], (FF, D), FF ** -0.5, 0.125, ((0, 4),)),
        "norm_in": jnp.clip(1.0 + 0.1 * jax.random.normal(arg_keys[10], (D,), jnp.float32), 0.5, 1.5).astype(jnp.bfloat16),
        "norm_attn": jnp.clip(1.0 + 0.1 * jax.random.normal(arg_keys[11], (D,), jnp.float32), 0.5, 1.5).astype(jnp.bfloat16),
        "norm_ffn_in": jnp.clip(1.0 + 0.1 * jax.random.normal(arg_keys[12], (D,), jnp.float32), 0.5, 1.5).astype(jnp.bfloat16),
        "norm_ffn_out": jnp.clip(1.0 + 0.1 * jax.random.normal(arg_keys[13], (D,), jnp.float32), 0.5, 1.5).astype(jnp.bfloat16),
        "norm_query": jnp.clip(1.0 + 0.15 * jax.random.normal(arg_keys[14], (HD,), jnp.float32), 0.25, 1.75).astype(jnp.bfloat16),
        "norm_key": jnp.clip(1.0 + 0.15 * jax.random.normal(arg_keys[15], (HD,), jnp.float32), 0.25, 1.75).astype(jnp.bfloat16),
    }


epsilon = 1e-06
rope_base = 10000.0
masked_value = -1e+30

@jax.custom_vjp
def low(v):
    return lax.optimization_barrier(v.astype(jnp.bfloat16)).astype(jnp.float32)

@jax.custom_vjp
def low_back(v):
    return v

def low_keep(v):
    return (low(v), None)

def low_pass(kept, grad):
    return (grad,)

def back_keep(v):
    return (v, None)

def back_low(kept, grad):
    return (low(grad),)
low.defvjp(low_keep, low_pass)
low_back.defvjp(back_keep, back_low)

def norm_rows(values, gain):
    return values * lax.rsqrt(lax.optimization_barrier(jnp.mean(values * values, axis=-1, keepdims=True)) + epsilon) * gain

def rotate(values, offsets):
    half_width = HD // 2
    powers = jnp.arange(half_width, dtype=jnp.float32) * (2.0 / HD)
    angles = offsets.astype(jnp.float32)[:, None] * (rope_base ** (-powers))[None, :]
    cosine = jnp.cos(angles)[:, None, :]
    sine_part = jnp.sin(angles)[:, None, :]
    leading = values[..., :half_width]
    trailing = values[..., half_width:]
    return jnp.concatenate([leading * cosine - trailing * sine_part, trailing * cosine + leading * sine_part], axis=-1)

def layer(inputs, weights, offsets):
    query_weight, key_weight, value_weight, output_weight, gate_weight, up_weight, down_weight, norm_in, norm_attn, norm_ffn_in, norm_ffn_out, norm_query, norm_key = weights
    highest = lax.Precision.HIGHEST
    length = inputs.shape[0]
    normed = low(norm_rows(inputs, norm_in))
    query_proj = low_back(jnp.dot(normed, query_weight, precision=highest))
    key_proj = low_back(jnp.dot(normed, key_weight, precision=highest))
    values = low(low_back(jnp.dot(normed, value_weight, precision=highest)))
    queries = low(rotate(norm_rows(query_proj.reshape(length, H, HD), norm_query), offsets))
    keys = low(rotate(norm_rows(key_proj.reshape(length, 1, HD), norm_key), offsets)[:, 0])
    key_pad = jnp.concatenate([jnp.zeros((WINDOW, HD), jnp.float32), keys], axis=0)
    value_pad = jnp.concatenate([jnp.zeros((WINDOW, HD), jnp.float32), values], axis=0)

    def attend_block(index):
        start = index * WINDOW
        query_rows = lax.dynamic_slice_in_dim(queries, start, WINDOW, 0)
        key_rows = lax.dynamic_slice_in_dim(key_pad, start, 2 * WINDOW, 0)
        value_rows = lax.dynamic_slice_in_dim(value_pad, start, 2 * WINDOW, 0)
        block_offsets = lax.dynamic_slice_in_dim(offsets, start, WINDOW, 0)
        distance = jnp.arange(WINDOW, dtype=jnp.int32)[:, None] + WINDOW - jnp.arange(2 * WINDOW, dtype=jnp.int32)[None, :]
        visible = (distance >= 0) & (distance < WINDOW) & (distance <= block_offsets[:, None])
        scores = low_back(jnp.einsum('qhd,kd->hqk', query_rows, key_rows, precision=highest) * HD ** (-0.5))
        scores = jnp.where(visible[None], scores, masked_value)
        soft = jax.nn.softmax(scores, axis=-1)
        return jnp.einsum('hqk,kd->qhd', low(soft), value_rows, precision=highest)
    blocks = lax.map(jax.checkpoint(attend_block), jnp.arange(length // WINDOW, dtype=jnp.int32))
    attended = low_back(low(blocks.reshape(length, H * HD)))
    attn_out = low_back(jnp.dot(attended, output_weight, precision=highest))
    middle = inputs + norm_rows(attn_out, norm_attn)
    ffn_in = low(norm_rows(middle, norm_ffn_in))
    gate_proj = low_back(jnp.dot(ffn_in, gate_weight, precision=highest))
    upward = low_back(jnp.dot(ffn_in, up_weight, precision=highest))
    hidden = low(jax.nn.gelu(gate_proj, approximate=True) * upward)
    ffn_out = low_back(jnp.dot(hidden, down_weight, precision=highest))
    return middle + norm_rows(ffn_out, norm_ffn_out)

def reference(hidden_in, cotangent, positions, query_weight, key_weight, value_weight, output_weight, gate_weight, up_weight, down_weight, norm_in, norm_attn, norm_ffn_in, norm_ffn_out, norm_query, norm_key):
    weights = tuple((tensor.astype(jnp.float32) for tensor in (query_weight, key_weight, value_weight, output_weight, gate_weight, up_weight, down_weight, norm_in, norm_attn, norm_ffn_in, norm_ffn_out, norm_query, norm_key)))

    def per_sequence(totals, items):
        inputs, offsets, upstream = items

        def forward(inputs_f, weights_f):
            return layer(inputs_f, weights_f, offsets)
        output, pullback = jax.vjp(forward, inputs.astype(jnp.float32), weights)
        input_grad, weight_grads = pullback(upstream.astype(jnp.float32))
        totals = jax.tree.map(jnp.add, totals, weight_grads)
        return (totals, (output.astype(jnp.bfloat16), input_grad.astype(jnp.bfloat16)))
    zeros = tuple((jnp.zeros(tensor.shape, jnp.float32) for tensor in weights))
    totals, (outputs, input_grads) = lax.scan(per_sequence, zeros, (hidden_in, positions, cotangent))
    return (outputs, input_grads, totals[0], totals[1], totals[2], totals[3], totals[4], totals[5], totals[6], totals[7], totals[8], totals[9], totals[10], totals[11], totals[12])
```

```python
import jax
import jax.numpy as jnp
from jax import lax
from jax.sharding import PartitionSpec as P

WINDOW = 512
epsilon = 1e-06
rope_base = 10000.0
masked_value = -1e30
bf16 = jnp.bfloat16
f32 = jnp.float32


def seq_index(z, x, y):
    return (z % 2 * 4 + x % 4) * 4 + y % 4


def along_xy(dx, dy):
    return [
        (seq_index(z, x, y), seq_index(z, x + dx, y + dy))
        for z in range(2)
        for x in range(4)
        for y in range(4)
    ]


def along_z(step):
    pairs = []
    for s in range(32):
        for f in range(4):
            z = s // 16 * 2 + f // 2
            t = step(z)
            pairs.append((s * 4 + f, (t // 2 * 16 + s % 16) * 4 + t % 2 * 2 + f % 2))
    return pairs


def swap_core(value):
    return lax.ppermute(value, "fsdp", [(0, 1), (1, 0), (2, 3), (3, 2)])


def swap_near(value):
    return lax.ppermute(value, "fsdp", [(0, 2), (1, 3), (2, 0), (3, 1)])


def swap_far(value):
    return lax.ppermute(value, ("seq", "fsdp"), along_z(lambda z: 3 - z))


def swap_hi(value):
    return lax.ppermute(value, "seq", [(s, (s + 16) % 32) for s in range(32)])


def move_x(value, d):
    return lax.ppermute(value, "seq", along_xy(d, 0))


def move_y(value, d):
    return lax.ppermute(value, "seq", along_xy(0, d))


def shifted(value, steps):
    first, last = (max(0, -steps), min(32, 32 - steps))
    return lax.ppermute(value, "seq", [(source, source + steps) for source in range(first, last)])


def pick(value, index, axis):
    return lax.dynamic_index_in_dim(value, index, axis, keepdims=False)


def total(parts):
    whole = parts[0].astype(f32)
    for part in parts[1:]:
        whole = whole + part.astype(f32)
    return whole.astype(bf16)


def in_order(pieces, me, sign):
    stack = jnp.stack(pieces)
    return jnp.stack([pick(stack, (sign * (me - j)) % 4, 0) for j in range(4)])


def reduce_group(buf, x, y, z_lo, core):
    rows = buf.shape[2]
    got = swap_core(pick(buf, 1 - core, 1))
    half = total([pick(buf, core, 1), got]).reshape(2, 2, 4, 4, rows // 32, 128)
    a, b = half[:, 0], half[:, 1]
    steps = (1, 3, 2)
    from_a = [move_x(pick(a, (x + d) % 4, 1), d) for d in steps]
    from_b = [move_y(pick(b, (y + d) % 4, 1), d) for d in steps]
    a = total([pick(a, x, 1)] + from_a)
    b = total([pick(b, y, 1)] + from_b)
    from_a = [move_y(pick(a, (y + d) % 4, 1), d) for d in steps]
    from_b = [move_x(pick(b, (x + d) % 4, 1), d) for d in steps]
    a = total([pick(a, y, 1)] + from_a)
    b = total([pick(b, x, 1)] + from_b)
    both = jnp.stack([a, b], axis=1)
    mine = pick(both, z_lo, 0)
    other = pick(both, 1 - z_lo, 0)
    both = total([mine, swap_near(other), swap_far(other), swap_hi(mine)])
    a, b = both[0], both[1]
    a = in_order([a] + [move_y(a, d) for d in (1, 2, 3)], y, 1)
    b = in_order([b] + [move_x(b, d) for d in (1, 2, 3)], x, 1)
    a = in_order([a] + [move_x(a, d) for d in (1, 2, 3)], x, 1)
    b = in_order([b] + [move_y(b, d) for d in (1, 2, 3)], y, 1)
    return jnp.stack([a, b]).reshape(rows, 128)


def blocks_of(grad):
    r, c = grad.shape[0] // 4, grad.shape[1]
    return grad.reshape(4, r, c // 128, 128).transpose(0, 2, 1, 3).reshape(4, r * c // 128, 128)


def from_blocks(flat, r, c):
    return flat.reshape(c // 128, r, 128).transpose(1, 0, 2).reshape(r, c).astype(f32)


def norm_rows(values, gain):
    return values * lax.rsqrt(jnp.mean(values * values, axis=-1, keepdims=True) + epsilon) * gain


def turn_pairs(values, cosine, sine_part):
    half_width = values.shape[-1] // 2
    leading = values[..., :half_width]
    trailing = values[..., half_width:]
    return jnp.concatenate(
        [leading * cosine - trailing * sine_part, trailing * cosine + leading * sine_part], axis=-1
    )


def dot(a, b, dims):
    return lax.dot_general(a, b, (dims, ((), ())), preferred_element_type=f32)


def body(
    hidden_in,
    cotangent,
    positions,
    query_weight,
    key_weight,
    value_weight,
    output_weight,
    gate_weight,
    up_weight,
    down_weight,
    norm_in,
    norm_attn,
    norm_ffn_in,
    norm_ffn_out,
    norm_query,
    norm_key,
):
    s = lax.axis_index("seq")
    f = lax.axis_index("fsdp")
    x, y, z_lo, core = s // 4 % 4, s % 4, f // 2, f % 2
    gains = jnp.concatenate(
        [norm_in, norm_attn, norm_ffn_in, norm_ffn_out, norm_query, norm_key]
    )
    gains = jnp.pad(gains, (0, 8 * 512 - gains.shape[0])).reshape(8, 512)
    kvg = jnp.concatenate([jnp.concatenate([key_weight, value_weight], axis=1), gains], axis=0)

    def everywhere(own, swap):
        partner = swap(own)
        sibling = swap_core(own)
        diagonal = swap_core(partner)
        out = []
        for j in range(4):
            low = jnp.where(j % 2 == core, own, sibling)
            high = jnp.where(j % 2 == core, partner, diagonal)
            out.append(jnp.where(j // 2 == z_lo, low, high))
        return out

    query_full = jnp.concatenate(everywhere(query_weight, swap_near))
    kvg_parts = everywhere(kvg, swap_far)
    halo = shifted(hidden_in[0], 1)
    output_full = jnp.concatenate(everywhere(output_weight, swap_near))
    gate_full = jnp.concatenate(everywhere(gate_weight, swap_near))
    upward_full = jnp.concatenate(everywhere(up_weight, swap_far))
    down_full = jnp.concatenate(everywhere(down_weight, swap_far))
    kv_full = jnp.concatenate([part[:160] for part in kvg_parts])
    gain_rows = jnp.stack([part[160:162] for part in kvg_parts]).reshape(4, 1024).astype(f32)
    gain_in, gain_attn, gain_ffn_in, gain_ffn_out = [
        gain_rows[:, 160 * k : 160 * (k + 1)].reshape(640) for k in range(4)
    ]
    gain_query, gain_key = [
        gain_rows[:, 640 + 64 * k : 704 + 64 * k].reshape(256) for k in range(2)
    ]

    inputs = hidden_in[0].astype(f32)
    offsets = positions[0]
    tokens = inputs.shape[0]
    head_width = 256
    heads = 4
    half_width = head_width // 2
    scale = head_width ** (-0.5)
    powers = jnp.arange(half_width, dtype=f32) * (2.0 / head_width)
    row = jnp.arange(tokens, dtype=jnp.int32)
    offsets_all = jnp.concatenate([offsets[0] - tokens + row, offsets])
    angles = offsets_all.astype(f32)[:, None] * (rope_base ** (-powers))[None, :]
    cosine = jnp.cos(angles)[:, None, :]
    sine_part = jnp.sin(angles)[:, None, :]
    inputs_all = jnp.concatenate([halo, hidden_in[0]]).astype(f32)
    normed_f, pull_in = jax.vjp(norm_rows, inputs_all, gain_in)
    normed_all = normed_f.astype(bf16)
    normed = normed_all[tokens:]
    query_proj = dot(normed, query_full, ((1,), (0,)))
    kv_proj = dot(normed_all, kv_full, ((1,), (0,)))
    key_proj = kv_proj[:, :head_width]
    values_all = kv_proj[:, head_width:].astype(bf16)

    def prepare(projected, gain, cosine, sine_part):
        return turn_pairs(
            norm_rows(projected.reshape(projected.shape[0], -1, head_width), gain),
            cosine,
            sine_part,
        )

    queries_f, pull_query = jax.vjp(
        lambda p, g: prepare(p, g, cosine[tokens:], sine_part[tokens:]), query_proj, gain_query
    )
    keys_f, pull_key = jax.vjp(
        lambda p, g: prepare(p, g, cosine, sine_part), key_proj, gain_key
    )
    queries = queries_f.astype(bf16)
    keys_all = keys_f[:, 0].astype(bf16)
    distance = row[:, None] + tokens - jnp.arange(2 * tokens, dtype=jnp.int32)[None, :]
    visible = (distance >= 0) & (distance < WINDOW) & (distance <= offsets[:, None])
    raw_scores = jnp.einsum("thd,kd->htk", queries, keys_all, preferred_element_type=f32) * scale
    masked = jnp.where(visible[None], raw_scores, masked_value)
    top_score = jnp.max(masked, axis=-1, keepdims=True)
    exponent = jnp.exp(masked - top_score)
    probs = exponent / jnp.sum(exponent, axis=-1, keepdims=True)
    probs_low = probs.astype(bf16)
    attended = jnp.einsum("htk,kd->thd", probs_low, values_all, preferred_element_type=f32)
    attended = attended.reshape(tokens, heads * head_width).astype(bf16)
    attn_out = dot(attended, output_full, ((1,), (0,)))

    def post_attention(out_value, resid_in, gain_out, gain_next):
        middle_value = resid_in + norm_rows(out_value, gain_out)
        return (middle_value, norm_rows(middle_value, gain_next))

    (middle, ffn_in_f), pull_middle = jax.vjp(
        post_attention, attn_out, inputs, gain_attn, gain_ffn_in
    )
    ffn_in = ffn_in_f.astype(bf16)
    gate_proj = dot(ffn_in, gate_full, ((1,), (0,)))
    upward = dot(ffn_in, upward_full, ((1,), (0,)))

    def activate(gate_value, up_value):
        return jax.nn.gelu(gate_value, approximate=True) * up_value

    hidden_f, pull_act = jax.vjp(activate, gate_proj, upward)
    hidden = hidden_f.astype(bf16)
    ffn_out = dot(hidden, down_full, ((1,), (0,)))

    def finish(ffn_value, middle_value, gain_last):
        return middle_value + norm_rows(ffn_value, gain_last)

    layer_out, pull_out = jax.vjp(finish, ffn_out, middle, gain_ffn_out)
    upstream = cotangent[0].astype(f32)
    back_ffn_out, back_middle_a, grad_gain_ffn_out = pull_out(upstream)
    back_ffn_low = back_ffn_out.astype(bf16)
    grad_down = dot(hidden, back_ffn_low, ((0,), (0,))).astype(bf16)
    back_hidden = dot(back_ffn_low, down_full, ((1,), (1,)))
    back_gate, back_upward = pull_act(back_hidden)
    back_gate_low = back_gate.astype(bf16)
    back_up_low = back_upward.astype(bf16)
    grad_gate = dot(ffn_in, back_gate_low, ((0,), (0,))).astype(bf16)
    grad_up = dot(ffn_in, back_up_low, ((0,), (0,))).astype(bf16)
    ffn_buf = jnp.concatenate([blocks_of(g) for g in (grad_gate, grad_up, grad_down)], axis=1)
    ffn_total = reduce_group(ffn_buf.reshape(2, 2, -1, 128), x, y, z_lo, core)

    back_ffn_in = dot(back_gate_low, gate_full, ((1,), (1,)))
    back_ffn_in = back_ffn_in + dot(back_up_low, upward_full, ((1,), (1,)))
    back_attn_out, back_inputs_a, grad_gain_attn, grad_gain_ffn_in = pull_middle(
        (back_middle_a, back_ffn_in)
    )
    back_attn_low = back_attn_out.astype(bf16)
    grad_output = dot(attended, back_attn_low, ((0,), (0,))).astype(bf16)
    back_attended = dot(back_attn_low, output_full, ((1,), (1,)))
    back_attended = back_attended.reshape(tokens, heads, head_width).astype(bf16)
    back_probs = jnp.einsum("thd,kd->htk", back_attended, values_all, preferred_element_type=f32)
    inner = jnp.sum(probs * back_probs, axis=-1, keepdims=True)
    back_scores = (probs * (back_probs - inner)).astype(bf16)
    back_queries = (
        jnp.einsum("htk,kd->thd", back_scores, keys_all, preferred_element_type=f32) * scale
    )
    back_keys_all = (
        jnp.einsum("htk,thd->kd", back_scores, queries, preferred_element_type=f32) * scale
    )
    back_values_all = jnp.einsum(
        "htk,thd->kd", probs_low, back_attended, preferred_element_type=f32
    )
    back_key_proj, grad_gain_key = pull_key(back_keys_all[:, None, :])
    back_kv_low = jnp.concatenate([back_key_proj, back_values_all], axis=1).astype(bf16)
    back_normed_kv = dot(back_kv_low, kv_full, ((1,), (1,)))
    returned = shifted(back_normed_kv[:tokens].astype(bf16), -1)
    back_query_proj, grad_gain_query = pull_query(back_queries)
    back_query_low = back_query_proj.astype(bf16)
    grad_query = dot(normed, back_query_low, ((0,), (0,))).astype(bf16)
    grad_kv = dot(normed_all, back_kv_low, ((0,), (0,))).astype(bf16)
    back_normed = back_normed_kv[tokens:] + dot(back_query_low, query_full, ((1,), (1,)))
    _, grad_gain_in = pull_in(jnp.concatenate([back_normed_kv[:tokens], back_normed]))
    gain_grads = jnp.concatenate(
        [
            g.reshape(4, -1)
            for g in (
                grad_gain_in,
                grad_gain_attn,
                grad_gain_ffn_in,
                grad_gain_ffn_out,
                grad_gain_query,
                grad_gain_key,
            )
        ],
        axis=1,
    ).astype(bf16)
    gain_grads = jnp.pad(gain_grads, ((0, 0), (0, 128 * 128 - 768))).reshape(4, 128, 128)
    attn_buf = jnp.concatenate(
        [blocks_of(g) for g in (grad_query, grad_kv, grad_output)] + [gain_grads], axis=1
    )
    attn_total = reduce_group(attn_buf.reshape(2, 2, -1, 128), x, y, z_lo, core)
    _, pull_own = jax.vjp(norm_rows, inputs, gain_in)
    back_inputs_b, _ = pull_own(back_normed + returned.astype(f32))
    grad_in = (back_inputs_a + back_inputs_b).astype(bf16)

    gain_total = attn_total[3200:3206].reshape(768).astype(f32)
    kv_total = from_blocks(attn_total[1280:1920], 160, 512)
    return (
        layer_out.astype(bf16)[None],
        grad_in[None],
        from_blocks(attn_total[:1280], 160, 1024),
        kv_total[:, :256],
        kv_total[:, 256:],
        from_blocks(attn_total[1920:3200], 256, 640),
        from_blocks(ffn_total[:2560], 160, 2048),
        from_blocks(ffn_total[2560:5120], 160, 2048),
        from_blocks(ffn_total[5120:], 512, 640),
        gain_total[:160],
        gain_total[160:320],
        gain_total[320:480],
        gain_total[480:640],
        gain_total[640:704],
        gain_total[704:768],
    )


def solution(mesh):
    three = P("fsdp", "seq", None)
    two = P("fsdp", None)
    one = P("fsdp")
    return jax.shard_map(
        body,
        mesh=mesh,
        in_specs=(three, three, P("fsdp", "seq")) + (two,) * 7 + (one,) * 6,
        out_specs=(three, three) + (two,) * 7 + (one,) * 6,
        check_vma=False,
    )
```

```python
import jax
import jax.numpy as jnp
from jax import lax
from jax.experimental import pallas as pl
from jax.experimental.pallas import tpu as pltpu
from jax.sharding import PartitionSpec as P

WINDOW = 512
epsilon = 1e-06
rope_base = 10000.0
masked_value = -1e30
bf16 = jnp.bfloat16
f32 = jnp.float32

rows_out = ((1,), (0,))
rows_both = ((1,), (1,))
cols_both = ((0,), (0,))


def dot(a, b, dims=rows_out):
    return lax.dot_general(a, b, (dims, ((), ())), preferred_element_type=f32)


def spec(*shape):
    return jax.ShapeDtypeStruct(shape[:-1], shape[-1])


def whole():
    return pl.BlockSpec(memory_space=pltpu.VMEM)


def params(mib):
    return pltpu.CompilerParams(vmem_limit_bytes=mib * 1024 * 1024)


def cost(flops, moved, exps=0):
    return pl.CostEstimate(flops=flops, bytes_accessed=moved, transcendentals=exps)


def inverse_rms(v):
    return lax.rsqrt(jnp.mean(v * v, axis=-1, keepdims=True) + epsilon)


def norm_back(v, r, gain, e):
    scaled = gain * e
    return r * scaled - v * (r * r * r * jnp.mean(v * scaled, axis=-1, keepdims=True))


def turn(v, cosine, sine):
    a, b = v[:, :128], v[:, 128:]
    return jnp.concatenate([a * cosine - b * sine, b * cosine + a * sine], axis=1)


def turn_back(v, cosine, sine):
    a, b = v[:, :128], v[:, 128:]
    return jnp.concatenate([a * cosine + b * sine, b * cosine - a * sine], axis=1)


def assemble(pieces, into, place, semaphores, first):
    rows = into.shape[0] // 4
    copies = []
    for r in range(4):
        at = pl.ds(pl.multiple_of((place ^ r) * rows, rows), rows)
        copies.append(
            pltpu.make_async_copy(
                pieces[r].at[pl.ds(0, rows), :], into.at[at, :], semaphores.at[first + r]
            )
        )
    for copy in copies:
        copy.start()
    return copies


def project_kernel(
    place,
    halo,
    own,
    gains,
    head_gains,
    q0,
    q1,
    q2,
    q3,
    kv0,
    kv1,
    kv2,
    kv3,
    cosine,
    sine,
    normed,
    q,
    k,
    v,
    q_proj,
    k_proj,
    wq,
    wkv,
    semaphores,
):
    i = pl.program_id(0)

    @pl.when(i == 0)
    def _():
        copies = assemble((kv0, kv1, kv2, kv3), wkv, place[0], semaphores, 0)
        copies += assemble((q0, q1, q2, q3), wq, place[0], semaphores, 4)
        for copy in copies:
            copy.wait()

    x = jnp.where(i < 2, halo[...], own[...]).astype(f32)
    n = (x * inverse_rms(x) * gains[0:1]).astype(bf16)
    normed[...] = n
    c, s = cosine[...], sine[...]
    kv = dot(n, wkv[...])
    kp = kv[:, :256]
    k_proj[...] = kp
    v[...] = kv[:, 256:].astype(bf16)
    k[...] = turn(kp * inverse_rms(kp) * head_gains[1:2], c, s).astype(bf16)

    @pl.when(i >= 2)
    def _():
        for h in range(4):
            cols = slice(256 * h, 256 * h + 256)
            qp = dot(n, wq[:, cols])
            q_proj[:, cols] = qp
            q[:, cols] = turn(qp * inverse_rms(qp) * head_gains[0:1], c, s).astype(bf16)


def project(place, halo, own, gains, head_gains, q_shares, kv_shares, cosine, sine):
    late = lambda i: (jnp.maximum(i - 2, 0), 0)
    row = lambda i: (i, 0)
    fixed = lambda i: (0, 0)
    return pl.pallas_call(
        project_kernel,
        name="project",
        grid=(4,),
        in_specs=[
            pl.BlockSpec(memory_space=pltpu.SMEM),
            pl.BlockSpec((256, 640), lambda i: (jnp.minimum(i, 1), 0)),
            pl.BlockSpec((256, 640), late),
            pl.BlockSpec((8, 640), fixed),
            pl.BlockSpec((8, 256), fixed),
        ]
        + [pl.BlockSpec(memory_space=pl.ANY)] * 8
        + [pl.BlockSpec((256, 128), row)] * 2,
        out_specs=[
            pl.BlockSpec((256, 640), row),
            pl.BlockSpec((256, 1024), late),
            pl.BlockSpec((256, 256), row),
            pl.BlockSpec((256, 256), row),
            pl.BlockSpec((256, 1024), late),
            pl.BlockSpec((256, 256), row),
        ],
        out_shape=[
            spec(1024, 640, bf16),
            spec(512, 1024, bf16),
            spec(1024, 256, bf16),
            spec(1024, 256, bf16),
            spec(512, 1024, f32),
            spec(1024, 256, f32),
        ],
        scratch_shapes=[
            pltpu.VMEM((640, 1024), bf16),
            pltpu.VMEM((640, 512), bf16),
            pltpu.SemaphoreType.DMA((8,)),
        ],
        compiler_params=params(20),
        cost_estimate=cost(1_350_000_000, 9_000_000),
    )(place, halo, own, gains, head_gains, *q_shares, *kv_shares, cosine, sine)


def visible_keys(offsets):
    distance = (
        lax.broadcasted_iota(jnp.int32, (256, 768), 0)
        + 512
        - lax.broadcasted_iota(jnp.int32, (256, 768), 1)
    )
    return (distance >= 0) & (distance < WINDOW) & (distance <= offsets)


def attend_kernel(q, k, v, offsets, attended, level):
    t = pl.program_id(0)
    near = pl.ds(pl.multiple_of(t * 256, 256), 768)
    keys, values = k[near, :], v[near, :]
    visible = visible_keys(offsets[...])
    for h in range(4):
        cols = slice(256 * h, 256 * h + 256)
        scores = jnp.where(visible, dot(q[:, cols], keys, rows_both) * 0.0625, masked_value)
        top = jnp.max(scores, axis=-1, keepdims=True)
        e = jnp.exp(scores - top)
        total = jnp.sum(e, axis=-1, keepdims=True)
        level[h] = top + jnp.log(total)
        probs = (e * (1.0 / total)).astype(bf16)
        attended[:, cols] = dot(probs, values).astype(bf16)


def attend(q, k, v, offsets):
    row = lambda i: (i, 0)
    fixed = lambda i: (0, 0)
    return pl.pallas_call(
        attend_kernel,
        name="attend",
        grid=(2,),
        in_specs=[
            pl.BlockSpec((256, 1024), row),
            pl.BlockSpec((1024, 256), fixed),
            pl.BlockSpec((1024, 256), fixed),
            pl.BlockSpec((256, 1), row),
        ],
        out_specs=[
            pl.BlockSpec((256, 1024), row),
            pl.BlockSpec((4, 256, 1), lambda i: (0, i, 0)),
        ],
        out_shape=[spec(512, 1024, bf16), spec(4, 512, 1, f32)],
        compiler_params=params(20),
        cost_estimate=cost(1_700_000_000, 4_000_000, 2_000_000),
    )(q, k, v, offsets)


def middle_kernel(
    place,
    x_ref,
    attended,
    upstream,
    gains,
    o0,
    o1,
    o2,
    o3,
    g0,
    g1,
    g2,
    g3,
    u0,
    u1,
    u2,
    u3,
    d0,
    d1,
    d2,
    d3,
    layer_out,
    back_middle,
    back_attn,
    back_attended,
    gain_grads,
    grads,
    ffn_in,
    kept_a,
    kept_b,
    hidden,
    back_out,
    in_turned,
    out_turned,
    total,
    wo,
    wg,
    wu,
    wd,
    semaphores,
):
    output_copies = assemble((o0, o1, o2, o3), wo, place[0], semaphores, 0)
    gate_copies = assemble((g0, g1, g2, g3), wg, place[0], semaphores, 4)
    up_copies = assemble((u0, u1, u2, u3), wu, place[0], semaphores, 8)
    down_copies = assemble((d0, d1, d2, d3), wd, place[0], semaphores, 12)
    for copy in output_copies:
        copy.wait()
    g_attn, g_in, g_out = gains[1:2], gains[2:3], gains[3:4]
    ao = dot(attended[...], wo[...])
    r1 = inverse_rms(ao)
    mid = x_ref[...].astype(f32) + ao * r1 * g_attn
    r2 = inverse_rms(mid)
    ffn_in[...] = (mid * r2 * g_in).astype(bf16)
    total[...] = jnp.zeros_like(total)
    for copy in gate_copies + up_copies + down_copies:
        copy.wait()

    @pl.loop(0, 8)
    def _(j):
        cols = pl.ds(pl.multiple_of(j * 256, 256), 256)
        u = dot(ffn_in[...], wg[:, cols])
        up = dot(ffn_in[...], wu[:, cols])
        root = 0.7978845608028654
        t = jnp.tanh(root * (u + 0.044715 * (u * u * u)))
        half = 0.5 * (1.0 + t)
        act = u * half
        slope = half + (0.5 * root) * u * (1.0 - t * t) * (1.0 + (3 * 0.044715) * (u * u))
        h = (act * up).astype(bf16)
        hidden[:, cols] = h
        kept_a[:, cols] = act
        kept_b[:, cols] = up * slope
        total[...] += dot(h, wd[cols, :])

    fo = total[...]
    r3 = inverse_rms(fo)
    layer_out[...] = (mid + fo * r3 * g_out).astype(bf16)
    g = upstream[...].astype(f32)
    gain_grads[2:3] = jnp.sum(fo * r3 * g, axis=0, keepdims=True)
    bfo = norm_back(fo, r3, g_out, g)
    back_out[...] = bfo.astype(bf16)
    out_turned[...] = bfo.T.astype(bf16)
    in_turned[...] = (mid * r2 * g_in).T.astype(bf16)
    total[...] = jnp.zeros_like(total)

    @pl.loop(0, 8)
    def _(j):
        cols = pl.ds(pl.multiple_of(j * 256, 256), 256)
        bh = dot(back_out[...], wd[cols, :], rows_both)
        bu = (bh * kept_a[:, cols]).astype(bf16)
        bg = (bh * kept_b[:, cols]).astype(bf16)
        total[...] += dot(bg, wg[:, cols], rows_both) + dot(bu, wu[:, cols], rows_both)
        for base, left, right in (
            (0, in_turned, bg),
            (2560, in_turned, bu),
        ):
            part = dot(left[...], right).astype(bf16)
            for b in range(2):
                at = pl.ds(pl.multiple_of(base + (2 * j + b) * 160, 160), 160)
                for f in range(4):
                    grads[f, at, :] = part[160 * f : 160 * f + 160, 128 * b : 128 * b + 128]
        part = dot(out_turned[...], hidden[:, cols]).astype(bf16)
        for b in range(2):
            at = pl.ds(pl.multiple_of(5120 + (j % 2 * 2 + b) * 640, 640), 640)
            grads[j // 2, at, :] = part[:, 128 * b : 128 * b + 128]

    e = total[...]
    gain_grads[1:2] = jnp.sum(mid * r2 * e, axis=0, keepdims=True)
    bm = g + norm_back(mid, r2, g_in, e)
    back_middle[...] = bm
    gain_grads[0:1] = jnp.sum(ao * r1 * bm, axis=0, keepdims=True)
    bao = norm_back(ao, r1, g_attn, bm).astype(bf16)
    back_attn[...] = bao
    back_attended[...] = dot(bao, wo[...], rows_both).astype(bf16)


def middle_part(place, x, attended, upstream, gains, shares):
    return pl.pallas_call(
        middle_kernel,
        name="middle_part",
        in_specs=[pl.BlockSpec(memory_space=pltpu.SMEM)]
        + [whole()] * 4
        + [pl.BlockSpec(memory_space=pl.ANY)] * 16,
        out_specs=[whole()] * 6,
        out_shape=[
            spec(512, 640, bf16),
            spec(512, 640, f32),
            spec(512, 640, bf16),
            spec(512, 1024, bf16),
            spec(8, 640, f32),
            spec(4, 7680, 128, bf16),
        ],
        scratch_shapes=[
            pltpu.VMEM((512, 640), bf16),
            pltpu.VMEM((512, 2048), f32),
            pltpu.VMEM((512, 2048), f32),
            pltpu.VMEM((512, 2048), bf16),
            pltpu.VMEM((512, 640), bf16),
            pltpu.VMEM((640, 512), bf16),
            pltpu.VMEM((640, 512), bf16),
            pltpu.VMEM((512, 640), f32),
            pltpu.VMEM((1024, 640), bf16),
            pltpu.VMEM((640, 2048), bf16),
            pltpu.VMEM((640, 2048), bf16),
            pltpu.VMEM((2048, 640), bf16),
            pltpu.SemaphoreType.DMA((16,)),
        ],
        compiler_params=params(50),
        cost_estimate=cost(13_400_000_000, 23_000_000, 1_000_000),
    )(place, x, attended, upstream, gains, *shares)


def attend_back_kernel(
    q,
    k,
    v,
    offsets,
    level,
    back_attended,
    q_proj,
    k_proj,
    head_gains,
    cosine,
    sine,
    back_q,
    back_kv,
    gain_grads,
    sum_k,
    sum_v,
):
    t = pl.program_id(0)

    @pl.when(t == 0)
    def _():
        sum_k[...] = jnp.zeros_like(sum_k)
        sum_v[...] = jnp.zeros_like(sum_v)
        gain_grads[...] = jnp.zeros_like(gain_grads)

    near = pl.ds(pl.multiple_of(t * 256, 256), 768)
    mine = pl.ds(pl.multiple_of(t * 256 + 512, 256), 256)
    keys, values = k[near, :], v[near, :]
    visible = visible_keys(offsets[...])
    c, s = cosine[mine, :], sine[mine, :]
    for h in range(4):
        cols = slice(256 * h, 256 * h + 256)
        qh, bah = q[:, cols], back_attended[:, cols]
        scores = jnp.where(visible, dot(qh, keys, rows_both) * 0.0625, masked_value)
        probs = jnp.exp(scores - level[h])
        bp = dot(bah, values, rows_both)
        inner = jnp.sum(probs * bp, axis=-1, keepdims=True)
        bs = (probs * (bp - inner)).astype(bf16)
        sum_k[near, :] += dot(bs, qh, cols_both)
        sum_v[near, :] += dot(probs.astype(bf16), bah, cols_both)
        e = turn_back(dot(bs, keys) * 0.0625, c, s)
        qp = q_proj[:, cols]
        r = inverse_rms(qp)
        gain_grads[0:1] += jnp.sum(qp * r * e, axis=0, keepdims=True)
        back_q[:, cols] = norm_back(qp, r, head_gains[0:1], e).astype(bf16)

    @pl.when(t == 1)
    def _():
        e = turn_back(sum_k[...] * 0.0625, cosine[...], sine[...])
        kp = k_proj[...]
        r = inverse_rms(kp)
        gain_grads[1:2] = jnp.sum(kp * r * e, axis=0, keepdims=True)
        back_kv[:, :256] = norm_back(kp, r, head_gains[1:2], e).astype(bf16)
        back_kv[:, 256:] = sum_v[...].astype(bf16)


def attend_back(
    q, k, v, offsets, level, back_attended, q_proj, k_proj, head_gains, cosine, sine
):
    row = lambda i: (i, 0)
    fixed = lambda i: (0, 0)
    return pl.pallas_call(
        attend_back_kernel,
        name="attend_back",
        grid=(2,),
        in_specs=[
            pl.BlockSpec((256, 1024), row),
            pl.BlockSpec((1024, 256), fixed),
            pl.BlockSpec((1024, 256), fixed),
            pl.BlockSpec((256, 1), row),
            pl.BlockSpec((4, 256, 1), lambda i: (0, i, 0)),
            pl.BlockSpec((256, 1024), row),
            pl.BlockSpec((256, 1024), row),
            pl.BlockSpec((1024, 256), fixed),
            pl.BlockSpec((8, 256), fixed),
            pl.BlockSpec((1024, 128), fixed),
            pl.BlockSpec((1024, 128), fixed),
        ],
        out_specs=[
            pl.BlockSpec((256, 1024), row),
            pl.BlockSpec((1024, 512), fixed),
            pl.BlockSpec((8, 256), fixed),
        ],
        out_shape=[spec(512, 1024, bf16), spec(1024, 512, bf16), spec(8, 256, f32)],
        scratch_shapes=[pltpu.VMEM((1024, 256), f32), pltpu.VMEM((1024, 256), f32)],
        compiler_params=params(30),
        cost_estimate=cost(4_300_000_000, 10_000_000, 2_000_000),
    )(q, k, v, offsets, level, back_attended, q_proj, k_proj, head_gains, cosine, sine)


def weights_kernel(
    place,
    normed,
    back_q,
    back_kv,
    attended,
    back_attn,
    halo,
    own,
    gain_mid,
    gain_head,
    q0,
    q1,
    q2,
    q3,
    kv0,
    kv1,
    kv2,
    kv3,
    back_halo,
    back_own,
    grads,
    wq,
    wkv,
    semaphores,
):
    copies = assemble((kv0, kv1, kv2, kv3), wkv, place[0], semaphores, 0)
    copies += assemble((q0, q1, q2, q3), wq, place[0], semaphores, 4)
    turned = normed[...].astype(f32).T.astype(bf16)
    bq, bkv = back_q[...], back_kv[...]
    part = dot(turned[:, 512:], bq).astype(bf16)
    for b in range(8):
        for f in range(4):
            grads[f, 160 * b : 160 * b + 160, :] = part[
                160 * f : 160 * f + 160, 128 * b : 128 * b + 128
            ]
    part = dot(turned, bkv).astype(bf16)
    for b in range(4):
        for f in range(4):
            grads[f, 1280 + 160 * b : 1440 + 160 * b, :] = part[
                160 * f : 160 * f + 160, 128 * b : 128 * b + 128
            ]
    turned = back_attn[...].astype(f32).T.astype(bf16)
    part = dot(turned, attended[...]).astype(bf16)
    for f in range(4):
        for b in range(2):
            grads[f, 1920 + 640 * b : 2560 + 640 * b, :] = part[
                :, 256 * f + 128 * b : 256 * f + 128 * b + 128
            ]
    for copy in copies:
        copy.wait()
    e = dot(bkv[:512], wkv[...], rows_both)
    back_halo[...] = e.astype(bf16)
    x = halo[...].astype(f32)
    grad = jnp.sum(x * inverse_rms(x) * e, axis=0, keepdims=True)
    e = dot(bkv[512:], wkv[...], rows_both) + dot(bq, wq[...], rows_both)
    back_own[...] = e
    x = own[...].astype(f32)
    grad = grad + jnp.sum(x * inverse_rms(x) * e, axis=0, keepdims=True)
    each = jnp.concatenate([grad, gain_mid[0:3]], axis=0)
    heads = gain_head[0:2]
    for f in range(4):
        share = each[:, 160 * f : 160 * f + 160]
        rest = jnp.concatenate([share[:, 128:], jnp.zeros((4, 96), f32)], axis=1)
        ends = jnp.concatenate([heads[:, 64 * f : 64 * f + 64], jnp.zeros((2, 64), f32)], axis=1)
        tile = jnp.concatenate([share[:, :128], rest, ends, jnp.zeros((6, 128), f32)], axis=0)
        grads[f, 3200:3216, :] = tile.astype(bf16)
        grads[f, 3216:, :] = jnp.zeros((368, 128), bf16)


def weights_part(
    place, normed, back_q, back_kv, attended, back_attn, halo, own, gain_mid, gain_head, shares
):
    return pl.pallas_call(
        weights_kernel,
        name="weights_part",
        in_specs=[pl.BlockSpec(memory_space=pltpu.SMEM)]
        + [whole()] * 9
        + [pl.BlockSpec(memory_space=pl.ANY)] * 8,
        out_specs=[whole()] * 3,
        out_shape=[
            spec(512, 640, bf16),
            spec(512, 640, f32),
            spec(4, 3584, 128, bf16),
        ],
        scratch_shapes=[
            pltpu.VMEM((640, 1024), bf16),
            pltpu.VMEM((640, 512), bf16),
            pltpu.SemaphoreType.DMA((8,)),
        ],
        compiler_params=params(40),
        cost_estimate=cost(3_400_000_000, 14_000_000),
    )(place, normed, back_q, back_kv, attended, back_attn, halo, own, gain_mid, gain_head, *shares)


def finish_kernel(own, back_own, returned, back_middle, gains, grad_in):
    x = own[...].astype(f32)
    e = back_own[...] + returned[...].astype(f32)
    grad_in[...] = (back_middle[...] + norm_back(x, inverse_rms(x), gains[0:1], e)).astype(bf16)


def finish(own, back_own, returned, back_middle, gains):
    row = lambda i: (i, 0)
    return pl.pallas_call(
        finish_kernel,
        name="finish",
        grid=(4,),
        in_specs=[pl.BlockSpec((128, 640), row)] * 4 + [pl.BlockSpec((8, 640), lambda i: (0, 0))],
        out_specs=pl.BlockSpec((128, 640), row),
        out_shape=spec(512, 640, bf16),
        compiler_params=params(10),
        cost_estimate=cost(4_000_000, 5_000_000),
    )(own, back_own, returned, back_middle, gains)


def rope_tables(offsets):
    powers = jnp.arange(128, dtype=f32) * (2.0 / 256)
    row = jnp.arange(512, dtype=jnp.int32)
    every = jnp.concatenate([offsets[0] - 512 + row, offsets])
    angles = every.astype(f32)[:, None] * (rope_base ** (-powers))[None, :]
    return jnp.cos(angles), jnp.sin(angles)


def unpack_kernel(
    spot, a0, a1, a2, a3, b0, b1, b2, b3, q, k, v, out, gate, up, down, gains, ffn, attn, semaphores
):
    x, y = spot[0], spot[1]
    copies = []
    for half, pieces in enumerate(((a0, a1, a2, a3), (b0, b1, b2, b3))):
        for i in range(4):
            for j in range(4):
                first, second = (x, y) if half == 0 else (y, x)
                block = 16 * half + (first - i + 4) % 4 * 4 + (second - j + 4) % 4
                n = (half * 4 + i) * 4 + j
                for m, (into, start, rows) in enumerate(((ffn, 0, 240), (attn, 240, 112))):
                    copies.append(
                        pltpu.make_async_copy(
                            pieces[i].at[j, pl.ds(start, rows), :],
                            into.at[pl.ds(pl.multiple_of(block * rows, 16), rows), :],
                            semaphores.at[2 * n + m],
                        )
                    )
    for copy in copies:
        copy.start()
    for copy in copies:
        copy.wait()
    for into, flat, first, count in (
        (gate, ffn, 0, 16),
        (up, ffn, 2560, 16),
        (q, attn, 0, 8),
        (k, attn, 1280, 2),
        (v, attn, 1600, 2),
    ):
        for b in range(count):
            at = first + 160 * b
            into[:, 128 * b : 128 * b + 128] = flat[at : at + 160, :].astype(f32)
    for into, flat, first, count in ((down, ffn, 5120, 4), (out, attn, 1920, 2)):
        for b in range(count):
            at = first + 640 * b
            into[128 * b : 128 * b + 128, :] = flat[at : at + 640, :].astype(f32).T
    gains[...] = attn[3200:3216, :].astype(f32)


def unpack(spot, pieces):
    return pl.pallas_call(
        unpack_kernel,
        name="unpack",
        in_specs=[pl.BlockSpec(memory_space=pltpu.SMEM)] + [pl.BlockSpec(memory_space=pl.ANY)] * 8,
        out_specs=[whole()] * 8,
        out_shape=[
            spec(160, 1024, f32),
            spec(160, 256, f32),
            spec(160, 256, f32),
            spec(256, 640, f32),
            spec(160, 2048, f32),
            spec(160, 2048, f32),
            spec(512, 640, f32),
            spec(16, 128, f32),
        ],
        scratch_shapes=[
            pltpu.VMEM((7680, 128), bf16),
            pltpu.VMEM((3584, 128), bf16),
            pltpu.SemaphoreType.DMA((64,)),
        ],
        compiler_params=params(20),
        cost_estimate=cost(4_000_000, 11_000_000),
    )(spot, *pieces)


def seq_index(z, x, y):
    return (z % 2 * 4 + x % 4) * 4 + y % 4


def along_xy(dx, dy):
    return [
        (seq_index(z, x, y), seq_index(z, x + dx, y + dy))
        for z in range(2)
        for x in range(4)
        for y in range(4)
    ]


def along_z(step):
    pairs = []
    for s in range(32):
        for f in range(4):
            z = s // 16 * 2 + f // 2
            t = step(z)
            pairs.append((s * 4 + f, (t // 2 * 16 + s % 16) * 4 + t % 2 * 2 + f % 2))
    return pairs


def swap_core(value):
    return lax.ppermute(value, "fsdp", [(0, 1), (1, 0), (2, 3), (3, 2)])


def swap_near(value):
    return lax.ppermute(value, "fsdp", [(0, 2), (1, 3), (2, 0), (3, 1)])


def swap_far(value):
    return lax.ppermute(value, ("seq", "fsdp"), along_z(lambda z: 3 - z))


def swap_hi(value):
    return lax.ppermute(value, "seq", [(s, (s + 16) % 32) for s in range(32)])


def move_x(value, d):
    return lax.ppermute(value, "seq", along_xy(d, 0))


def move_y(value, d):
    return lax.ppermute(value, "seq", along_xy(0, d))


def shifted(value, steps):
    first, last = (max(0, -steps), min(32, 32 - steps))
    return lax.ppermute(value, "seq", [(source, source + steps) for source in range(first, last)])


def pick(value, index, axis):
    return lax.dynamic_index_in_dim(value, index, axis, keepdims=False)


def total_of(parts):
    whole = parts[0].astype(f32)
    for part in parts[1:]:
        whole = whole + part.astype(f32)
    return whole.astype(bf16)


steps = (1, 3, 2)


def reduce_first(buf, x, y, core):
    rows = buf.shape[2]
    got = swap_core(pick(buf, 1 - core, 1))
    both = total_of([pick(buf, core, 1), got]).reshape(2, 2, 4, 4, rows // 32, 128)
    a, b = both[:, 0], both[:, 1]
    from_a = [move_x(pick(a, (x + d) % 4, 1), d) for d in steps]
    from_b = [move_y(pick(b, (y + d) % 4, 1), d) for d in steps]
    return total_of([pick(a, x, 1)] + from_a), total_of([pick(b, y, 1)] + from_b)


def reduce_rest(a, b, x, y, z_lo):
    from_a = [move_y(pick(a, (y + d) % 4, 1), d) for d in steps]
    from_b = [move_x(pick(b, (x + d) % 4, 1), d) for d in steps]
    a = total_of([pick(a, y, 1)] + from_a)
    b = total_of([pick(b, x, 1)] + from_b)
    both = jnp.stack([a, b], axis=1)
    mine = pick(both, z_lo, 0)
    other = pick(both, 1 - z_lo, 0)
    both = total_of([mine, swap_near(other), swap_far(other), swap_hi(mine)])
    a, b = both[0], both[1]
    a = jnp.stack([a] + [move_y(a, d) for d in (1, 2, 3)])
    b = jnp.stack([b] + [move_x(b, d) for d in (1, 2, 3)])
    return [a] + [move_x(a, d) for d in (1, 2, 3)] + [b] + [move_y(b, d) for d in (1, 2, 3)]


def body(
    hidden_in,
    cotangent,
    positions,
    query_weight,
    key_weight,
    value_weight,
    output_weight,
    gate_weight,
    up_weight,
    down_weight,
    norm_in,
    norm_attn,
    norm_ffn_in,
    norm_ffn_out,
    norm_query,
    norm_key,
):
    s = lax.axis_index("seq")
    f = lax.axis_index("fsdp")
    x, y, z_lo, core = s // 4 % 4, s % 4, f // 2, f % 2
    place = f.astype(jnp.int32).reshape(1)
    spot = jnp.stack([x, y]).astype(jnp.int32)
    own = hidden_in[0]
    upstream = cotangent[0]
    offsets = positions[0]

    rows = [norm_in, norm_attn, norm_ffn_in, norm_ffn_out, norm_query, norm_key]
    gain_rows = jnp.stack([jnp.pad(g, (0, 512 - g.shape[0])) for g in rows + [rows[0]] * 2])
    kvg = jnp.concatenate(
        [jnp.concatenate([key_weight, value_weight], axis=1), gain_rows], axis=0
    )
    q_partner = swap_near(query_weight)
    kvg_partner = swap_far(kvg)
    q_sibling = swap_core(query_weight)
    kvg_sibling = swap_core(kvg)
    q_diagonal = swap_core(q_partner)
    kvg_diagonal = swap_core(kvg_partner)
    halo = shifted(own, 1)
    wo, wg, wu, wd, _, _ = lax.optimization_barrier(
        (output_weight, gate_weight, up_weight, down_weight, q_partner, kvg_partner)
    )
    shares = []
    for share, swap in ((wo, swap_near), (wg, swap_near), (wu, swap_far), (wd, swap_far)):
        partner = swap(share)
        shares += [share, swap_core(share), partner, swap_core(partner)]

    q_shares = (query_weight, q_sibling, q_partner, q_diagonal)
    kv_shares = (kvg, kvg_sibling, kvg_partner, kvg_diagonal)
    tails = [share[160:168] for share in kv_shares]
    tails = [
        jnp.where(
            j // 2 == z_lo,
            jnp.where(j % 2 == core, tails[0], tails[1]),
            jnp.where(j % 2 == core, tails[2], tails[3]),
        )
        for j in range(4)
    ]
    gains = jnp.concatenate([tail[:, :160] for tail in tails], axis=1).astype(f32)
    head_gains = jnp.concatenate([tail[:, :64] for tail in tails], axis=1).astype(f32)
    head_gains = jnp.concatenate([head_gains[4:8], head_gains[4:8]], axis=0)

    cosine, sine = rope_tables(offsets)
    column = offsets[:, None]
    normed, q, k, v, q_proj, k_proj = project(
        place, halo, own, gains, head_gains, q_shares, kv_shares, cosine, sine
    )
    attended, level = attend(q, k, v, column)
    layer_out, back_middle, back_attn, back_attended, gain_mid, ffn_grads = middle_part(
        place, own, attended, upstream, gains, shares
    )
    ffn_a, ffn_b = reduce_first(ffn_grads.reshape(2, 2, 7680, 128), x, y, core)
    back_q, back_kv, gain_head = attend_back(
        q, k, v, column, level, back_attended, q_proj, k_proj, head_gains, cosine, sine
    )
    back_halo, back_own, attn_grads = weights_part(
        place,
        normed,
        back_q,
        back_kv,
        attended,
        back_attn,
        halo,
        own,
        gain_mid,
        gain_head,
        q_shares + kv_shares,
    )
    returned = shifted(back_halo, -1)
    attn_a, attn_b = reduce_first(attn_grads.reshape(2, 2, 3584, 128), x, y, core)
    pieces = reduce_rest(
        jnp.concatenate([ffn_a, attn_a], axis=2),
        jnp.concatenate([ffn_b, attn_b], axis=2),
        x,
        y,
        z_lo,
    )
    grad_q, grad_k, grad_v, grad_o, grad_g, grad_u, grad_d, tile = unpack(spot, pieces)
    grad_in = finish(own, back_own, returned, back_middle, gains)
    wide = jnp.concatenate([tile[0:4], tile[4:8, :32]], axis=1)
    return (
        layer_out[None],
        grad_in[None],
        grad_q,
        grad_k,
        grad_v,
        grad_o,
        grad_g,
        grad_u,
        grad_d,
        wide[0],
        wide[1],
        wide[2],
        wide[3],
        tile[8, :64],
        tile[9, :64],
    )


def solution(mesh):
    three = P("fsdp", "seq", None)
    two = P("fsdp", None)
    one = P("fsdp")
    return jax.shard_map(
        body,
        mesh=mesh,
        in_specs=(three, three, P("fsdp", "seq")) + (two,) * 7 + (one,) * 6,
        out_specs=(three, three) + (two,) * 7 + (one,) * 6,
        check_vma=False,
    )
```

```python
import jax
import jax.numpy as jnp
from jax import lax
from jax.experimental import pallas as pl
from jax.experimental.pallas import tpu as pltpu
from jax.sharding import PartitionSpec as P

WINDOW = 512
epsilon = 1e-06
rope_base = 10000.0
masked_value = -1e30
bf16 = jnp.bfloat16
f32 = jnp.float32

rows_out = ((1,), (0,))
rows_both = ((1,), (1,))
cols_both = ((0,), (0,))


def dot(a, b, dims=rows_out):
    return lax.dot_general(a, b, (dims, ((), ())), preferred_element_type=f32)


def spec(*shape):
    return jax.ShapeDtypeStruct(shape[:-1], shape[-1])


def whole():
    return pl.BlockSpec(memory_space=pltpu.VMEM)


def params(mib):
    return pltpu.CompilerParams(vmem_limit_bytes=mib * 1024 * 1024)


def cost(flops, moved, exps=0):
    return pl.CostEstimate(flops=flops, bytes_accessed=moved, transcendentals=exps)


def inverse_rms(v):
    return lax.rsqrt(jnp.mean(v * v, axis=-1, keepdims=True) + epsilon)


def norm_back(v, r, gain, e):
    scaled = gain * e
    return r * scaled - v * (r * r * r * jnp.mean(v * scaled, axis=-1, keepdims=True))


def turn(v, cosine, sine):
    a, b = v[:, :128], v[:, 128:]
    return jnp.concatenate([a * cosine - b * sine, b * cosine + a * sine], axis=1)


def turn_back(v, cosine, sine):
    a, b = v[:, :128], v[:, 128:]
    return jnp.concatenate([a * cosine + b * sine, b * cosine - a * sine], axis=1)


def assemble(pieces, into, place, semaphores, first):
    rows = into.shape[0] // 4
    copies = []
    for r in range(4):
        at = pl.ds(pl.multiple_of((place ^ r) * rows, rows), rows)
        copies.append(
            pltpu.make_async_copy(
                pieces[r].at[pl.ds(0, rows), :], into.at[at, :], semaphores.at[first + r]
            )
        )
    for copy in copies:
        copy.start()
    return copies


def split_out(grads, kept, sent, place, semaphores, first):
    core = lax.rem(place, 2)
    copies = []
    for z in range(2):
        copies.append(
            pltpu.make_async_copy(
                grads.at[2 * z + 1 - core], sent.at[z], semaphores.at[first + 2 * z]
            )
        )
        copies.append(
            pltpu.make_async_copy(
                grads.at[2 * z + core], kept.at[z], semaphores.at[first + 2 * z + 1]
            )
        )
    for copy in copies:
        copy.start()
    return copies


def project_kernel(
    place,
    halo,
    own,
    gains,
    head_gains,
    q0,
    q1,
    q2,
    q3,
    kv0,
    kv1,
    kv2,
    kv3,
    cosine,
    sine,
    normed,
    q,
    k,
    v,
    q_proj,
    k_proj,
    wq,
    wkv,
    semaphores,
):
    i = pl.program_id(0)

    @pl.when(i == 0)
    def _():
        copies = assemble((kv0, kv1, kv2, kv3), wkv, place[0], semaphores, 0)
        copies += assemble((q0, q1, q2, q3), wq, place[0], semaphores, 4)
        for copy in copies:
            copy.wait()

    x = jnp.where(i < 2, halo[...], own[...]).astype(f32)
    n = (x * inverse_rms(x) * gains[0:1]).astype(bf16)
    normed[...] = n
    c, s = cosine[...], sine[...]
    kv = dot(n, wkv[...])
    kp = kv[:, :256]
    k_proj[...] = kp
    v[...] = kv[:, 256:].astype(bf16)
    k[...] = turn(kp * inverse_rms(kp) * head_gains[1:2], c, s).astype(bf16)

    @pl.when(i >= 2)
    def _():
        for h in range(4):
            cols = slice(256 * h, 256 * h + 256)
            qp = dot(n, wq[:, cols])
            q_proj[:, cols] = qp
            q[:, cols] = turn(qp * inverse_rms(qp) * head_gains[0:1], c, s).astype(bf16)


def project(place, halo, own, gains, head_gains, q_shares, kv_shares, cosine, sine):
    late = lambda i: (jnp.maximum(i - 2, 0), 0)
    row = lambda i: (i, 0)
    fixed = lambda i: (0, 0)
    return pl.pallas_call(
        project_kernel,
        name="project",
        grid=(4,),
        in_specs=[
            pl.BlockSpec(memory_space=pltpu.SMEM),
            pl.BlockSpec((256, 640), lambda i: (jnp.minimum(i, 1), 0)),
            pl.BlockSpec((256, 640), late),
            pl.BlockSpec((8, 640), fixed),
            pl.BlockSpec((8, 256), fixed),
        ]
        + [pl.BlockSpec(memory_space=pl.ANY)] * 8
        + [pl.BlockSpec((256, 128), row)] * 2,
        out_specs=[
            pl.BlockSpec((256, 640), row),
            pl.BlockSpec((256, 1024), late),
            pl.BlockSpec((256, 256), row),
            pl.BlockSpec((256, 256), row),
            pl.BlockSpec((256, 1024), late),
            pl.BlockSpec((256, 256), row),
        ],
        out_shape=[
            spec(1024, 640, bf16),
            spec(512, 1024, bf16),
            spec(1024, 256, bf16),
            spec(1024, 256, bf16),
            spec(512, 1024, f32),
            spec(1024, 256, f32),
        ],
        scratch_shapes=[
            pltpu.VMEM((640, 1024), bf16),
            pltpu.VMEM((640, 512), bf16),
            pltpu.SemaphoreType.DMA((8,)),
        ],
        compiler_params=params(20),
        cost_estimate=cost(1_350_000_000, 9_000_000),
    )(place, halo, own, gains, head_gains, *q_shares, *kv_shares, cosine, sine)


def visible_keys(offsets):
    distance = (
        lax.broadcasted_iota(jnp.int32, (256, 768), 0)
        + 512
        - lax.broadcasted_iota(jnp.int32, (256, 768), 1)
    )
    return (distance >= 0) & (distance < WINDOW) & (distance <= offsets)


def attend_kernel(q, k, v, offsets, attended, level):
    t = pl.program_id(0)
    near = pl.ds(pl.multiple_of(t * 256, 256), 768)
    keys, values = k[near, :], v[near, :]
    visible = visible_keys(offsets[...])
    for h in range(4):
        cols = slice(256 * h, 256 * h + 256)
        scores = jnp.where(visible, dot(q[:, cols], keys, rows_both) * 0.0625, masked_value)
        top = jnp.max(scores, axis=-1, keepdims=True)
        e = jnp.exp(scores - top)
        total = jnp.sum(e, axis=-1, keepdims=True)
        level[h] = top + jnp.log(total)
        probs = (e * (1.0 / total)).astype(bf16)
        attended[:, cols] = dot(probs, values).astype(bf16)


def attend(q, k, v, offsets):
    row = lambda i: (i, 0)
    fixed = lambda i: (0, 0)
    return pl.pallas_call(
        attend_kernel,
        name="attend",
        grid=(2,),
        in_specs=[
            pl.BlockSpec((256, 1024), row),
            pl.BlockSpec((1024, 256), fixed),
            pl.BlockSpec((1024, 256), fixed),
            pl.BlockSpec((256, 1), row),
        ],
        out_specs=[
            pl.BlockSpec((256, 1024), row),
            pl.BlockSpec((4, 256, 1), lambda i: (0, i, 0)),
        ],
        out_shape=[spec(512, 1024, bf16), spec(4, 512, 1, f32)],
        compiler_params=params(20),
        cost_estimate=cost(1_700_000_000, 4_000_000, 2_000_000),
    )(q, k, v, offsets)


def middle_kernel(
    place,
    x_ref,
    attended,
    upstream,
    gains,
    o0,
    o1,
    o2,
    o3,
    g0,
    g1,
    g2,
    g3,
    u0,
    u1,
    u2,
    u3,
    d0,
    d1,
    d2,
    d3,
    layer_out,
    back_middle,
    back_attn,
    back_attended,
    gain_grads,
    kept,
    sent,
    ffn_in,
    kept_a,
    kept_b,
    hidden,
    back_out,
    in_turned,
    out_turned,
    total,
    wo,
    wg,
    wu,
    wd,
    grads,
    semaphores,
):
    output_copies = assemble((o0, o1, o2, o3), wo, place[0], semaphores, 0)
    gate_copies = assemble((g0, g1, g2, g3), wg, place[0], semaphores, 4)
    up_copies = assemble((u0, u1, u2, u3), wu, place[0], semaphores, 8)
    down_copies = assemble((d0, d1, d2, d3), wd, place[0], semaphores, 12)
    for copy in output_copies:
        copy.wait()
    g_attn, g_in, g_out = gains[1:2], gains[2:3], gains[3:4]
    ao = dot(attended[...], wo[...])
    r1 = inverse_rms(ao)
    mid = x_ref[...].astype(f32) + ao * r1 * g_attn
    r2 = inverse_rms(mid)
    ffn_in[...] = (mid * r2 * g_in).astype(bf16)
    total[...] = jnp.zeros_like(total)
    for copy in gate_copies + up_copies + down_copies:
        copy.wait()

    @pl.loop(0, 8)
    def _(j):
        cols = pl.ds(pl.multiple_of(j * 256, 256), 256)
        u = dot(ffn_in[...], wg[:, cols])
        up = dot(ffn_in[...], wu[:, cols])
        root = 0.7978845608028654
        t = jnp.tanh(root * (u + 0.044715 * (u * u * u)))
        half = 0.5 * (1.0 + t)
        act = u * half
        slope = half + (0.5 * root) * u * (1.0 - t * t) * (1.0 + (3 * 0.044715) * (u * u))
        h = (act * up).astype(bf16)
        hidden[:, cols] = h
        kept_a[:, cols] = act
        kept_b[:, cols] = up * slope
        total[...] += dot(h, wd[cols, :])

    fo = total[...]
    r3 = inverse_rms(fo)
    layer_out[...] = (mid + fo * r3 * g_out).astype(bf16)
    g = upstream[...].astype(f32)
    gain_grads[2:3] = jnp.sum(fo * r3 * g, axis=0, keepdims=True)
    bfo = norm_back(fo, r3, g_out, g)
    back_out[...] = bfo.astype(bf16)
    out_turned[...] = bfo.T.astype(bf16)
    in_turned[...] = (mid * r2 * g_in).T.astype(bf16)
    total[...] = jnp.zeros_like(total)

    @pl.loop(0, 8)
    def _(j):
        cols = pl.ds(pl.multiple_of(j * 256, 256), 256)
        bh = dot(back_out[...], wd[cols, :], rows_both)
        bu = (bh * kept_a[:, cols]).astype(bf16)
        bg = (bh * kept_b[:, cols]).astype(bf16)
        total[...] += dot(bg, wg[:, cols], rows_both) + dot(bu, wu[:, cols], rows_both)
        for base, left, right in (
            (0, in_turned, bg),
            (2560, in_turned, bu),
        ):
            part = dot(left[...], right).astype(bf16)
            for b in range(2):
                at = pl.ds(pl.multiple_of(base + (2 * j + b) * 160, 160), 160)
                for f in range(4):
                    grads[f, at, :] = part[160 * f : 160 * f + 160, 128 * b : 128 * b + 128]
        part = dot(out_turned[...], hidden[:, cols]).astype(bf16)
        for b in range(2):
            at = pl.ds(pl.multiple_of(5120 + (j % 2 * 2 + b) * 640, 640), 640)
            grads[j // 2, at, :] = part[:, 128 * b : 128 * b + 128]

    outward = split_out(grads, kept, sent, place[0], semaphores, 16)
    e = total[...]
    gain_grads[1:2] = jnp.sum(mid * r2 * e, axis=0, keepdims=True)
    bm = g + norm_back(mid, r2, g_in, e)
    back_middle[...] = bm
    gain_grads[0:1] = jnp.sum(ao * r1 * bm, axis=0, keepdims=True)
    bao = norm_back(ao, r1, g_attn, bm).astype(bf16)
    back_attn[...] = bao
    back_attended[...] = dot(bao, wo[...], rows_both).astype(bf16)
    for copy in outward:
        copy.wait()


def middle_part(place, x, attended, upstream, gains, shares):
    return pl.pallas_call(
        middle_kernel,
        name="middle_part",
        in_specs=[pl.BlockSpec(memory_space=pltpu.SMEM)]
        + [whole()] * 4
        + [pl.BlockSpec(memory_space=pl.ANY)] * 16,
        out_specs=[whole()] * 5 + [pl.BlockSpec(memory_space=pl.ANY)] * 2,
        out_shape=[
            spec(512, 640, bf16),
            spec(512, 640, f32),
            spec(512, 640, bf16),
            spec(512, 1024, bf16),
            spec(8, 640, f32),
            spec(2, 7680, 128, bf16),
            spec(2, 7680, 128, bf16),
        ],
        scratch_shapes=[
            pltpu.VMEM((512, 640), bf16),
            pltpu.VMEM((512, 2048), f32),
            pltpu.VMEM((512, 2048), f32),
            pltpu.VMEM((512, 2048), bf16),
            pltpu.VMEM((512, 640), bf16),
            pltpu.VMEM((640, 512), bf16),
            pltpu.VMEM((640, 512), bf16),
            pltpu.VMEM((512, 640), f32),
            pltpu.VMEM((1024, 640), bf16),
            pltpu.VMEM((640, 2048), bf16),
            pltpu.VMEM((640, 2048), bf16),
            pltpu.VMEM((2048, 640), bf16),
            pltpu.VMEM((4, 7680, 128), bf16),
            pltpu.SemaphoreType.DMA((20,)),
        ],
        compiler_params=params(50),
        cost_estimate=cost(13_400_000_000, 23_000_000, 1_000_000),
    )(place, x, attended, upstream, gains, *shares)


def attend_back_kernel(
    q,
    k,
    v,
    offsets,
    level,
    back_attended,
    q_proj,
    k_proj,
    head_gains,
    cosine,
    sine,
    back_q,
    back_kv,
    gain_grads,
    sum_k,
    sum_v,
):
    t = pl.program_id(0)

    @pl.when(t == 0)
    def _():
        sum_k[...] = jnp.zeros_like(sum_k)
        sum_v[...] = jnp.zeros_like(sum_v)
        gain_grads[...] = jnp.zeros_like(gain_grads)

    near = pl.ds(pl.multiple_of(t * 256, 256), 768)
    mine = pl.ds(pl.multiple_of(t * 256 + 512, 256), 256)
    keys, values = k[near, :], v[near, :]
    visible = visible_keys(offsets[...])
    c, s = cosine[mine, :], sine[mine, :]
    for h in range(4):
        cols = slice(256 * h, 256 * h + 256)
        qh, bah = q[:, cols], back_attended[:, cols]
        scores = jnp.where(visible, dot(qh, keys, rows_both) * 0.0625, masked_value)
        probs = jnp.exp(scores - level[h])
        bp = dot(bah, values, rows_both)
        inner = jnp.sum(probs * bp, axis=-1, keepdims=True)
        bs = (probs * (bp - inner)).astype(bf16)
        sum_k[near, :] += dot(bs, qh, cols_both)
        sum_v[near, :] += dot(probs.astype(bf16), bah, cols_both)
        e = turn_back(dot(bs, keys) * 0.0625, c, s)
        qp = q_proj[:, cols]
        r = inverse_rms(qp)
        gain_grads[0:1] += jnp.sum(qp * r * e, axis=0, keepdims=True)
        back_q[:, cols] = norm_back(qp, r, head_gains[0:1], e).astype(bf16)

    @pl.when(t == 1)
    def _():
        e = turn_back(sum_k[...] * 0.0625, cosine[...], sine[...])
        kp = k_proj[...]
        r = inverse_rms(kp)
        gain_grads[1:2] = jnp.sum(kp * r * e, axis=0, keepdims=True)
        back_kv[:, :256] = norm_back(kp, r, head_gains[1:2], e).astype(bf16)
        back_kv[:, 256:] = sum_v[...].astype(bf16)


def attend_back(
    q, k, v, offsets, level, back_attended, q_proj, k_proj, head_gains, cosine, sine
):
    row = lambda i: (i, 0)
    fixed = lambda i: (0, 0)
    return pl.pallas_call(
        attend_back_kernel,
        name="attend_back",
        grid=(2,),
        in_specs=[
            pl.BlockSpec((256, 1024), row),
            pl.BlockSpec((1024, 256), fixed),
            pl.BlockSpec((1024, 256), fixed),
            pl.BlockSpec((256, 1), row),
            pl.BlockSpec((4, 256, 1), lambda i: (0, i, 0)),
            pl.BlockSpec((256, 1024), row),
            pl.BlockSpec((256, 1024), row),
            pl.BlockSpec((1024, 256), fixed),
            pl.BlockSpec((8, 256), fixed),
            pl.BlockSpec((1024, 128), fixed),
            pl.BlockSpec((1024, 128), fixed),
        ],
        out_specs=[
            pl.BlockSpec((256, 1024), row),
            pl.BlockSpec((1024, 512), fixed),
            pl.BlockSpec((8, 256), fixed),
        ],
        out_shape=[spec(512, 1024, bf16), spec(1024, 512, bf16), spec(8, 256, f32)],
        scratch_shapes=[pltpu.VMEM((1024, 256), f32), pltpu.VMEM((1024, 256), f32)],
        compiler_params=params(30),
        cost_estimate=cost(4_300_000_000, 10_000_000, 2_000_000),
    )(q, k, v, offsets, level, back_attended, q_proj, k_proj, head_gains, cosine, sine)


def weights_kernel(
    place,
    normed,
    back_q,
    back_kv,
    attended,
    back_attn,
    halo,
    own,
    gain_mid,
    gain_head,
    q0,
    q1,
    q2,
    q3,
    kv0,
    kv1,
    kv2,
    kv3,
    back_halo,
    back_own,
    kept,
    sent,
    wq,
    wkv,
    grads,
    semaphores,
):
    copies = assemble((kv0, kv1, kv2, kv3), wkv, place[0], semaphores, 0)
    copies += assemble((q0, q1, q2, q3), wq, place[0], semaphores, 4)
    turned = normed[...].astype(f32).T.astype(bf16)
    bq, bkv = back_q[...], back_kv[...]
    part = dot(turned[:, 512:], bq).astype(bf16)
    for b in range(8):
        for f in range(4):
            grads[f, 160 * b : 160 * b + 160, :] = part[
                160 * f : 160 * f + 160, 128 * b : 128 * b + 128
            ]
    part = dot(turned, bkv).astype(bf16)
    for b in range(4):
        for f in range(4):
            grads[f, 1280 + 160 * b : 1440 + 160 * b, :] = part[
                160 * f : 160 * f + 160, 128 * b : 128 * b + 128
            ]
    turned = back_attn[...].astype(f32).T.astype(bf16)
    part = dot(turned, attended[...]).astype(bf16)
    for f in range(4):
        for b in range(2):
            grads[f, 1920 + 640 * b : 2560 + 640 * b, :] = part[
                :, 256 * f + 128 * b : 256 * f + 128 * b + 128
            ]
    for copy in copies:
        copy.wait()
    e = dot(bkv[:512], wkv[...], rows_both)
    back_halo[...] = e.astype(bf16)
    x = halo[...].astype(f32)
    grad = jnp.sum(x * inverse_rms(x) * e, axis=0, keepdims=True)
    e = dot(bkv[512:], wkv[...], rows_both) + dot(bq, wq[...], rows_both)
    back_own[...] = e
    x = own[...].astype(f32)
    grad = grad + jnp.sum(x * inverse_rms(x) * e, axis=0, keepdims=True)
    each = jnp.concatenate([grad, gain_mid[0:3]], axis=0)
    heads = gain_head[0:2]
    for f in range(4):
        share = each[:, 160 * f : 160 * f + 160]
        rest = jnp.concatenate([share[:, 128:], jnp.zeros((4, 96), f32)], axis=1)
        ends = jnp.concatenate([heads[:, 64 * f : 64 * f + 64], jnp.zeros((2, 64), f32)], axis=1)
        tile = jnp.concatenate([share[:, :128], rest, ends, jnp.zeros((6, 128), f32)], axis=0)
        grads[f, 3200:3216, :] = tile.astype(bf16)
        grads[f, 3216:, :] = jnp.zeros((368, 128), bf16)
    for copy in split_out(grads, kept, sent, place[0], semaphores, 8):
        copy.wait()


def weights_part(
    place, normed, back_q, back_kv, attended, back_attn, halo, own, gain_mid, gain_head, shares
):
    return pl.pallas_call(
        weights_kernel,
        name="weights_part",
        in_specs=[pl.BlockSpec(memory_space=pltpu.SMEM)]
        + [whole()] * 9
        + [pl.BlockSpec(memory_space=pl.ANY)] * 8,
        out_specs=[whole()] * 2 + [pl.BlockSpec(memory_space=pl.ANY)] * 2,
        out_shape=[
            spec(512, 640, bf16),
            spec(512, 640, f32),
            spec(2, 3584, 128, bf16),
            spec(2, 3584, 128, bf16),
        ],
        scratch_shapes=[
            pltpu.VMEM((640, 1024), bf16),
            pltpu.VMEM((640, 512), bf16),
            pltpu.VMEM((4, 3584, 128), bf16),
            pltpu.SemaphoreType.DMA((12,)),
        ],
        compiler_params=params(40),
        cost_estimate=cost(3_400_000_000, 14_000_000),
    )(place, normed, back_q, back_kv, attended, back_attn, halo, own, gain_mid, gain_head, *shares)


def finish_kernel(own, back_own, returned, back_middle, gains, grad_in):
    x = own[...].astype(f32)
    e = back_own[...] + returned[...].astype(f32)
    grad_in[...] = (back_middle[...] + norm_back(x, inverse_rms(x), gains[0:1], e)).astype(bf16)


def finish(own, back_own, returned, back_middle, gains):
    row = lambda i: (i, 0)
    return pl.pallas_call(
        finish_kernel,
        name="finish",
        grid=(4,),
        in_specs=[pl.BlockSpec((128, 640), row)] * 4 + [pl.BlockSpec((8, 640), lambda i: (0, 0))],
        out_specs=pl.BlockSpec((128, 640), row),
        out_shape=spec(512, 640, bf16),
        compiler_params=params(10),
        cost_estimate=cost(4_000_000, 5_000_000),
    )(own, back_own, returned, back_middle, gains)


def rope_tables(offsets):
    powers = jnp.arange(128, dtype=f32) * (2.0 / 256)
    row = jnp.arange(512, dtype=jnp.int32)
    every = jnp.concatenate([offsets[0] - 512 + row, offsets])
    angles = every.astype(f32)[:, None] * (rope_base ** (-powers))[None, :]
    return jnp.cos(angles), jnp.sin(angles)


def unpack_kernel(
    spot, a0, a1, a2, a3, b0, b1, b2, b3, q, k, v, out, gate, up, down, gains, ffn, attn, semaphores
):
    x, y = spot[0], spot[1]
    copies = []
    for half, pieces in enumerate(((a0, a1, a2, a3), (b0, b1, b2, b3))):
        for i in range(4):
            for j in range(4):
                first, second = (x, y) if half == 0 else (y, x)
                block = 16 * half + (first - i + 4) % 4 * 4 + (second - j + 4) % 4
                n = (half * 4 + i) * 4 + j
                for m, (into, start, rows) in enumerate(((ffn, 0, 240), (attn, 240, 112))):
                    copies.append(
                        pltpu.make_async_copy(
                            pieces[i].at[j, pl.ds(start, rows), :],
                            into.at[pl.ds(pl.multiple_of(block * rows, 16), rows), :],
                            semaphores.at[2 * n + m],
                        )
                    )
    for copy in copies:
        copy.start()
    for copy in copies:
        copy.wait()
    for into, flat, first, count in (
        (gate, ffn, 0, 16),
        (up, ffn, 2560, 16),
        (q, attn, 0, 8),
        (k, attn, 1280, 2),
        (v, attn, 1600, 2),
    ):
        for b in range(count):
            at = first + 160 * b
            into[:, 128 * b : 128 * b + 128] = flat[at : at + 160, :].astype(f32)
    for into, flat, first, count in ((down, ffn, 5120, 4), (out, attn, 1920, 2)):
        for b in range(count):
            at = first + 640 * b
            into[128 * b : 128 * b + 128, :] = flat[at : at + 640, :].astype(f32).T
    gains[...] = attn[3200:3216, :].astype(f32)


def unpack(spot, pieces):
    return pl.pallas_call(
        unpack_kernel,
        name="unpack",
        in_specs=[pl.BlockSpec(memory_space=pltpu.SMEM)] + [pl.BlockSpec(memory_space=pl.ANY)] * 8,
        out_specs=[whole()] * 8,
        out_shape=[
            spec(160, 1024, f32),
            spec(160, 256, f32),
            spec(160, 256, f32),
            spec(256, 640, f32),
            spec(160, 2048, f32),
            spec(160, 2048, f32),
            spec(512, 640, f32),
            spec(16, 128, f32),
        ],
        scratch_shapes=[
            pltpu.VMEM((7680, 128), bf16),
            pltpu.VMEM((3584, 128), bf16),
            pltpu.SemaphoreType.DMA((64,)),
        ],
        compiler_params=params(20),
        cost_estimate=cost(4_000_000, 11_000_000),
    )(spot, *pieces)


def sum_of(parts):
    whole = parts[0].astype(f32)
    for part in parts[1:]:
        whole = whole + part.astype(f32)
    return whole.astype(bf16)


def turn_around(position, d):
    return lax.rem(position + d, 4)


def first_kernel(spot, kept, got, *outs):
    for half in range(2):
        for i, d in enumerate((0, 1, 3, 2)):
            at = turn_around(spot[half], d)
            for z in range(2):
                outs[4 * half + i][z] = sum_of([kept[z, half, at], got[z, half, at]])


def first_sums(spot, kept, got):
    rows = kept.shape[1]
    shape = (2, 2, 4, rows // 8, 128)
    return pl.pallas_call(
        first_kernel,
        name="first_sums",
        in_specs=[pl.BlockSpec(memory_space=pltpu.SMEM), whole(), whole()],
        out_specs=[whole()] * 8,
        out_shape=[spec(2, rows // 8, 128, bf16)] * 8,
        compiler_params=params(24),
        cost_estimate=cost(1_000_000, 6 * rows * 256),
    )(spot, kept.reshape(shape), got.reshape(shape))


def second_kernel(spot, *refs):
    ins, outs = refs[:16], refs[16:]
    for half in range(2):
        ffn, attn = ins[4 * half : 4 * half + 4], ins[8 + 4 * half : 12 + 4 * half]
        for i, d in enumerate((0, 1, 3, 2)):
            at = turn_around(spot[1 - half], d)
            for z in range(2):
                outs[4 * half + i][z, :240] = sum_of([r[z, at] for r in ffn])
                outs[4 * half + i][z, 240:] = sum_of([r[z, at] for r in attn])


def second_sums(spot, ffn, attn):
    ins = [p.reshape(2, 4, 240, 128) for p in ffn] + [p.reshape(2, 4, 112, 128) for p in attn]
    return pl.pallas_call(
        second_kernel,
        name="second_sums",
        in_specs=[pl.BlockSpec(memory_space=pltpu.SMEM)] + [whole()] * 16,
        out_specs=[whole()] * 8,
        out_shape=[spec(2, 352, 128, bf16)] * 8,
        compiler_params=params(20),
        cost_estimate=cost(1_000_000, 7_200_000),
    )(spot, *ins)


def third_kernel(place, *refs):
    ins, (mine, other) = refs[:8], refs[8:]
    z = lax.div(place[0], 2)
    for half in range(2):
        parts = ins[4 * half : 4 * half + 4]
        mine[half] = sum_of([r[z] for r in parts])
        other[half] = sum_of([r[1 - z] for r in parts])


def third_sums(place, parts):
    return pl.pallas_call(
        third_kernel,
        name="third_sums",
        in_specs=[pl.BlockSpec(memory_space=pltpu.SMEM)] + [whole()] * 8,
        out_specs=[whole()] * 2,
        out_shape=[spec(2, 352, 128, bf16)] * 2,
        compiler_params=params(10),
        cost_estimate=cost(1_000_000, 1_800_000),
    )(place, *parts)


def fourth_kernel(p0, p1, p2, p3, a, b):
    for half, out in enumerate((a, b)):
        out[...] = sum_of([p0[half], p1[half], p2[half], p3[half]])


def fourth_sums(parts):
    return pl.pallas_call(
        fourth_kernel,
        name="fourth_sums",
        in_specs=[whole()] * 4,
        out_specs=[whole()] * 2,
        out_shape=[spec(352, 128, bf16)] * 2,
        compiler_params=params(10),
        cost_estimate=cost(1_000_000, 900_000),
    )(*parts)


def seq_index(z, x, y):
    return (z % 2 * 4 + x % 4) * 4 + y % 4


def along_xy(dx, dy):
    return [
        (seq_index(z, x, y), seq_index(z, x + dx, y + dy))
        for z in range(2)
        for x in range(4)
        for y in range(4)
    ]


def along_z(step):
    pairs = []
    for s in range(32):
        for f in range(4):
            z = s // 16 * 2 + f // 2
            t = step(z)
            pairs.append((s * 4 + f, (t // 2 * 16 + s % 16) * 4 + t % 2 * 2 + f % 2))
    return pairs


def swap_core(value):
    return lax.ppermute(value, "fsdp", [(0, 1), (1, 0), (2, 3), (3, 2)])


def swap_near(value):
    return lax.ppermute(value, "fsdp", [(0, 2), (1, 3), (2, 0), (3, 1)])


def swap_far(value):
    return lax.ppermute(value, ("seq", "fsdp"), along_z(lambda z: 3 - z))


def swap_hi(value):
    return lax.ppermute(value, "seq", [(s, (s + 16) % 32) for s in range(32)])


def move_x(value, d):
    return lax.ppermute(value, "seq", along_xy(d, 0))


def move_y(value, d):
    return lax.ppermute(value, "seq", along_xy(0, d))


def shifted(value, steps):
    first, last = (max(0, -steps), min(32, 32 - steps))
    return lax.ppermute(value, "seq", [(source, source + steps) for source in range(first, last)])


steps = (1, 3, 2)


def move_first(parts):
    return (
        [parts[0]]
        + [move_x(p, d) for p, d in zip(parts[1:4], steps)]
        + [parts[4]]
        + [move_y(p, d) for p, d in zip(parts[5:8], steps)]
    )


def move_second(parts):
    return (
        [parts[0]]
        + [move_y(p, d) for p, d in zip(parts[1:4], steps)]
        + [parts[4]]
        + [move_x(p, d) for p, d in zip(parts[5:8], steps)]
    )


def together(*groups):
    leaves, tree = jax.tree.flatten(groups)
    return jax.tree.unflatten(tree, lax.optimization_barrier(tuple(leaves)))


def body(
    hidden_in,
    cotangent,
    positions,
    query_weight,
    key_weight,
    value_weight,
    output_weight,
    gate_weight,
    up_weight,
    down_weight,
    norm_in,
    norm_attn,
    norm_ffn_in,
    norm_ffn_out,
    norm_query,
    norm_key,
):
    s = lax.axis_index("seq")
    f = lax.axis_index("fsdp")
    x, y, z_lo, core = s // 4 % 4, s % 4, f // 2, f % 2
    place = f.astype(jnp.int32).reshape(1)
    spot = jnp.stack([x, y]).astype(jnp.int32)
    own = hidden_in[0]
    upstream = cotangent[0]
    offsets = positions[0]

    rows = [norm_in, norm_attn, norm_ffn_in, norm_ffn_out, norm_query, norm_key]
    rows = [jnp.pad(g[None], ((0, 0), (0, 512 - g.shape[0]))) for g in rows]
    kvg = jnp.concatenate(
        [jnp.concatenate([key_weight, value_weight], axis=1)]
        + rows
        + [jnp.zeros((2, 512), bf16)],
        axis=0,
    )
    q_partner = swap_near(query_weight)
    kvg_partner = swap_far(kvg)
    q_sibling = swap_core(query_weight)
    kvg_sibling = swap_core(kvg)
    halo = shifted(own, 1)
    (q_partner, kvg_partner), (wo, wg, wu, wd) = together(
        (q_partner, kvg_partner), (output_weight, gate_weight, up_weight, down_weight)
    )
    q_diagonal = swap_core(q_partner)
    kvg_diagonal = swap_core(kvg_partner)
    wo_partner, wg_partner = swap_near(wo), swap_near(wg)
    wu_partner, wd_partner = swap_far(wu), swap_far(wd)

    q_shares = (query_weight, q_sibling, q_partner, q_diagonal)
    kv_shares = (kvg, kvg_sibling, kvg_partner, kvg_diagonal)
    tails = [share[160:168] for share in kv_shares]
    tails = [
        jnp.where(
            j // 2 == z_lo,
            jnp.where(j % 2 == core, tails[0], tails[1]),
            jnp.where(j % 2 == core, tails[2], tails[3]),
        )
        for j in range(4)
    ]
    gains = jnp.concatenate([tail[:, :160] for tail in tails], axis=1).astype(f32)
    head_gains = jnp.concatenate([tail[:, :64] for tail in tails], axis=1).astype(f32)
    head_gains = jnp.concatenate([head_gains[4:8], head_gains[4:8]], axis=0)

    cosine, sine = rope_tables(offsets)
    column = offsets[:, None]
    normed, q, k, v, q_proj, k_proj = project(
        place, halo, own, gains, head_gains, q_shares, kv_shares, cosine, sine
    )
    attended, level = attend(q, k, v, column)
    attended, (wo, wg, wu, wd) = together(attended, (wo, wg, wu, wd))
    siblings = [swap_core(w) for w in (wo, wg, wu, wd)]
    attended, wo_partner, wg_partner = together(attended, wo_partner, wg_partner)
    attended, wu_partner, wd_partner = together(attended, wu_partner, wd_partner)
    wo_shares = [wo, siblings[0], wo_partner, swap_core(wo_partner)]
    wg_shares = [wg, siblings[1], wg_partner, swap_core(wg_partner)]
    wu_shares = [wu, siblings[2], wu_partner, swap_core(wu_partner)]
    wd_shares = [wd, siblings[3], wd_partner, swap_core(wd_partner)]
    layer_out, back_middle, back_attn, back_attended, gain_mid, kept, sent = middle_part(
        place, own, attended, upstream, gains, wo_shares + wg_shares + wu_shares + wd_shares
    )
    got = swap_core(sent)
    back_q, back_kv, gain_head = attend_back(
        q, k, v, column, level, back_attended, q_proj, k_proj, head_gains, cosine, sine
    )
    (back_q, back_kv), got = together((back_q, back_kv), got)
    ffn = first_sums(spot, kept, got)
    (back_q, back_kv), ffn = together((back_q, back_kv), ffn)
    ffn = move_first(ffn)
    back_halo, back_own, kept, sent = weights_part(
        place,
        normed,
        back_q,
        back_kv,
        attended,
        back_attn,
        halo,
        own,
        gain_mid,
        gain_head,
        q_shares + kv_shares,
    )
    got = swap_core(sent)
    returned = shifted(back_halo, -1)
    attn = move_first(first_sums(spot, kept, got))
    mine, other = third_sums(place, move_second(second_sums(spot, ffn, attn)))
    a, b = fourth_sums([mine, swap_near(other), swap_far(other), swap_hi(mine)])
    a = jnp.stack([a] + [move_y(a, d) for d in (1, 2, 3)])
    b = jnp.stack([b] + [move_x(b, d) for d in (1, 2, 3)])
    pieces = [a] + [move_x(a, d) for d in (1, 2, 3)] + [b] + [move_y(b, d) for d in (1, 2, 3)]
    grad_q, grad_k, grad_v, grad_o, grad_g, grad_u, grad_d, tile = unpack(spot, pieces)
    grad_in = finish(own, back_own, returned, back_middle, gains)
    wide = jnp.concatenate([tile[0:4], tile[4:8, :32]], axis=1)
    return (
        layer_out[None],
        grad_in[None],
        grad_q,
        grad_k,
        grad_v,
        grad_o,
        grad_g,
        grad_u,
        grad_d,
        wide[0],
        wide[1],
        wide[2],
        wide[3],
        tile[8, :64],
        tile[9, :64],
    )


def solution(mesh):
    three = P("fsdp", "seq", None)
    two = P("fsdp", None)
    one = P("fsdp")
    return jax.shard_map(
        body,
        mesh=mesh,
        in_specs=(three, three, P("fsdp", "seq")) + (two,) * 7 + (one,) * 6,
        out_specs=(three, three) + (two,) * 7 + (one,) * 6,
        check_vma=False,
    )
```

```python
import jax
import jax.numpy as jnp
from jax import lax
from jax.experimental import pallas as pl
from jax.experimental.pallas import tpu as pltpu
from jax.sharding import PartitionSpec as P

WINDOW = 512
epsilon = 1e-06
rope_base = 10000.0
masked_value = -1e30
bf16 = jnp.bfloat16
f32 = jnp.float32

rows_out = ((1,), (0,))
rows_both = ((1,), (1,))
cols_both = ((0,), (0,))


def dot(a, b, dims=rows_out):
    return lax.dot_general(a, b, (dims, ((), ())), preferred_element_type=f32)


def spec(*shape):
    return jax.ShapeDtypeStruct(shape[:-1], shape[-1])


def whole():
    return pl.BlockSpec(memory_space=pltpu.VMEM)


def params(mib):
    return pltpu.CompilerParams(vmem_limit_bytes=mib * 1024 * 1024)


def cost(flops, moved, exps=0):
    return pl.CostEstimate(flops=flops, bytes_accessed=moved, transcendentals=exps)


def inverse_rms(v):
    return lax.rsqrt(jnp.mean(v * v, axis=-1, keepdims=True) + epsilon)


def norm_back(v, r, gain, e):
    scaled = gain * e
    return r * scaled - v * (r * r * r * jnp.mean(v * scaled, axis=-1, keepdims=True))


def turn(v, cosine, sine):
    a, b = v[:, :128], v[:, 128:]
    return jnp.concatenate([a * cosine - b * sine, b * cosine + a * sine], axis=1)


def turn_back(v, cosine, sine):
    a, b = v[:, :128], v[:, 128:]
    return jnp.concatenate([a * cosine + b * sine, b * cosine - a * sine], axis=1)


def assemble(pieces, into, place, semaphores, first):
    rows = into.shape[0] // 4
    copies = []
    for r in range(4):
        at = pl.ds(pl.multiple_of((place ^ r) * rows, rows), rows)
        copies.append(
            pltpu.make_async_copy(
                pieces[r].at[pl.ds(0, rows), :], into.at[at, :], semaphores.at[first + r]
            )
        )
    for copy in copies:
        copy.start()
    return copies


def split_out(grads, kept, sent, place, semaphores, first):
    core = lax.rem(place, 2)
    copies = []
    for z in range(2):
        copies.append(
            pltpu.make_async_copy(
                grads.at[2 * z + 1 - core], sent.at[z], semaphores.at[first + 2 * z]
            )
        )
        copies.append(
            pltpu.make_async_copy(
                grads.at[2 * z + core], kept.at[z], semaphores.at[first + 2 * z + 1]
            )
        )
    for copy in copies:
        copy.start()
    return copies


def pack_kernel(g0, g1, g2, g3, g4, g5, k, v, kv, *rest):
    held, semaphores = rest[:6], rest[6]
    copies = [
        pltpu.make_async_copy(source, into, semaphores.at[i])
        for i, (source, into) in enumerate(zip((g0, g1, g2, g3, g4, g5), held))
    ]
    for copy in copies:
        copy.start()
    kv[:160, :256] = k[...]
    kv[:160, 256:] = v[...]
    tile = []
    for copy in copies:
        copy.wait()
    for i, ref in enumerate(held):
        n = ref.shape[0]
        row = ref[...].astype(f32).reshape(1, n)
        tile.append(jnp.concatenate([row, jnp.zeros((1, 512 - n), f32)], axis=1))
    tile.append(jnp.zeros((10, 512), f32))
    kv[160:, :] = jnp.concatenate(tile, axis=0).astype(bf16)


def pack(rows, key_weight, value_weight):
    return pl.pallas_call(
        pack_kernel,
        name="pack",
        in_specs=[pl.BlockSpec(memory_space=pl.ANY)] * 6 + [whole()] * 2,
        out_specs=whole(),
        out_shape=spec(176, 512, bf16),
        scratch_shapes=[pltpu.VMEM(row.shape, bf16) for row in rows]
        + [pltpu.SemaphoreType.DMA((6,))],
        compiler_params=params(4),
        cost_estimate=cost(100_000, 400_000),
    )(*rows, key_weight, value_weight)


def project_kernel(
    place,
    halo,
    own,
    gains,
    head_gains,
    q0,
    q1,
    q2,
    q3,
    kv0,
    kv1,
    kv2,
    kv3,
    cosine,
    sine,
    normed,
    q,
    k,
    v,
    q_proj,
    k_proj,
    wq,
    wkv,
    semaphores,
):
    i = pl.program_id(0)

    @pl.when(i == 0)
    def _():
        copies = assemble((kv0, kv1, kv2, kv3), wkv, place[0], semaphores, 0)
        copies += assemble((q0, q1, q2, q3), wq, place[0], semaphores, 4)
        for copy in copies:
            copy.wait()

    x = jnp.where(i < 2, halo[...], own[...]).astype(f32)
    n = (x * inverse_rms(x) * gains[0:1]).astype(bf16)
    normed[...] = n
    c, s = cosine[...], sine[...]
    kv = dot(n, wkv[...])
    kp = kv[:, :256]
    k_proj[...] = kp
    v[...] = kv[:, 256:].astype(bf16)
    k[...] = turn(kp * inverse_rms(kp) * head_gains[5:6], c, s).astype(bf16)

    @pl.when(i >= 2)
    def _():
        for h in range(4):
            cols = slice(256 * h, 256 * h + 256)
            qp = dot(n, wq[:, cols])
            q_proj[:, cols] = qp
            q[:, cols] = turn(qp * inverse_rms(qp) * head_gains[4:5], c, s).astype(bf16)


def project(place, halo, own, gains, head_gains, q_shares, kv_shares, cosine, sine):
    late = lambda i: (jnp.maximum(i - 2, 0), 0)
    row = lambda i: (i, 0)
    fixed = lambda i: (0, 0)
    return pl.pallas_call(
        project_kernel,
        name="project",
        grid=(4,),
        in_specs=[
            pl.BlockSpec(memory_space=pltpu.SMEM),
            pl.BlockSpec((256, 640), lambda i: (jnp.minimum(i, 1), 0)),
            pl.BlockSpec((256, 640), late),
            pl.BlockSpec((8, 640), fixed),
            pl.BlockSpec((8, 256), fixed),
        ]
        + [pl.BlockSpec(memory_space=pl.ANY)] * 8
        + [pl.BlockSpec((256, 128), row)] * 2,
        out_specs=[
            pl.BlockSpec((256, 640), row),
            pl.BlockSpec((256, 1024), late),
            pl.BlockSpec((256, 256), row),
            pl.BlockSpec((256, 256), row),
            pl.BlockSpec((256, 1024), late),
            pl.BlockSpec((256, 256), row),
        ],
        out_shape=[
            spec(1024, 640, bf16),
            spec(512, 1024, bf16),
            spec(1024, 256, bf16),
            spec(1024, 256, bf16),
            spec(512, 1024, f32),
            spec(1024, 256, f32),
        ],
        scratch_shapes=[
            pltpu.VMEM((640, 1024), bf16),
            pltpu.VMEM((640, 512), bf16),
            pltpu.SemaphoreType.DMA((8,)),
        ],
        compiler_params=params(20),
        cost_estimate=cost(1_350_000_000, 9_000_000),
    )(place, halo, own, gains, head_gains, *q_shares, *kv_shares, cosine, sine)


def visible_keys(offsets):
    distance = (
        lax.broadcasted_iota(jnp.int32, (256, 768), 0)
        + 512
        - lax.broadcasted_iota(jnp.int32, (256, 768), 1)
    )
    return (distance >= 0) & (distance < WINDOW) & (distance <= offsets)


def attend_kernel(q, k, v, offsets, attended, level):
    t = pl.program_id(0)
    near = pl.ds(pl.multiple_of(t * 256, 256), 768)
    keys, values = k[near, :], v[near, :]
    visible = visible_keys(offsets[...])
    for h in range(4):
        cols = slice(256 * h, 256 * h + 256)
        scores = jnp.where(visible, dot(q[:, cols], keys, rows_both) * 0.0625, masked_value)
        top = jnp.max(scores, axis=-1, keepdims=True)
        e = jnp.exp(scores - top)
        total = jnp.sum(e, axis=-1, keepdims=True)
        level[h] = top + jnp.log(total)
        probs = (e * (1.0 / total)).astype(bf16)
        attended[:, cols] = dot(probs, values).astype(bf16)


def attend(q, k, v, offsets):
    row = lambda i: (i, 0)
    fixed = lambda i: (0, 0)
    return pl.pallas_call(
        attend_kernel,
        name="attend",
        grid=(2,),
        in_specs=[
            pl.BlockSpec((256, 1024), row),
            pl.BlockSpec((1024, 256), fixed),
            pl.BlockSpec((1024, 256), fixed),
            pl.BlockSpec((256, 1), row),
        ],
        out_specs=[
            pl.BlockSpec((256, 1024), row),
            pl.BlockSpec((4, 256, 1), lambda i: (0, i, 0)),
        ],
        out_shape=[spec(512, 1024, bf16), spec(4, 512, 1, f32)],
        compiler_params=params(20),
        cost_estimate=cost(1_700_000_000, 4_000_000, 2_000_000),
    )(q, k, v, offsets)


def middle_kernel(
    place,
    x_ref,
    attended,
    upstream,
    gains,
    o0,
    o1,
    o2,
    o3,
    g0,
    g1,
    g2,
    g3,
    u0,
    u1,
    u2,
    u3,
    d0,
    d1,
    d2,
    d3,
    layer_out,
    back_middle,
    back_attn,
    back_attended,
    gain_grads,
    kept,
    sent,
    ffn_in,
    kept_a,
    kept_b,
    hidden,
    back_out,
    in_turned,
    out_turned,
    back_gate,
    back_up,
    wo,
    wg,
    wu,
    wd,
    grads,
    semaphores,
):
    output_copies = assemble((o0, o1, o2, o3), wo, place[0], semaphores, 0)
    gate_copies = assemble((g0, g1, g2, g3), wg, place[0], semaphores, 4)
    up_copies = assemble((u0, u1, u2, u3), wu, place[0], semaphores, 8)
    down_copies = assemble((d0, d1, d2, d3), wd, place[0], semaphores, 12)
    for copy in output_copies:
        copy.wait()
    g_attn, g_in, g_out = gains[1:2], gains[2:3], gains[3:4]
    ao = dot(attended[...], wo[...])
    r1 = inverse_rms(ao)
    mid = x_ref[...].astype(f32) + ao * r1 * g_attn
    r2 = inverse_rms(mid)
    ffn_in[...] = (mid * r2 * g_in).astype(bf16)
    for copy in gate_copies + up_copies:
        copy.wait()

    for j in range(8):
        cols = slice(256 * j, 256 * j + 256)
        u = dot(ffn_in[...], wg[:, cols])
        up = dot(ffn_in[...], wu[:, cols])
        root = 0.7978845608028654
        square = u * u
        t = jnp.tanh(u * (root + (root * 0.044715) * square))
        half = 0.5 + 0.5 * t
        act = u * half
        slope = half + act * (1.0 - t) * (root + (3 * 0.044715 * root) * square)
        hidden[:, cols] = (act * up).astype(bf16)
        kept_a[:, cols] = act
        kept_b[:, cols] = up * slope

    for copy in down_copies:
        copy.wait()
    fo = dot(hidden[...], wd[...])
    r3 = inverse_rms(fo)
    layer_out[...] = (mid + fo * r3 * g_out).astype(bf16)
    g = upstream[...].astype(f32)
    gain_grads[2:3] = jnp.sum(fo * r3 * g, axis=0, keepdims=True)
    bfo = norm_back(fo, r3, g_out, g)
    back_out[...] = bfo.astype(bf16)
    out_turned[...] = back_out[...].T
    in_turned[...] = ffn_in[...].T

    for j in range(8):
        cols = slice(256 * j, 256 * j + 256)
        bh = dot(back_out[...], wd[cols, :], rows_both)
        bu = (bh * kept_a[:, cols]).astype(bf16)
        bg = (bh * kept_b[:, cols]).astype(bf16)
        back_gate[:, cols] = bg
        back_up[:, cols] = bu

    for base, right in ((0, back_gate), (2560, back_up)):
        for j in range(2048 // 512):
            part = dot(in_turned[...], right[:, 512 * j : 512 * j + 512]).astype(bf16)
            for b in range(512 // 128):
                at = base + (512 // 128 * j + b) * 160
                for f in range(4):
                    grads[f, at : at + 160, :] = part[
                        160 * f : 160 * f + 160, 128 * b : 128 * b + 128
                    ]
    for f in range(4):
        part = dot(out_turned[...], hidden[:, 512 * f : 512 * f + 512]).astype(bf16)
        for b in range(4):
            at = 5120 + 640 * b
            grads[f, at : at + 640, :] = part[:, 128 * b : 128 * b + 128]

    outward = split_out(grads, kept, sent, place[0], semaphores, 16)
    e = dot(back_gate[...], wg[...], rows_both) + dot(back_up[...], wu[...], rows_both)
    gain_grads[1:2] = jnp.sum(mid * r2 * e, axis=0, keepdims=True)
    bm = g + norm_back(mid, r2, g_in, e)
    back_middle[...] = bm
    gain_grads[0:1] = jnp.sum(ao * r1 * bm, axis=0, keepdims=True)
    bao = norm_back(ao, r1, g_attn, bm).astype(bf16)
    back_attn[...] = bao
    back_attended[...] = dot(bao, wo[...], rows_both).astype(bf16)
    for copy in outward:
        copy.wait()


def middle_part(place, x, attended, upstream, gains, shares):
    return pl.pallas_call(
        middle_kernel,
        name="middle_part",
        in_specs=[pl.BlockSpec(memory_space=pltpu.SMEM)]
        + [whole()] * 4
        + [pl.BlockSpec(memory_space=pl.ANY)] * 16,
        out_specs=[whole()] * 5 + [pl.BlockSpec(memory_space=pl.ANY)] * 2,
        out_shape=[
            spec(512, 640, bf16),
            spec(512, 640, f32),
            spec(512, 640, bf16),
            spec(512, 1024, bf16),
            spec(8, 640, f32),
            spec(2, 7680, 128, bf16),
            spec(2, 7680, 128, bf16),
        ],
        scratch_shapes=[
            pltpu.VMEM((512, 640), bf16),
            pltpu.VMEM((512, 2048), f32),
            pltpu.VMEM((512, 2048), f32),
            pltpu.VMEM((512, 2048), bf16),
            pltpu.VMEM((512, 640), bf16),
            pltpu.VMEM((640, 512), bf16),
            pltpu.VMEM((640, 512), bf16),
            pltpu.VMEM((512, 2048), bf16),
            pltpu.VMEM((512, 2048), bf16),
            pltpu.VMEM((1024, 640), bf16),
            pltpu.VMEM((640, 2048), bf16),
            pltpu.VMEM((640, 2048), bf16),
            pltpu.VMEM((2048, 640), bf16),
            pltpu.VMEM((4, 7680, 128), bf16),
            pltpu.SemaphoreType.DMA((20,)),
        ],
        compiler_params=params(46),
        cost_estimate=cost(13_400_000_000, 23_000_000, 1_000_000),
    )(place, x, attended, upstream, gains, *shares)


def attend_back_kernel(
    q,
    k,
    v,
    offsets,
    level,
    back_attended,
    q_proj,
    k_proj,
    head_gains,
    cosine,
    sine,
    back_q,
    back_kv,
    gain_grads,
    sum_k,
    sum_v,
):
    t = pl.program_id(0)

    @pl.when(t == 0)
    def _():
        sum_k[...] = jnp.zeros_like(sum_k)
        sum_v[...] = jnp.zeros_like(sum_v)
        gain_grads[...] = jnp.zeros_like(gain_grads)

    near = pl.ds(pl.multiple_of(t * 256, 256), 768)
    mine = pl.ds(pl.multiple_of(t * 256 + 512, 256), 256)
    keys, values = k[near, :], v[near, :]
    visible = visible_keys(offsets[...])
    c, s = cosine[mine, :], sine[mine, :]
    for h in range(4):
        cols = slice(256 * h, 256 * h + 256)
        qh, bah = q[:, cols], back_attended[:, cols]
        scores = jnp.where(visible, dot(qh, keys, rows_both) * 0.0625, masked_value)
        probs = jnp.exp(scores - level[h])
        bp = dot(bah, values, rows_both)
        inner = jnp.sum(probs * bp, axis=-1, keepdims=True)
        bs = (probs * (bp - inner)).astype(bf16)
        sum_k[near, :] += dot(bs, qh, cols_both)
        sum_v[near, :] += dot(probs.astype(bf16), bah, cols_both)
        e = turn_back(dot(bs, keys) * 0.0625, c, s)
        qp = q_proj[:, cols]
        r = inverse_rms(qp)
        gain_grads[0:1] += jnp.sum(qp * r * e, axis=0, keepdims=True)
        back_q[:, cols] = norm_back(qp, r, head_gains[4:5], e).astype(bf16)

    @pl.when(t == 1)
    def _():
        e = turn_back(sum_k[...] * 0.0625, cosine[...], sine[...])
        kp = k_proj[...]
        r = inverse_rms(kp)
        gain_grads[1:2] = jnp.sum(kp * r * e, axis=0, keepdims=True)
        back_kv[:, :256] = norm_back(kp, r, head_gains[5:6], e).astype(bf16)
        back_kv[:, 256:] = sum_v[...].astype(bf16)


def attend_back(
    q, k, v, offsets, level, back_attended, q_proj, k_proj, head_gains, cosine, sine
):
    row = lambda i: (i, 0)
    fixed = lambda i: (0, 0)
    return pl.pallas_call(
        attend_back_kernel,
        name="attend_back",
        grid=(2,),
        in_specs=[
            pl.BlockSpec((256, 1024), row),
            pl.BlockSpec((1024, 256), fixed),
            pl.BlockSpec((1024, 256), fixed),
            pl.BlockSpec((256, 1), row),
            pl.BlockSpec((4, 256, 1), lambda i: (0, i, 0)),
            pl.BlockSpec((256, 1024), row),
            pl.BlockSpec((256, 1024), row),
            pl.BlockSpec((1024, 256), fixed),
            pl.BlockSpec((8, 256), fixed),
            pl.BlockSpec((1024, 128), fixed),
            pl.BlockSpec((1024, 128), fixed),
        ],
        out_specs=[
            pl.BlockSpec((256, 1024), row),
            pl.BlockSpec((1024, 512), fixed),
            pl.BlockSpec((8, 256), fixed),
        ],
        out_shape=[spec(512, 1024, bf16), spec(1024, 512, bf16), spec(8, 256, f32)],
        scratch_shapes=[pltpu.VMEM((1024, 256), f32), pltpu.VMEM((1024, 256), f32)],
        compiler_params=params(30),
        cost_estimate=cost(4_300_000_000, 10_000_000, 2_000_000),
    )(q, k, v, offsets, level, back_attended, q_proj, k_proj, head_gains, cosine, sine)


def weights_kernel(
    place,
    normed,
    back_q,
    back_kv,
    attended,
    back_attn,
    halo,
    own,
    gain_mid,
    gain_head,
    q0,
    q1,
    q2,
    q3,
    kv0,
    kv1,
    kv2,
    kv3,
    back_halo,
    back_own,
    kept,
    sent,
    wq,
    wkv,
    grads,
    semaphores,
):
    copies = assemble((kv0, kv1, kv2, kv3), wkv, place[0], semaphores, 0)
    copies += assemble((q0, q1, q2, q3), wq, place[0], semaphores, 4)
    turned = normed[...].astype(f32).T.astype(bf16)
    bq, bkv = back_q[...], back_kv[...]
    part = dot(turned[:, 512:], bq).astype(bf16)
    for b in range(8):
        for f in range(4):
            grads[f, 160 * b : 160 * b + 160, :] = part[
                160 * f : 160 * f + 160, 128 * b : 128 * b + 128
            ]
    part = dot(turned, bkv).astype(bf16)
    for b in range(4):
        for f in range(4):
            grads[f, 1280 + 160 * b : 1440 + 160 * b, :] = part[
                160 * f : 160 * f + 160, 128 * b : 128 * b + 128
            ]
    turned = back_attn[...].astype(f32).T.astype(bf16)
    part = dot(turned, attended[...]).astype(bf16)
    for f in range(4):
        for b in range(2):
            grads[f, 1920 + 640 * b : 2560 + 640 * b, :] = part[
                :, 256 * f + 128 * b : 256 * f + 128 * b + 128
            ]
    for copy in copies:
        copy.wait()
    e = dot(bkv[:512], wkv[...], rows_both)
    back_halo[...] = e.astype(bf16)
    x = halo[...].astype(f32)
    grad = jnp.sum(x * inverse_rms(x) * e, axis=0, keepdims=True)
    e = dot(bkv[512:], wkv[...], rows_both) + dot(bq, wq[...], rows_both)
    back_own[...] = e
    x = own[...].astype(f32)
    grad = grad + jnp.sum(x * inverse_rms(x) * e, axis=0, keepdims=True)
    each = jnp.concatenate([grad, gain_mid[0:3]], axis=0)
    heads = gain_head[0:2]
    for f in range(4):
        share = each[:, 160 * f : 160 * f + 160]
        rest = jnp.concatenate([share[:, 128:], jnp.zeros((4, 96), f32)], axis=1)
        ends = jnp.concatenate([heads[:, 64 * f : 64 * f + 64], jnp.zeros((2, 64), f32)], axis=1)
        tile = jnp.concatenate([share[:, :128], rest, ends, jnp.zeros((6, 128), f32)], axis=0)
        grads[f, 3200:3216, :] = tile.astype(bf16)
        grads[f, 3216:, :] = jnp.zeros((368, 128), bf16)
    for copy in split_out(grads, kept, sent, place[0], semaphores, 8):
        copy.wait()


def weights_part(
    place, normed, back_q, back_kv, attended, back_attn, halo, own, gain_mid, gain_head, shares
):
    return pl.pallas_call(
        weights_kernel,
        name="weights_part",
        in_specs=[pl.BlockSpec(memory_space=pltpu.SMEM)]
        + [whole()] * 9
        + [pl.BlockSpec(memory_space=pl.ANY)] * 8,
        out_specs=[whole()] * 2 + [pl.BlockSpec(memory_space=pl.ANY)] * 2,
        out_shape=[
            spec(512, 640, bf16),
            spec(512, 640, f32),
            spec(2, 3584, 128, bf16),
            spec(2, 3584, 128, bf16),
        ],
        scratch_shapes=[
            pltpu.VMEM((640, 1024), bf16),
            pltpu.VMEM((640, 512), bf16),
            pltpu.VMEM((4, 3584, 128), bf16),
            pltpu.SemaphoreType.DMA((12,)),
        ],
        compiler_params=params(40),
        cost_estimate=cost(3_400_000_000, 14_000_000),
    )(place, normed, back_q, back_kv, attended, back_attn, halo, own, gain_mid, gain_head, *shares)


def finish_kernel(own, back_own, returned, back_middle, gains, grad_in):
    x = own[...].astype(f32)
    e = back_own[...] + returned[...].astype(f32)
    grad_in[...] = (back_middle[...] + norm_back(x, inverse_rms(x), gains[0:1], e)).astype(bf16)


def finish(own, back_own, returned, back_middle, gains):
    row = lambda i: (i, 0)
    return pl.pallas_call(
        finish_kernel,
        name="finish",
        grid=(4,),
        in_specs=[pl.BlockSpec((128, 640), row)] * 4 + [pl.BlockSpec((8, 640), lambda i: (0, 0))],
        out_specs=pl.BlockSpec((128, 640), row),
        out_shape=spec(512, 640, bf16),
        compiler_params=params(10),
        cost_estimate=cost(4_000_000, 5_000_000),
    )(own, back_own, returned, back_middle, gains)


def rope_tables(offsets):
    powers = jnp.arange(128, dtype=f32) * (2.0 / 256)
    row = jnp.arange(512, dtype=jnp.int32)
    every = jnp.concatenate([offsets[0] - 512 + row, offsets])
    angles = every.astype(f32)[:, None] * (rope_base ** (-powers))[None, :]
    return jnp.cos(angles), jnp.sin(angles)


def unpack_kernel(spot, a0, a1, a2, a3, b0, b1, b2, b3, *rest):
    outs, gains, held, (ffn, attn, semaphores) = rest[:7], rest[7], rest[8:15], rest[15:]
    q, k, v, out, gate, up, down = held
    x, y = spot[0], spot[1]
    copies = []
    for half, pieces in enumerate(((a0, a1, a2, a3), (b0, b1, b2, b3))):
        for i in range(4):
            for j in range(4):
                first, second = (x, y) if half == 0 else (y, x)
                block = 16 * half + lax.rem(first - i + 4, 4) * 4 + lax.rem(second - j + 4, 4)
                n = (half * 4 + i) * 4 + j
                for m, (into, start, rows) in enumerate(((ffn, 0, 240), (attn, 240, 112))):
                    copies.append(
                        pltpu.make_async_copy(
                            pieces[i].at[j, pl.ds(start, rows), :],
                            into.at[pl.ds(pl.multiple_of(block * rows, 16), rows), :],
                            semaphores.at[2 * n + m],
                        )
                    )
    for copy in copies:
        copy.start()
    for copy in copies:
        copy.wait()
    outward = []

    def leave(n):
        copy = pltpu.make_async_copy(held[n], outs[n], semaphores.at[64 + n])
        copy.start()
        outward.append(copy)

    for n, into, flat, first, count in (
        (4, gate, ffn, 0, 16),
        (5, up, ffn, 2560, 16),
        (0, q, attn, 0, 8),
        (1, k, attn, 1280, 2),
        (2, v, attn, 1600, 2),
    ):
        for b in range(count):
            at = first + 160 * b
            into[:, 128 * b : 128 * b + 128] = flat[at : at + 160, :].astype(f32)
        leave(n)
    for n, into, flat, first, count in ((6, down, ffn, 5120, 4), (3, out, attn, 1920, 2)):
        for b in range(count):
            at = first + 640 * b
            into[128 * b : 128 * b + 128, :] = flat[at : at + 640, :].astype(f32).T
        leave(n)
    gains[...] = attn[3200:3216, :].astype(f32)
    for copy in outward:
        copy.wait()


def unpack(spot, pieces):
    shapes = [(160, 1024), (160, 256), (160, 256), (256, 640), (160, 2048), (160, 2048), (512, 640)]
    return pl.pallas_call(
        unpack_kernel,
        name="unpack",
        in_specs=[pl.BlockSpec(memory_space=pltpu.SMEM)] + [pl.BlockSpec(memory_space=pl.ANY)] * 8,
        out_specs=[pl.BlockSpec(memory_space=pl.ANY)] * 7 + [whole()],
        out_shape=[spec(*shape, f32) for shape in shapes] + [spec(16, 128, f32)],
        scratch_shapes=[pltpu.VMEM(shape, f32) for shape in shapes]
        + [
            pltpu.VMEM((7680, 128), bf16),
            pltpu.VMEM((3584, 128), bf16),
            pltpu.SemaphoreType.DMA((71,)),
        ],
        compiler_params=params(20),
        cost_estimate=cost(4_000_000, 11_000_000),
    )(spot, *pieces)


def sum_of(parts):
    whole = parts[0].astype(f32)
    for part in parts[1:]:
        whole = whole + part.astype(f32)
    return whole.astype(bf16)


def turn_around(position, d):
    return lax.rem(position + d, 4)


def first_kernel(spot, kept_ffn, got_ffn, kept_attn, got_attn, *outs):
    for half in range(2):
        for i, d in enumerate((0, 1, 3, 2)):
            at = turn_around(spot[half], d)
            out = outs[4 * half + i]
            for z in range(2):
                for j in range(4):
                    out[z, j, :240] = sum_of([r[z, half, at, j] for r in (kept_ffn, got_ffn)])
                    out[z, j, 240:] = sum_of([r[z, half, at, j] for r in (kept_attn, got_attn)])


def first_sums(spot, kept_ffn, got_ffn, kept_attn, got_attn):
    ins = [p.reshape(2, 2, 4, 4, p.shape[1] // 32, 128) for p in (kept_ffn, got_ffn, kept_attn, got_attn)]
    return pl.pallas_call(
        first_kernel,
        name="first_sums",
        in_specs=[pl.BlockSpec(memory_space=pltpu.SMEM)] + [whole()] * 4,
        out_specs=[whole()] * 8,
        out_shape=[spec(2, 4, 352, 128, bf16)] * 8,
        compiler_params=params(30),
        cost_estimate=cost(3_000_000, 17_000_000),
    )(spot, *ins)


def second_kernel(spot, *refs):
    ins, outs = refs[:8], refs[8:]
    for half in range(2):
        parts = ins[4 * half : 4 * half + 4]
        for i, d in enumerate((0, 1, 3, 2)):
            at = turn_around(spot[1 - half], d)
            for z in range(2):
                outs[4 * half + i][z] = sum_of([r[z, at] for r in parts])


def second_sums(spot, parts):
    return pl.pallas_call(
        second_kernel,
        name="second_sums",
        in_specs=[pl.BlockSpec(memory_space=pltpu.SMEM)] + [whole()] * 8,
        out_specs=[whole()] * 8,
        out_shape=[spec(2, 352, 128, bf16)] * 8,
        compiler_params=params(20),
        cost_estimate=cost(1_000_000, 7_200_000),
    )(spot, *parts)


def third_kernel(place, *refs):
    ins, (mine, other) = refs[:8], refs[8:]
    z = lax.div(place[0], 2)
    for half in range(2):
        parts = ins[4 * half : 4 * half + 4]
        mine[half] = sum_of([r[z] for r in parts])
        other[half] = sum_of([r[1 - z] for r in parts])


def third_sums(place, parts):
    return pl.pallas_call(
        third_kernel,
        name="third_sums",
        in_specs=[pl.BlockSpec(memory_space=pltpu.SMEM)] + [whole()] * 8,
        out_specs=[whole()] * 2,
        out_shape=[spec(2, 352, 128, bf16)] * 2,
        compiler_params=params(10),
        cost_estimate=cost(1_000_000, 1_800_000),
    )(place, *parts)


def fourth_kernel(p0, p1, p2, p3, a, b):
    for half, out in enumerate((a, b)):
        out[...] = sum_of([p0[half], p1[half], p2[half], p3[half]])


def fourth_sums(parts):
    return pl.pallas_call(
        fourth_kernel,
        name="fourth_sums",
        in_specs=[whole()] * 4,
        out_specs=[whole()] * 2,
        out_shape=[spec(352, 128, bf16)] * 2,
        compiler_params=params(10),
        cost_estimate=cost(1_000_000, 900_000),
    )(*parts)


def seq_index(z, x, y):
    return (z % 2 * 4 + x % 4) * 4 + y % 4


def along_xy(dx, dy):
    return [
        (seq_index(z, x, y), seq_index(z, x + dx, y + dy))
        for z in range(2)
        for x in range(4)
        for y in range(4)
    ]


def along_z(step):
    pairs = []
    for s in range(32):
        for f in range(4):
            z = s // 16 * 2 + f // 2
            t = step(z)
            pairs.append((s * 4 + f, (t // 2 * 16 + s % 16) * 4 + t % 2 * 2 + f % 2))
    return pairs


def swap_core(value):
    return lax.ppermute(value, "fsdp", [(0, 1), (1, 0), (2, 3), (3, 2)])


def swap_near(value):
    return lax.ppermute(value, "fsdp", [(0, 2), (1, 3), (2, 0), (3, 1)])


def swap_far(value):
    return lax.ppermute(value, ("seq", "fsdp"), along_z(lambda z: 3 - z))


def swap_hi(value):
    return lax.ppermute(value, "seq", [(s, (s + 16) % 32) for s in range(32)])


def move_x(value, d):
    return lax.ppermute(value, "seq", along_xy(d, 0))


def move_y(value, d):
    return lax.ppermute(value, "seq", along_xy(0, d))


def shifted(value, steps):
    first, last = (max(0, -steps), min(32, 32 - steps))
    return lax.ppermute(value, "seq", [(source, source + steps) for source in range(first, last)])


steps = (1, 3, 2)


def move_first(parts):
    return (
        [parts[0]]
        + [move_x(p, d) for p, d in zip(parts[1:4], steps)]
        + [parts[4]]
        + [move_y(p, d) for p, d in zip(parts[5:8], steps)]
    )


def move_second(parts):
    return (
        [parts[0]]
        + [move_y(p, d) for p, d in zip(parts[1:4], steps)]
        + [parts[4]]
        + [move_x(p, d) for p, d in zip(parts[5:8], steps)]
    )


def together(*groups):
    leaves, tree = jax.tree.flatten(groups)
    return jax.tree.unflatten(tree, lax.optimization_barrier(tuple(leaves)))


def body(
    hidden_in,
    cotangent,
    positions,
    query_weight,
    key_weight,
    value_weight,
    output_weight,
    gate_weight,
    up_weight,
    down_weight,
    norm_in,
    norm_attn,
    norm_ffn_in,
    norm_ffn_out,
    norm_query,
    norm_key,
):
    s = lax.axis_index("seq")
    f = lax.axis_index("fsdp")
    x, y, z_lo, core = s // 4 % 4, s % 4, f // 2, f % 2
    place = f.astype(jnp.int32).reshape(1)
    spot = jnp.stack([x, y]).astype(jnp.int32)
    own = hidden_in[0]
    upstream = cotangent[0]
    offsets = positions[0]

    q_partner = swap_near(query_weight)
    kv = pack(
        [norm_in, norm_attn, norm_ffn_in, norm_ffn_out, norm_query, norm_key],
        key_weight,
        value_weight,
    )
    kv_partner = swap_far(kv)
    q_sibling = swap_core(query_weight)
    kv_sibling = swap_core(kv)
    halo = shifted(own, 1)
    (q_sibling, kv_sibling), (wg, wu) = together(
        (q_sibling, kv_sibling), (gate_weight, up_weight)
    )
    wg_partner, wu_partner = swap_near(wg), swap_far(wu)
    q_diagonal = swap_core(q_partner)
    kv_diagonal = swap_core(kv_partner)
    (q_diagonal, kv_diagonal), (wo, wd) = together(
        (q_diagonal, kv_diagonal), (output_weight, down_weight)
    )
    wo_partner, wd_partner = swap_near(wo), swap_far(wd)
    q_shares = (query_weight, q_sibling, q_partner, q_diagonal)
    kv_shares = (kv, kv_sibling, kv_partner, kv_diagonal)
    tails = [share[160:168] for share in kv_shares]
    tails = [
        jnp.where(
            j // 2 == z_lo,
            jnp.where(j % 2 == core, tails[0], tails[1]),
            jnp.where(j % 2 == core, tails[2], tails[3]),
        )
        for j in range(4)
    ]
    gains = jnp.concatenate([tail[:, :160] for tail in tails], axis=1).astype(f32)
    head_gains = jnp.concatenate([tail[:, :64] for tail in tails], axis=1).astype(f32)

    cosine, sine = rope_tables(offsets)
    column = offsets[:, None]
    normed, q, k, v, q_proj, k_proj = project(
        place, halo, own, gains, head_gains, q_shares, kv_shares, cosine, sine
    )
    attended, level = attend(q, k, v, column)
    attended, (wo, wg, wu, wd) = together(attended, (wo, wg, wu, wd))
    siblings = [swap_core(w) for w in (wo, wg, wu, wd)]
    attended, wo_partner, wg_partner = together(attended, wo_partner, wg_partner)
    attended, wu_partner, wd_partner = together(attended, wu_partner, wd_partner)
    wo_shares = [wo, siblings[0], wo_partner, swap_core(wo_partner)]
    wg_shares = [wg, siblings[1], wg_partner, swap_core(wg_partner)]
    wu_shares = [wu, siblings[2], wu_partner, swap_core(wu_partner)]
    wd_shares = [wd, siblings[3], wd_partner, swap_core(wd_partner)]
    layer_out, back_middle, back_attn, back_attended, gain_mid, kept, sent = middle_part(
        place, own, attended, upstream, gains, wo_shares + wg_shares + wu_shares + wd_shares
    )
    got = swap_core(sent)
    back_q, back_kv, gain_head = attend_back(
        q, k, v, column, level, back_attended, q_proj, k_proj, head_gains, cosine, sine
    )
    back_halo, back_own, kept_attn, sent = weights_part(
        place,
        normed,
        back_q,
        back_kv,
        attended,
        back_attn,
        halo,
        own,
        gain_mid,
        gain_head,
        q_shares + kv_shares,
    )
    got_attn = swap_core(sent)
    first = move_first(first_sums(spot, kept, got, kept_attn, got_attn))
    returned = shifted(back_halo, -1)
    mine, other = third_sums(place, move_second(second_sums(spot, first)))
    a, b = fourth_sums([mine, swap_near(other), swap_far(other), swap_hi(mine)])
    a = jnp.stack([a] + [move_y(a, d) for d in (1, 2, 3)])
    b = jnp.stack([b] + [move_x(b, d) for d in (1, 2, 3)])
    a, b = together(a, b)
    pieces = [a] + [move_x(a, d) for d in (1, 2, 3)] + [b] + [move_y(b, d) for d in (1, 2, 3)]
    grad_q, grad_k, grad_v, grad_o, grad_g, grad_u, grad_d, tile = unpack(spot, pieces)
    grad_in = finish(own, back_own, returned, back_middle, gains)
    wide = jnp.concatenate([tile[0:4], tile[4:8, :32]], axis=1)
    return (
        layer_out[None],
        grad_in[None],
        grad_q,
        grad_k,
        grad_v,
        grad_o,
        grad_g,
        grad_u,
        grad_d,
        wide[0],
        wide[1],
        wide[2],
        wide[3],
        tile[8, :64],
        tile[9, :64],
    )


def solution(mesh):
    three = P("fsdp", "seq", None)
    two = P("fsdp", None)
    one = P("fsdp")
    return jax.shard_map(
        body,
        mesh=mesh,
        in_specs=(three, three, P("fsdp", "seq")) + (two,) * 7 + (one,) * 6,
        out_specs=(three, three) + (two,) * 7 + (one,) * 6,
        check_vma=False,
    )
```

```python
import jax
import jax.numpy as jnp
from jax import lax
from jax.experimental import pallas as pl
from jax.experimental.pallas import tpu as pltpu
from jax.sharding import PartitionSpec as P

WINDOW = 512
epsilon = 1e-06
rope_base = 10000.0
masked_value = -1e30
bf16 = jnp.bfloat16
f32 = jnp.float32

rows_out = ((1,), (0,))
rows_both = ((1,), (1,))
cols_both = ((0,), (0,))


def dot(a, b, dims=rows_out):
    return lax.dot_general(a, b, (dims, ((), ())), preferred_element_type=f32)


def spec(*shape):
    return jax.ShapeDtypeStruct(shape[:-1], shape[-1])


def whole():
    return pl.BlockSpec(memory_space=pltpu.VMEM)


def params(mib):
    return pltpu.CompilerParams(vmem_limit_bytes=mib * 1024 * 1024)


def cost(flops, moved, exps=0):
    return pl.CostEstimate(flops=flops, bytes_accessed=moved, transcendentals=exps)


def inverse_rms(v):
    return lax.rsqrt(jnp.mean(v * v, axis=-1, keepdims=True) + epsilon)


def norm_back(v, r, gain, e):
    scaled = gain * e
    return r * scaled - v * (r * r * r * jnp.mean(v * scaled, axis=-1, keepdims=True))


def turn(v, cosine, sine):
    a, b = v[:, :128], v[:, 128:]
    return jnp.concatenate([a * cosine - b * sine, b * cosine + a * sine], axis=1)


def turn_back(v, cosine, sine):
    a, b = v[:, :128], v[:, 128:]
    return jnp.concatenate([a * cosine + b * sine, b * cosine - a * sine], axis=1)


def assemble(pieces, into, place, semaphores, first):
    rows = into.shape[0] // 4
    copies = []
    for r in range(4):
        at = pl.ds(pl.multiple_of((place ^ r) * rows, rows), rows)
        copies.append(
            pltpu.make_async_copy(
                pieces[r].at[pl.ds(0, rows), :], into.at[at, :], semaphores.at[first + r]
            )
        )
    for copy in copies:
        copy.start()
    return copies


def split_out(grads, kept, sent, place, semaphores, first):
    core = lax.rem(place, 2)
    copies = []
    for z in range(2):
        copies.append(
            pltpu.make_async_copy(
                grads.at[2 * z + 1 - core], sent.at[z], semaphores.at[first + 2 * z]
            )
        )
        copies.append(
            pltpu.make_async_copy(
                grads.at[2 * z + core], kept.at[z], semaphores.at[first + 2 * z + 1]
            )
        )
    for copy in copies:
        copy.start()
    return copies


def pack_kernel(g0, g1, g2, g3, g4, g5, k, v, kv, *rest):
    held, semaphores = rest[:6], rest[6]
    copies = [
        pltpu.make_async_copy(source, into, semaphores.at[i])
        for i, (source, into) in enumerate(zip((g0, g1, g2, g3, g4, g5), held))
    ]
    for copy in copies:
        copy.start()
    kv[:160, :256] = k[...]
    kv[:160, 256:] = v[...]
    tile = []
    for copy in copies:
        copy.wait()
    for i, ref in enumerate(held):
        n = ref.shape[0]
        row = ref[...].astype(f32).reshape(1, n)
        tile.append(jnp.concatenate([row, jnp.zeros((1, 512 - n), f32)], axis=1))
    tile.append(jnp.zeros((10, 512), f32))
    kv[160:, :] = jnp.concatenate(tile, axis=0).astype(bf16)


def pack(rows, key_weight, value_weight):
    return pl.pallas_call(
        pack_kernel,
        name="pack",
        in_specs=[pl.BlockSpec(memory_space=pltpu.HBM)] * 6 + [whole()] * 2,
        out_specs=whole(),
        out_shape=spec(176, 512, bf16),
        scratch_shapes=[pltpu.VMEM(row.shape, bf16) for row in rows]
        + [pltpu.SemaphoreType.DMA((6,))],
        compiler_params=params(4),
        cost_estimate=cost(100_000, 400_000),
    )(*rows, key_weight, value_weight)


def project_kernel(
    place,
    halo,
    own,
    gains,
    head_gains,
    q0,
    q1,
    q2,
    q3,
    kv0,
    kv1,
    kv2,
    kv3,
    cosine,
    sine,
    normed,
    q,
    k,
    v,
    q_proj,
    k_proj,
    wq,
    wkv,
    semaphores,
):
    i = pl.program_id(0)

    @pl.when(i == 0)
    def _():
        copies = assemble((kv0, kv1, kv2, kv3), wkv, place[0], semaphores, 0)
        copies += assemble((q0, q1, q2, q3), wq, place[0], semaphores, 4)
        for copy in copies:
            copy.wait()

    x = jnp.where(i < 2, halo[...], own[...]).astype(f32)
    n = (x * inverse_rms(x) * gains[0:1]).astype(bf16)
    normed[...] = n
    c, s = cosine[...], sine[...]
    kv = dot(n, wkv[...])
    kp = kv[:, :256]
    k_proj[...] = kp
    v[...] = kv[:, 256:].astype(bf16)
    k[...] = turn(kp * inverse_rms(kp) * head_gains[5:6], c, s).astype(bf16)

    @pl.when(i >= 2)
    def _():
        for h in range(4):
            cols = slice(256 * h, 256 * h + 256)
            qp = dot(n, wq[:, cols])
            q_proj[:, cols] = qp
            q[:, cols] = turn(qp * inverse_rms(qp) * head_gains[4:5], c, s).astype(bf16)


def project(place, halo, own, gains, head_gains, q_shares, kv_shares, cosine, sine):
    late = lambda i: (jnp.maximum(i - 2, 0), 0)
    row = lambda i: (i, 0)
    fixed = lambda i: (0, 0)
    return pl.pallas_call(
        project_kernel,
        name="project",
        grid=(4,),
        in_specs=[
            pl.BlockSpec(memory_space=pltpu.SMEM),
            pl.BlockSpec((256, 640), lambda i: (jnp.minimum(i, 1), 0)),
            pl.BlockSpec((256, 640), late),
            pl.BlockSpec((8, 640), fixed),
            pl.BlockSpec((8, 256), fixed),
        ]
        + [pl.BlockSpec(memory_space=pltpu.HBM)] * 8
        + [pl.BlockSpec((256, 128), row)] * 2,
        out_specs=[
            pl.BlockSpec((256, 640), row),
            pl.BlockSpec((256, 1024), late),
            pl.BlockSpec((256, 256), row),
            pl.BlockSpec((256, 256), row),
            pl.BlockSpec((256, 1024), late),
            pl.BlockSpec((256, 256), row),
        ],
        out_shape=[
            spec(1024, 640, bf16),
            spec(512, 1024, bf16),
            spec(1024, 256, bf16),
            spec(1024, 256, bf16),
            spec(512, 1024, f32),
            spec(1024, 256, f32),
        ],
        scratch_shapes=[
            pltpu.VMEM((640, 1024), bf16),
            pltpu.VMEM((640, 512), bf16),
            pltpu.SemaphoreType.DMA((8,)),
        ],
        compiler_params=params(20),
        cost_estimate=cost(1_350_000_000, 9_000_000),
    )(place, halo, own, gains, head_gains, *q_shares, *kv_shares, cosine, sine)


def visible_keys(offsets):
    distance = (
        lax.broadcasted_iota(jnp.int32, (256, 768), 0)
        + 512
        - lax.broadcasted_iota(jnp.int32, (256, 768), 1)
    )
    return (distance >= 0) & (distance < WINDOW) & (distance <= offsets)


def attend_kernel(q, k, v, offsets, attended, level):
    t = pl.program_id(0)
    near = pl.ds(pl.multiple_of(t * 256, 256), 768)
    keys, values = k[near, :], v[near, :]
    visible = visible_keys(offsets[...])
    for h in range(4):
        cols = slice(256 * h, 256 * h + 256)
        scores = jnp.where(visible, dot(q[:, cols], keys, rows_both) * 0.0625, masked_value)
        top = jnp.max(scores, axis=-1, keepdims=True)
        e = jnp.exp(scores - top)
        total = jnp.sum(e, axis=-1, keepdims=True)
        level[h] = top + jnp.log(total)
        probs = (e * (1.0 / total)).astype(bf16)
        attended[:, cols] = dot(probs, values).astype(bf16)


def attend(q, k, v, offsets):
    row = lambda i: (i, 0)
    fixed = lambda i: (0, 0)
    return pl.pallas_call(
        attend_kernel,
        name="attend",
        grid=(2,),
        in_specs=[
            pl.BlockSpec((256, 1024), row),
            pl.BlockSpec((1024, 256), fixed),
            pl.BlockSpec((1024, 256), fixed),
            pl.BlockSpec((256, 1), row),
        ],
        out_specs=[
            pl.BlockSpec((256, 1024), row),
            pl.BlockSpec((4, 256, 1), lambda i: (0, i, 0)),
        ],
        out_shape=[spec(512, 1024, bf16), spec(4, 512, 1, f32)],
        compiler_params=params(20),
        cost_estimate=cost(1_700_000_000, 4_000_000, 2_000_000),
    )(q, k, v, offsets)


def middle_kernel(
    place,
    x_ref,
    attended,
    upstream,
    gains,
    o0,
    o1,
    o2,
    o3,
    g0,
    g1,
    g2,
    g3,
    u0,
    u1,
    u2,
    u3,
    d0,
    d1,
    d2,
    d3,
    layer_out,
    back_middle,
    back_attn,
    back_attended,
    gain_grads,
    kept,
    sent,
    ffn_in,
    kept_a,
    kept_b,
    hidden,
    back_out,
    in_turned,
    out_turned,
    back_gate,
    back_up,
    wo,
    wg,
    wu,
    wd,
    grads,
    semaphores,
):
    output_copies = assemble((o0, o1, o2, o3), wo, place[0], semaphores, 0)
    gate_copies = assemble((g0, g1, g2, g3), wg, place[0], semaphores, 4)
    up_copies = assemble((u0, u1, u2, u3), wu, place[0], semaphores, 8)
    down_copies = assemble((d0, d1, d2, d3), wd, place[0], semaphores, 12)
    for copy in output_copies:
        copy.wait()
    g_attn, g_in, g_out = gains[1:2], gains[2:3], gains[3:4]
    ao = dot(attended[...], wo[...])
    r1 = inverse_rms(ao)
    mid = x_ref[...].astype(f32) + ao * r1 * g_attn
    r2 = inverse_rms(mid)
    ffn_in[...] = (mid * r2 * g_in).astype(bf16)
    for copy in gate_copies + up_copies:
        copy.wait()

    for j in range(8):
        cols = slice(256 * j, 256 * j + 256)
        u = dot(ffn_in[...], wg[:, cols])
        up = dot(ffn_in[...], wu[:, cols])
        root = 0.7978845608028654
        square = u * u
        t = jnp.tanh(u * (root + (root * 0.044715) * square))
        half = 0.5 + 0.5 * t
        act = u * half
        slope = half + act * (1.0 - t) * (root + (3 * 0.044715 * root) * square)
        hidden[:, cols] = (act * up).astype(bf16)
        kept_a[:, cols] = act
        kept_b[:, cols] = up * slope

    for copy in down_copies:
        copy.wait()
    fo = dot(hidden[...], wd[...])
    r3 = inverse_rms(fo)
    layer_out[...] = (mid + fo * r3 * g_out).astype(bf16)
    g = upstream[...].astype(f32)
    gain_grads[2:3] = jnp.sum(fo * r3 * g, axis=0, keepdims=True)
    bfo = norm_back(fo, r3, g_out, g)
    back_out[...] = bfo.astype(bf16)
    out_turned[...] = back_out[...].T
    in_turned[...] = ffn_in[...].T

    for j in range(8):
        cols = slice(256 * j, 256 * j + 256)
        bh = dot(back_out[...], wd[cols, :], rows_both)
        bu = (bh * kept_a[:, cols]).astype(bf16)
        bg = (bh * kept_b[:, cols]).astype(bf16)
        back_gate[:, cols] = bg
        back_up[:, cols] = bu

    for base, right in ((0, back_gate), (2560, back_up)):
        for j in range(2048 // 512):
            part = dot(in_turned[...], right[:, 512 * j : 512 * j + 512]).astype(bf16)
            for b in range(512 // 128):
                at = base + (512 // 128 * j + b) * 160
                for f in range(4):
                    grads[f, at : at + 160, :] = part[
                        160 * f : 160 * f + 160, 128 * b : 128 * b + 128
                    ]
    for f in range(4):
        part = dot(out_turned[...], hidden[:, 512 * f : 512 * f + 512]).astype(bf16)
        for b in range(4):
            at = 5120 + 640 * b
            grads[f, at : at + 640, :] = part[:, 128 * b : 128 * b + 128]

    outward = split_out(grads, kept, sent, place[0], semaphores, 16)
    e = dot(back_gate[...], wg[...], rows_both) + dot(back_up[...], wu[...], rows_both)
    gain_grads[1:2] = jnp.sum(mid * r2 * e, axis=0, keepdims=True)
    bm = g + norm_back(mid, r2, g_in, e)
    back_middle[...] = bm
    gain_grads[0:1] = jnp.sum(ao * r1 * bm, axis=0, keepdims=True)
    bao = norm_back(ao, r1, g_attn, bm).astype(bf16)
    back_attn[...] = bao
    back_attended[...] = dot(bao, wo[...], rows_both).astype(bf16)
    for copy in outward:
        copy.wait()


def middle_part(place, x, attended, upstream, gains, shares):
    return pl.pallas_call(
        middle_kernel,
        name="middle_part",
        in_specs=[pl.BlockSpec(memory_space=pltpu.SMEM)]
        + [whole()] * 4
        + [pl.BlockSpec(memory_space=pltpu.HBM)] * 16,
        out_specs=[whole()] * 5 + [pl.BlockSpec(memory_space=pltpu.HBM)] * 2,
        out_shape=[
            spec(512, 640, bf16),
            spec(512, 640, f32),
            spec(512, 640, bf16),
            spec(512, 1024, bf16),
            spec(8, 640, f32),
            spec(2, 7680, 128, bf16),
            spec(2, 7680, 128, bf16),
        ],
        scratch_shapes=[
            pltpu.VMEM((512, 640), bf16),
            pltpu.VMEM((512, 2048), f32),
            pltpu.VMEM((512, 2048), f32),
            pltpu.VMEM((512, 2048), bf16),
            pltpu.VMEM((512, 640), bf16),
            pltpu.VMEM((640, 512), bf16),
            pltpu.VMEM((640, 512), bf16),
            pltpu.VMEM((512, 2048), bf16),
            pltpu.VMEM((512, 2048), bf16),
            pltpu.VMEM((1024, 640), bf16),
            pltpu.VMEM((640, 2048), bf16),
            pltpu.VMEM((640, 2048), bf16),
            pltpu.VMEM((2048, 640), bf16),
            pltpu.VMEM((4, 7680, 128), bf16),
            pltpu.SemaphoreType.DMA((20,)),
        ],
        compiler_params=params(46),
        cost_estimate=cost(13_400_000_000, 23_000_000, 1_000_000),
    )(place, x, attended, upstream, gains, *shares)


def attend_back_kernel(
    q,
    k,
    v,
    offsets,
    level,
    back_attended,
    q_proj,
    k_proj,
    head_gains,
    cosine,
    sine,
    place,
    kv0,
    kv1,
    kv2,
    kv3,
    back_q,
    back_kv,
    gain_grads,
    back_halo,
    sum_k,
    sum_v,
    wkv,
    semaphores,
):
    t = pl.program_id(0)

    @pl.when(t == 0)
    def _():
        for copy in assemble((kv0, kv1, kv2, kv3), wkv, place[0], semaphores, 0):
            copy.wait()
        sum_k[...] = jnp.zeros_like(sum_k)
        sum_v[...] = jnp.zeros_like(sum_v)
        gain_grads[...] = jnp.zeros_like(gain_grads)

    near = pl.ds(pl.multiple_of(t * 256, 256), 768)
    mine = pl.ds(pl.multiple_of(t * 256 + 512, 256), 256)
    keys, values = k[near, :], v[near, :]
    visible = visible_keys(offsets[...])
    c, s = cosine[mine, :], sine[mine, :]
    for h in range(4):
        cols = slice(256 * h, 256 * h + 256)
        qh, bah = q[:, cols], back_attended[:, cols]
        scores = jnp.where(visible, dot(qh, keys, rows_both) * 0.0625, masked_value)
        probs = jnp.exp(scores - level[h])
        bp = dot(bah, values, rows_both)
        inner = jnp.sum(probs * bp, axis=-1, keepdims=True)
        bs = (probs * (bp - inner)).astype(bf16)
        sum_k[near, :] += dot(bs, qh, cols_both)
        sum_v[near, :] += dot(probs.astype(bf16), bah, cols_both)
        e = turn_back(dot(bs, keys) * 0.0625, c, s)
        qp = q_proj[:, cols]
        r = inverse_rms(qp)
        gain_grads[0:1] += jnp.sum(qp * r * e, axis=0, keepdims=True)
        back_q[:, cols] = norm_back(qp, r, head_gains[4:5], e).astype(bf16)

    @pl.when(t == 1)
    def _():
        e = turn_back(sum_k[...] * 0.0625, cosine[...], sine[...])
        kp = k_proj[...]
        r = inverse_rms(kp)
        gain_grads[1:2] = jnp.sum(kp * r * e, axis=0, keepdims=True)
        back_kv[:, :256] = norm_back(kp, r, head_gains[5:6], e).astype(bf16)
        back_kv[:, 256:] = sum_v[...].astype(bf16)
        back_halo[...] = dot(back_kv[:512, :], wkv[...], rows_both).astype(bf16)


def attend_back(
    q, k, v, offsets, level, back_attended, q_proj, k_proj, head_gains, cosine, sine, place, shares
):
    row = lambda i: (i, 0)
    fixed = lambda i: (0, 0)
    return pl.pallas_call(
        attend_back_kernel,
        name="attend_back",
        grid=(2,),
        in_specs=[
            pl.BlockSpec((256, 1024), row),
            pl.BlockSpec((1024, 256), fixed),
            pl.BlockSpec((1024, 256), fixed),
            pl.BlockSpec((256, 1), row),
            pl.BlockSpec((4, 256, 1), lambda i: (0, i, 0)),
            pl.BlockSpec((256, 1024), row),
            pl.BlockSpec((256, 1024), row),
            pl.BlockSpec((1024, 256), fixed),
            pl.BlockSpec((8, 256), fixed),
            pl.BlockSpec((1024, 128), fixed),
            pl.BlockSpec((1024, 128), fixed),
            pl.BlockSpec(memory_space=pltpu.SMEM),
        ]
        + [pl.BlockSpec(memory_space=pltpu.HBM)] * 4,
        out_specs=[
            pl.BlockSpec((256, 1024), row),
            pl.BlockSpec((1024, 512), fixed),
            pl.BlockSpec((8, 256), fixed),
            pl.BlockSpec((512, 640), fixed),
        ],
        out_shape=[
            spec(512, 1024, bf16),
            spec(1024, 512, bf16),
            spec(8, 256, f32),
            spec(512, 640, bf16),
        ],
        scratch_shapes=[
            pltpu.VMEM((1024, 256), f32),
            pltpu.VMEM((1024, 256), f32),
            pltpu.VMEM((640, 512), bf16),
            pltpu.SemaphoreType.DMA((4,)),
        ],
        compiler_params=params(30),
        cost_estimate=cost(4_300_000_000, 10_000_000, 2_000_000),
    )(
        q, k, v, offsets, level, back_attended, q_proj, k_proj, head_gains, cosine, sine, place, *shares
    )


def weights_kernel(
    place,
    normed,
    back_q,
    back_kv,
    attended,
    back_attn,
    halo,
    own,
    gain_mid,
    gain_head,
    q0,
    q1,
    q2,
    q3,
    kv0,
    kv1,
    kv2,
    kv3,
    back_own,
    kept,
    sent,
    wq,
    wkv,
    grads,
    semaphores,
):
    copies = assemble((kv0, kv1, kv2, kv3), wkv, place[0], semaphores, 0)
    copies += assemble((q0, q1, q2, q3), wq, place[0], semaphores, 4)
    turned = normed[...].astype(f32).T.astype(bf16)
    bq, bkv = back_q[...], back_kv[...]
    part = dot(turned[:, 512:], bq).astype(bf16)
    for b in range(8):
        for f in range(4):
            grads[f, 160 * b : 160 * b + 160, :] = part[
                160 * f : 160 * f + 160, 128 * b : 128 * b + 128
            ]
    part = dot(turned, bkv).astype(bf16)
    for b in range(4):
        for f in range(4):
            grads[f, 1280 + 160 * b : 1440 + 160 * b, :] = part[
                160 * f : 160 * f + 160, 128 * b : 128 * b + 128
            ]
    turned = back_attn[...].astype(f32).T.astype(bf16)
    part = dot(turned, attended[...]).astype(bf16)
    for f in range(4):
        for b in range(2):
            grads[f, 1920 + 640 * b : 2560 + 640 * b, :] = part[
                :, 256 * f + 128 * b : 256 * f + 128 * b + 128
            ]
    for copy in copies:
        copy.wait()
    e = dot(bkv[:512], wkv[...], rows_both)
    x = halo[...].astype(f32)
    grad = jnp.sum(x * inverse_rms(x) * e, axis=0, keepdims=True)
    e = dot(bkv[512:], wkv[...], rows_both) + dot(bq, wq[...], rows_both)
    back_own[...] = e
    x = own[...].astype(f32)
    grad = grad + jnp.sum(x * inverse_rms(x) * e, axis=0, keepdims=True)
    each = jnp.concatenate([grad, gain_mid[0:3]], axis=0)
    heads = gain_head[0:2]
    for f in range(4):
        share = each[:, 160 * f : 160 * f + 160]
        rest = jnp.concatenate([share[:, 128:], jnp.zeros((4, 96), f32)], axis=1)
        ends = jnp.concatenate([heads[:, 64 * f : 64 * f + 64], jnp.zeros((2, 64), f32)], axis=1)
        tile = jnp.concatenate([share[:, :128], rest, ends, jnp.zeros((6, 128), f32)], axis=0)
        grads[f, 3200:3216, :] = tile.astype(bf16)
        grads[f, 3216:, :] = jnp.zeros((368, 128), bf16)
    for copy in split_out(grads, kept, sent, place[0], semaphores, 8):
        copy.wait()


def weights_part(
    place, normed, back_q, back_kv, attended, back_attn, halo, own, gain_mid, gain_head, shares
):
    return pl.pallas_call(
        weights_kernel,
        name="weights_part",
        in_specs=[pl.BlockSpec(memory_space=pltpu.SMEM)]
        + [whole()] * 9
        + [pl.BlockSpec(memory_space=pltpu.HBM)] * 8,
        out_specs=[whole()] + [pl.BlockSpec(memory_space=pltpu.HBM)] * 2,
        out_shape=[
            spec(512, 640, f32),
            spec(2, 3584, 128, bf16),
            spec(2, 3584, 128, bf16),
        ],
        scratch_shapes=[
            pltpu.VMEM((640, 1024), bf16),
            pltpu.VMEM((640, 512), bf16),
            pltpu.VMEM((4, 3584, 128), bf16),
            pltpu.SemaphoreType.DMA((12,)),
        ],
        compiler_params=params(40),
        cost_estimate=cost(3_400_000_000, 14_000_000),
    )(place, normed, back_q, back_kv, attended, back_attn, halo, own, gain_mid, gain_head, *shares)


def finish_kernel(own, back_own, returned, back_middle, gains, grad_in):
    x = own[...].astype(f32)
    e = back_own[...] + returned[...].astype(f32)
    grad_in[...] = (back_middle[...] + norm_back(x, inverse_rms(x), gains[0:1], e)).astype(bf16)


def finish(own, back_own, returned, back_middle, gains):
    row = lambda i: (i, 0)
    return pl.pallas_call(
        finish_kernel,
        name="finish",
        grid=(4,),
        in_specs=[pl.BlockSpec((128, 640), row)] * 4 + [pl.BlockSpec((8, 640), lambda i: (0, 0))],
        out_specs=pl.BlockSpec((128, 640), row),
        out_shape=spec(512, 640, bf16),
        compiler_params=params(10),
        cost_estimate=cost(4_000_000, 5_000_000),
    )(own, back_own, returned, back_middle, gains)


def rope_tables(offsets):
    powers = jnp.arange(128, dtype=f32) * (2.0 / 256)
    row = jnp.arange(512, dtype=jnp.int32)
    every = jnp.concatenate([offsets[0] - 512 + row, offsets])
    angles = every.astype(f32)[:, None] * (rope_base ** (-powers))[None, :]
    return jnp.cos(angles), jnp.sin(angles)


def unpack_kernel(spot, a0, a1, a2, a3, b0, b1, b2, b3, *rest):
    outs, gains, held, (ffn, attn, semaphores) = rest[:7], rest[7], rest[8:15], rest[15:]
    q, k, v, out, gate, up, down = held
    x, y = spot[0], spot[1]
    copies = []
    for half, pieces in enumerate(((a0, a1, a2, a3), (b0, b1, b2, b3))):
        for i in range(4):
            for j in range(4):
                first, second = (x, y) if half == 0 else (y, x)
                block = 16 * half + lax.rem(first - i + 4, 4) * 4 + lax.rem(second - j + 4, 4)
                n = (half * 4 + i) * 4 + j
                for m, (into, start, rows) in enumerate(((ffn, 0, 240), (attn, 240, 112))):
                    copies.append(
                        pltpu.make_async_copy(
                            pieces[i].at[j, pl.ds(start, rows), :],
                            into.at[pl.ds(pl.multiple_of(block * rows, 16), rows), :],
                            semaphores.at[2 * n + m],
                        )
                    )
    for copy in copies:
        copy.start()
    for copy in copies:
        copy.wait()
    outward = []

    def leave(n):
        copy = pltpu.make_async_copy(held[n], outs[n], semaphores.at[64 + n])
        copy.start()
        outward.append(copy)

    for n, into, flat, first, count in (
        (4, gate, ffn, 0, 16),
        (5, up, ffn, 2560, 16),
        (0, q, attn, 0, 8),
        (1, k, attn, 1280, 2),
        (2, v, attn, 1600, 2),
    ):
        for b in range(count):
            at = first + 160 * b
            into[:, 128 * b : 128 * b + 128] = flat[at : at + 160, :].astype(f32)
        leave(n)
    for n, into, flat, first, count in ((6, down, ffn, 5120, 4), (3, out, attn, 1920, 2)):
        for b in range(count):
            at = first + 640 * b
            into[128 * b : 128 * b + 128, :] = flat[at : at + 640, :].astype(f32).T
        leave(n)
    gains[...] = attn[3200:3216, :].astype(f32)
    for copy in outward:
        copy.wait()


def unpack(spot, pieces):
    shapes = [(160, 1024), (160, 256), (160, 256), (256, 640), (160, 2048), (160, 2048), (512, 640)]
    return pl.pallas_call(
        unpack_kernel,
        name="unpack",
        in_specs=[pl.BlockSpec(memory_space=pltpu.SMEM)] + [pl.BlockSpec(memory_space=pltpu.HBM)] * 8,
        out_specs=[pl.BlockSpec(memory_space=pltpu.HBM)] * 7 + [whole()],
        out_shape=[spec(*shape, f32) for shape in shapes] + [spec(16, 128, f32)],
        scratch_shapes=[pltpu.VMEM(shape, f32) for shape in shapes]
        + [
            pltpu.VMEM((7680, 128), bf16),
            pltpu.VMEM((3584, 128), bf16),
            pltpu.SemaphoreType.DMA((71,)),
        ],
        compiler_params=params(20),
        cost_estimate=cost(4_000_000, 11_000_000),
    )(spot, *pieces)


def sum_of(parts):
    whole = parts[0].astype(f32)
    for part in parts[1:]:
        whole = whole + part.astype(f32)
    return whole.astype(bf16)


def turn_around(position, d):
    return lax.rem(position + d, 4)


def first_kernel(spot, kept_ffn, got_ffn, kept_attn, got_attn, *outs):
    for half in range(2):
        for i, d in enumerate((0, 1, 3, 2)):
            at = turn_around(spot[half], d)
            out = outs[4 * half + i]
            for z in range(2):
                for j in range(4):
                    out[z, j, :240] = sum_of([r[z, half, at, j] for r in (kept_ffn, got_ffn)])
                    out[z, j, 240:] = sum_of([r[z, half, at, j] for r in (kept_attn, got_attn)])


def first_sums(spot, kept_ffn, got_ffn, kept_attn, got_attn):
    ins = [p.reshape(2, 2, 4, 4, p.shape[1] // 32, 128) for p in (kept_ffn, got_ffn, kept_attn, got_attn)]
    return pl.pallas_call(
        first_kernel,
        name="first_sums",
        in_specs=[pl.BlockSpec(memory_space=pltpu.SMEM)] + [whole()] * 4,
        out_specs=[whole()] * 8,
        out_shape=[spec(2, 4, 352, 128, bf16)] * 8,
        compiler_params=params(30),
        cost_estimate=cost(3_000_000, 17_000_000),
    )(spot, *ins)


def second_kernel(spot, *refs):
    ins, outs = refs[:8], refs[8:]
    for half in range(2):
        parts = ins[4 * half : 4 * half + 4]
        for i, d in enumerate((0, 1, 3, 2)):
            at = turn_around(spot[1 - half], d)
            for z in range(2):
                outs[4 * half + i][z] = sum_of([r[z, at] for r in parts])


def second_sums(spot, parts):
    return pl.pallas_call(
        second_kernel,
        name="second_sums",
        in_specs=[pl.BlockSpec(memory_space=pltpu.SMEM)] + [whole()] * 8,
        out_specs=[whole()] * 8,
        out_shape=[spec(2, 352, 128, bf16)] * 8,
        compiler_params=params(20),
        cost_estimate=cost(1_000_000, 7_200_000),
    )(spot, *parts)


def third_kernel(place, *refs):
    ins, (mine, other) = refs[:8], refs[8:]
    z = lax.div(place[0], 2)
    for half in range(2):
        parts = ins[4 * half : 4 * half + 4]
        mine[half] = sum_of([r[z] for r in parts])
        other[half] = sum_of([r[1 - z] for r in parts])


def third_sums(place, parts):
    return pl.pallas_call(
        third_kernel,
        name="third_sums",
        in_specs=[pl.BlockSpec(memory_space=pltpu.SMEM)] + [whole()] * 8,
        out_specs=[whole()] * 2,
        out_shape=[spec(2, 352, 128, bf16)] * 2,
        compiler_params=params(10),
        cost_estimate=cost(1_000_000, 1_800_000),
    )(place, *parts)


def fourth_kernel(p0, p1, p2, p3, a, b):
    for half, out in enumerate((a, b)):
        out[...] = sum_of([p0[half], p1[half], p2[half], p3[half]])


def fourth_sums(parts):
    return pl.pallas_call(
        fourth_kernel,
        name="fourth_sums",
        in_specs=[whole()] * 4,
        out_specs=[whole()] * 2,
        out_shape=[spec(352, 128, bf16)] * 2,
        compiler_params=params(10),
        cost_estimate=cost(1_000_000, 900_000),
    )(*parts)


def seq_index(z, x, y):
    return (z % 2 * 4 + x % 4) * 4 + y % 4


def along_xy(dx, dy):
    return [
        (seq_index(z, x, y), seq_index(z, x + dx, y + dy))
        for z in range(2)
        for x in range(4)
        for y in range(4)
    ]


def along_z(step):
    pairs = []
    for s in range(32):
        for f in range(4):
            z = s // 16 * 2 + f // 2
            t = step(z)
            pairs.append((s * 4 + f, (t // 2 * 16 + s % 16) * 4 + t % 2 * 2 + f % 2))
    return pairs


def swap_core(value):
    return lax.ppermute(value, "fsdp", [(0, 1), (1, 0), (2, 3), (3, 2)])


def swap_near(value):
    return lax.ppermute(value, "fsdp", [(0, 2), (1, 3), (2, 0), (3, 1)])


def swap_far(value):
    return lax.ppermute(value, ("seq", "fsdp"), along_z(lambda z: 3 - z))


def swap_hi(value):
    return lax.ppermute(value, "seq", [(s, (s + 16) % 32) for s in range(32)])


def move_x(value, d):
    return lax.ppermute(value, "seq", along_xy(d, 0))


def move_y(value, d):
    return lax.ppermute(value, "seq", along_xy(0, d))


def shifted(value, steps):
    first, last = (max(0, -steps), min(32, 32 - steps))
    return lax.ppermute(value, "seq", [(source, source + steps) for source in range(first, last)])


steps = (1, 3, 2)


def move_first(parts):
    return (
        [parts[0]]
        + [move_x(p, d) for p, d in zip(parts[1:4], steps)]
        + [parts[4]]
        + [move_y(p, d) for p, d in zip(parts[5:8], steps)]
    )


def move_second(parts):
    return (
        [parts[0]]
        + [move_y(p, d) for p, d in zip(parts[1:4], steps)]
        + [parts[4]]
        + [move_x(p, d) for p, d in zip(parts[5:8], steps)]
    )


def together(*groups):
    leaves, tree = jax.tree.flatten(groups)
    return jax.tree.unflatten(tree, lax.optimization_barrier(tuple(leaves)))


def body(
    hidden_in,
    cotangent,
    positions,
    query_weight,
    key_weight,
    value_weight,
    output_weight,
    gate_weight,
    up_weight,
    down_weight,
    norm_in,
    norm_attn,
    norm_ffn_in,
    norm_ffn_out,
    norm_query,
    norm_key,
):
    s = lax.axis_index("seq")
    f = lax.axis_index("fsdp")
    x, y, z_lo, core = s // 4 % 4, s % 4, f // 2, f % 2
    place = f.astype(jnp.int32).reshape(1)
    spot = jnp.stack([x, y]).astype(jnp.int32)
    own = hidden_in[0]
    upstream = cotangent[0]
    offsets = positions[0]

    q_partner = swap_near(query_weight)
    wg_partner, wu_partner = swap_near(gate_weight), swap_far(up_weight)
    kv = pack(
        [norm_in, norm_attn, norm_ffn_in, norm_ffn_out, norm_query, norm_key],
        key_weight,
        value_weight,
    )
    kv_partner = swap_far(kv)
    q_sibling = swap_core(query_weight)
    kv_sibling = swap_core(kv)
    halo = shifted(own, 1)
    q_diagonal = swap_core(q_partner)
    kv_diagonal = swap_core(kv_partner)
    (q_diagonal, kv_diagonal, halo), (wg_partner, wu_partner), (wo, wd) = together(
        (q_diagonal, kv_diagonal, halo), (wg_partner, wu_partner), (output_weight, down_weight)
    )
    wo_partner, wd_partner = swap_near(wo), swap_far(wd)
    q_shares = (query_weight, q_sibling, q_partner, q_diagonal)
    kv_shares = (kv, kv_sibling, kv_partner, kv_diagonal)
    tails = [share[160:168] for share in kv_shares]
    tails = [
        jnp.where(
            j // 2 == z_lo,
            jnp.where(j % 2 == core, tails[0], tails[1]),
            jnp.where(j % 2 == core, tails[2], tails[3]),
        )
        for j in range(4)
    ]
    gains = jnp.concatenate([tail[:, :160] for tail in tails], axis=1).astype(f32)
    head_gains = jnp.concatenate([tail[:, :64] for tail in tails], axis=1).astype(f32)

    cosine, sine = rope_tables(offsets)
    column = offsets[:, None]
    normed, q, k, v, q_proj, k_proj = project(
        place, halo, own, gains, head_gains, q_shares, kv_shares, cosine, sine
    )
    attended, level = attend(q, k, v, column)
    attended, (wo, wg, wu, wd) = together(attended, (wo, gate_weight, up_weight, wd))
    siblings = [swap_core(w) for w in (wo, wg, wu, wd)]
    attended, wo_partner, wg_partner = together(attended, wo_partner, wg_partner)
    attended, wu_partner, wd_partner = together(attended, wu_partner, wd_partner)
    wo_shares = [wo, siblings[0], wo_partner, swap_core(wo_partner)]
    wg_shares = [wg, siblings[1], wg_partner, swap_core(wg_partner)]
    wu_shares = [wu, siblings[2], wu_partner, swap_core(wu_partner)]
    wd_shares = [wd, siblings[3], wd_partner, swap_core(wd_partner)]
    layer_out, back_middle, back_attn, back_attended, gain_mid, kept, sent = middle_part(
        place, own, attended, upstream, gains, wo_shares + wg_shares + wu_shares + wd_shares
    )
    got = swap_core(sent)
    back_q, back_kv, gain_head, back_halo = attend_back(
        q,
        k,
        v,
        column,
        level,
        back_attended,
        q_proj,
        k_proj,
        head_gains,
        cosine,
        sine,
        place,
        kv_shares,
    )
    back_own, kept_attn, sent = weights_part(
        place,
        normed,
        back_q,
        back_kv,
        attended,
        back_attn,
        halo,
        own,
        gain_mid,
        gain_head,
        q_shares + kv_shares,
    )
    got_attn = swap_core(sent)
    first = move_first(first_sums(spot, kept, got, kept_attn, got_attn))
    mine, other = third_sums(place, move_second(second_sums(spot, first)))
    mine, other, back_halo = together(mine, other, back_halo)
    returned = shifted(back_halo, -1)
    a, b = fourth_sums([mine, swap_near(other), swap_far(other), swap_hi(mine)])
    a = jnp.stack([a] + [move_y(a, d) for d in (1, 2, 3)])
    b = jnp.stack([b] + [move_x(b, d) for d in (1, 2, 3)])
    a, b = together(a, b)
    pieces = [a] + [move_x(a, d) for d in (1, 2, 3)] + [b] + [move_y(b, d) for d in (1, 2, 3)]
    grad_q, grad_k, grad_v, grad_o, grad_g, grad_u, grad_d, tile = unpack(spot, pieces)
    grad_in = finish(own, back_own, returned, back_middle, gains)
    wide = jnp.concatenate([tile[0:4], tile[4:8, :32]], axis=1)
    return (
        layer_out[None],
        grad_in[None],
        grad_q,
        grad_k,
        grad_v,
        grad_o,
        grad_g,
        grad_u,
        grad_d,
        wide[0],
        wide[1],
        wide[2],
        wide[3],
        tile[8, :64],
        tile[9, :64],
    )


def solution(mesh):
    three = P("fsdp", "seq", None)
    two = P("fsdp", None)
    one = P("fsdp")
    return jax.shard_map(
        body,
        mesh=mesh,
        in_specs=(three, three, P("fsdp", "seq")) + (two,) * 7 + (one,) * 6,
        out_specs=(three, three) + (two,) * 7 + (one,) * 6,
        check_vma=False,
    )
```

```python
import jax
import jax.numpy as jnp
from jax import lax
from jax.experimental import pallas as pl
from jax.experimental.pallas import tpu as pltpu
from jax.sharding import PartitionSpec as P

WINDOW = 512
epsilon = 1e-06
rope_base = 10000.0
masked_value = -1e30
bf16 = jnp.bfloat16
f32 = jnp.float32

rows_out = ((1,), (0,))
rows_both = ((1,), (1,))
cols_both = ((0,), (0,))


def dot(a, b, dims=rows_out):
    return lax.dot_general(a, b, (dims, ((), ())), preferred_element_type=f32)


def spec(*shape):
    return jax.ShapeDtypeStruct(shape[:-1], shape[-1])


def whole():
    return pl.BlockSpec(memory_space=pltpu.VMEM)


def params(mib):
    return pltpu.CompilerParams(vmem_limit_bytes=mib * 1024 * 1024)


def cost(flops, moved, exps=0):
    return pl.CostEstimate(flops=flops, bytes_accessed=moved, transcendentals=exps)


def inverse_rms(v):
    return lax.rsqrt(jnp.mean(v * v, axis=-1, keepdims=True) + epsilon)


def norm_back(v, r, gain, e):
    scaled = gain * e
    return r * scaled - v * (r * r * r * jnp.mean(v * scaled, axis=-1, keepdims=True))


def turn(v, cosine, sine):
    a, b = v[:, :128], v[:, 128:]
    return jnp.concatenate([a * cosine - b * sine, b * cosine + a * sine], axis=1)


def turn_back(v, cosine, sine):
    a, b = v[:, :128], v[:, 128:]
    return jnp.concatenate([a * cosine + b * sine, b * cosine - a * sine], axis=1)


def assemble(pieces, into, place, semaphores, first, column=0):
    rows = into.shape[0] // 4
    copies = []
    for r in range(4):
        at = pl.ds(pl.multiple_of((place ^ r) * rows, rows), rows)
        copies.append(
            pltpu.make_async_copy(
                pieces[r].at[:, pl.ds(column, into.shape[1])],
                into.at[at, :],
                semaphores.at[first + r],
            )
        )
    for copy in copies:
        copy.start()
    return copies


def split_out(grads, kept, sent, place, semaphores, first):
    core = lax.rem(place, 2)
    copies = []
    for z in range(2):
        copies.append(
            pltpu.make_async_copy(
                grads.at[2 * z + 1 - core], sent.at[z], semaphores.at[first + 2 * z]
            )
        )
        copies.append(
            pltpu.make_async_copy(
                grads.at[2 * z + core], kept.at[z], semaphores.at[first + 2 * z + 1]
            )
        )
    for copy in copies:
        copy.start()
    return copies


def pack_kernel(g0, g1, g2, g3, g4, g5, out, *rest):
    held, semaphores = rest[:6], rest[6]
    copies = [
        pltpu.make_async_copy(source, into, semaphores.at[i])
        for i, (source, into) in enumerate(zip((g0, g1, g2, g3, g4, g5), held))
    ]
    for copy in copies:
        copy.start()
    out[...] = jnp.zeros_like(out)
    for copy in copies:
        copy.wait()
    for i, ref in enumerate(held):
        n = ref.shape[0]
        out[i : i + 1, :n] = ref[...].astype(f32).reshape(1, n)


def pack(rows):
    return pl.pallas_call(
        pack_kernel,
        name="pack",
        in_specs=[pl.BlockSpec(memory_space=pltpu.HBM)] * 6,
        out_specs=whole(),
        out_shape=spec(8, 256, f32),
        scratch_shapes=[pltpu.VMEM(row.shape, bf16) for row in rows]
        + [pltpu.SemaphoreType.DMA((6,))],
        compiler_params=params(4),
        cost_estimate=cost(100_000, 20_000),
    )(*rows)


def project_kernel(
    place,
    halo,
    own,
    gains,
    head_gains,
    q0,
    q1,
    q2,
    q3,
    kv0,
    kv1,
    kv2,
    kv3,
    cosine,
    sine,
    normed,
    q,
    k,
    v,
    q_proj,
    k_proj,
    wq,
    wkv,
    semaphores,
):
    i = pl.program_id(0)

    @pl.when(i == 0)
    def _():
        copies = assemble((kv0, kv1, kv2, kv3), wkv, place[0], semaphores, 0)
        copies += assemble((q0, q1, q2, q3), wq, place[0], semaphores, 4)
        for copy in copies:
            copy.wait()

    x = jnp.where(i < 2, halo[...], own[...]).astype(f32)
    n = (x * inverse_rms(x) * gains[0:1]).astype(bf16)
    normed[...] = n
    c, s = cosine[...], sine[...]
    kv = dot(n, wkv[...])
    kp = kv[:, :256]
    k_proj[...] = kp
    v[...] = kv[:, 256:].astype(bf16)
    k[...] = turn(kp * inverse_rms(kp) * head_gains[5:6], c, s).astype(bf16)

    @pl.when(i >= 2)
    def _():
        for h in range(4):
            cols = slice(256 * h, 256 * h + 256)
            qp = dot(n, wq[:, cols])
            q_proj[:, cols] = qp
            q[:, cols] = turn(qp * inverse_rms(qp) * head_gains[4:5], c, s).astype(bf16)


def project(place, halo, own, gains, head_gains, q_shares, kv_shares, cosine, sine):
    late = lambda i: (jnp.maximum(i - 2, 0), 0)
    row = lambda i: (i, 0)
    fixed = lambda i: (0, 0)
    return pl.pallas_call(
        project_kernel,
        name="project",
        grid=(4,),
        in_specs=[
            pl.BlockSpec(memory_space=pltpu.SMEM),
            pl.BlockSpec((256, 640), lambda i: (jnp.minimum(i, 1), 0)),
            pl.BlockSpec((256, 640), late),
            pl.BlockSpec((8, 640), fixed),
            pl.BlockSpec((8, 256), fixed),
        ]
        + [pl.BlockSpec(memory_space=pltpu.HBM)] * 8
        + [pl.BlockSpec((256, 128), row)] * 2,
        out_specs=[
            pl.BlockSpec((256, 640), row),
            pl.BlockSpec((256, 1024), late),
            pl.BlockSpec((256, 256), row),
            pl.BlockSpec((256, 256), row),
            pl.BlockSpec((256, 1024), late),
            pl.BlockSpec((256, 256), row),
        ],
        out_shape=[
            spec(1024, 640, bf16),
            spec(512, 1024, bf16),
            spec(1024, 256, bf16),
            spec(1024, 256, bf16),
            spec(512, 1024, f32),
            spec(1024, 256, f32),
        ],
        scratch_shapes=[
            pltpu.VMEM((640, 1024), bf16),
            pltpu.VMEM((640, 512), bf16),
            pltpu.SemaphoreType.DMA((8,)),
        ],
        compiler_params=params(20),
        cost_estimate=cost(1_350_000_000, 9_000_000),
    )(place, halo, own, gains, head_gains, *q_shares, *kv_shares, cosine, sine)


def visible_keys(offsets):
    distance = (
        lax.broadcasted_iota(jnp.int32, (256, 768), 0)
        + 512
        - lax.broadcasted_iota(jnp.int32, (256, 768), 1)
    )
    return (distance >= 0) & (distance < WINDOW) & (distance <= offsets)


def attend_kernel(q, k, v, offsets, attended, level):
    t = pl.program_id(0)
    near = pl.ds(pl.multiple_of(t * 256, 256), 768)
    keys, values = k[near, :], v[near, :]
    visible = visible_keys(offsets[...])
    for h in range(4):
        cols = slice(256 * h, 256 * h + 256)
        scores = jnp.where(visible, dot(q[:, cols], keys, rows_both) * 0.0625, masked_value)
        top = jnp.max(scores, axis=-1, keepdims=True)
        e = jnp.exp(scores - top)
        total = jnp.sum(e, axis=-1, keepdims=True)
        level[h] = top + jnp.log(total)
        probs = (e * (1.0 / total)).astype(bf16)
        attended[:, cols] = dot(probs, values).astype(bf16)


def attend(q, k, v, offsets):
    row = lambda i: (i, 0)
    fixed = lambda i: (0, 0)
    return pl.pallas_call(
        attend_kernel,
        name="attend",
        grid=(2,),
        in_specs=[
            pl.BlockSpec((256, 1024), row),
            pl.BlockSpec((1024, 256), fixed),
            pl.BlockSpec((1024, 256), fixed),
            pl.BlockSpec((256, 1), row),
        ],
        out_specs=[
            pl.BlockSpec((256, 1024), row),
            pl.BlockSpec((4, 256, 1), lambda i: (0, i, 0)),
        ],
        out_shape=[spec(512, 1024, bf16), spec(4, 512, 1, f32)],
        compiler_params=params(20),
        cost_estimate=cost(1_700_000_000, 4_000_000, 2_000_000),
    )(q, k, v, offsets)


def middle_kernel(
    place,
    x_ref,
    attended,
    upstream,
    gains,
    o0,
    o1,
    o2,
    o3,
    g0,
    g1,
    g2,
    g3,
    u0,
    u1,
    u2,
    u3,
    d0,
    d1,
    d2,
    d3,
    layer_out,
    back_middle,
    back_attn,
    back_attended,
    gain_grads,
    kept,
    sent,
    ffn_in,
    kept_a,
    kept_b,
    hidden,
    back_out,
    in_turned,
    out_turned,
    back_gate,
    back_up,
    wo,
    wg,
    wu,
    wd,
    grads,
    semaphores,
):
    output_copies = assemble((o0, o1, o2, o3), wo, place[0], semaphores, 0)
    gate_copies = assemble((g0, g1, g2, g3), wg, place[0], semaphores, 4, 1024)
    up_copies = assemble((u0, u1, u2, u3), wu, place[0], semaphores, 8, 512)
    down_copies = assemble((d0, d1, d2, d3), wd, place[0], semaphores, 12)
    for copy in output_copies:
        copy.wait()
    g_attn, g_in, g_out = gains[1:2], gains[2:3], gains[3:4]
    ao = dot(attended[...], wo[...])
    r1 = inverse_rms(ao)
    mid = x_ref[...].astype(f32) + ao * r1 * g_attn
    r2 = inverse_rms(mid)
    ffn_in[...] = (mid * r2 * g_in).astype(bf16)
    for copy in gate_copies + up_copies:
        copy.wait()

    for j in range(8):
        cols = slice(256 * j, 256 * j + 256)
        u = dot(ffn_in[...], wg[:, cols])
        up = dot(ffn_in[...], wu[:, cols])
        root = 0.7978845608028654
        square = u * u
        t = jnp.tanh(u * (root + (root * 0.044715) * square))
        half = 0.5 + 0.5 * t
        act = u * half
        slope = half + act * (1.0 - t) * (root + (3 * 0.044715 * root) * square)
        hidden[:, cols] = (act * up).astype(bf16)
        kept_a[:, cols] = act
        kept_b[:, cols] = up * slope

    for copy in down_copies:
        copy.wait()
    fo = dot(hidden[...], wd[...])
    r3 = inverse_rms(fo)
    layer_out[...] = (mid + fo * r3 * g_out).astype(bf16)
    g = upstream[...].astype(f32)
    gain_grads[2:3] = jnp.sum(fo * r3 * g, axis=0, keepdims=True)
    bfo = norm_back(fo, r3, g_out, g)
    back_out[...] = bfo.astype(bf16)
    out_turned[...] = back_out[...].T
    in_turned[...] = ffn_in[...].T

    for j in range(8):
        cols = slice(256 * j, 256 * j + 256)
        bh = dot(back_out[...], wd[cols, :], rows_both)
        bu = (bh * kept_a[:, cols]).astype(bf16)
        bg = (bh * kept_b[:, cols]).astype(bf16)
        back_gate[:, cols] = bg
        back_up[:, cols] = bu

    for base, right in ((0, back_gate), (2560, back_up)):
        for j in range(2048 // 512):
            part = dot(in_turned[...], right[:, 512 * j : 512 * j + 512]).astype(bf16)
            for b in range(512 // 128):
                at = base + (512 // 128 * j + b) * 160
                for f in range(4):
                    grads[f, at : at + 160, :] = part[
                        160 * f : 160 * f + 160, 128 * b : 128 * b + 128
                    ]
    for f in range(4):
        part = dot(out_turned[...], hidden[:, 512 * f : 512 * f + 512]).astype(bf16)
        for b in range(4):
            at = 5120 + 640 * b
            grads[f, at : at + 640, :] = part[:, 128 * b : 128 * b + 128]

    outward = split_out(grads, kept, sent, place[0], semaphores, 16)
    e = dot(back_gate[...], wg[...], rows_both) + dot(back_up[...], wu[...], rows_both)
    gain_grads[1:2] = jnp.sum(mid * r2 * e, axis=0, keepdims=True)
    bm = g + norm_back(mid, r2, g_in, e)
    back_middle[...] = bm
    gain_grads[0:1] = jnp.sum(ao * r1 * bm, axis=0, keepdims=True)
    bao = norm_back(ao, r1, g_attn, bm).astype(bf16)
    back_attn[...] = bao
    back_attended[...] = dot(bao, wo[...], rows_both).astype(bf16)
    for copy in outward:
        copy.wait()


def middle_part(place, x, attended, upstream, gains, shares):
    return pl.pallas_call(
        middle_kernel,
        name="middle_part",
        in_specs=[pl.BlockSpec(memory_space=pltpu.SMEM)]
        + [whole()] * 4
        + [pl.BlockSpec(memory_space=pltpu.HBM)] * 16,
        out_specs=[whole()] * 5 + [pl.BlockSpec(memory_space=pltpu.HBM)] * 2,
        out_shape=[
            spec(512, 640, bf16),
            spec(512, 640, f32),
            spec(512, 640, bf16),
            spec(512, 1024, bf16),
            spec(8, 640, f32),
            spec(2, 7680, 128, bf16),
            spec(2, 7680, 128, bf16),
        ],
        scratch_shapes=[
            pltpu.VMEM((512, 640), bf16),
            pltpu.VMEM((512, 2048), f32),
            pltpu.VMEM((512, 2048), f32),
            pltpu.VMEM((512, 2048), bf16),
            pltpu.VMEM((512, 640), bf16),
            pltpu.VMEM((640, 512), bf16),
            pltpu.VMEM((640, 512), bf16),
            pltpu.VMEM((512, 2048), bf16),
            pltpu.VMEM((512, 2048), bf16),
            pltpu.VMEM((1024, 640), bf16),
            pltpu.VMEM((640, 2048), bf16),
            pltpu.VMEM((640, 2048), bf16),
            pltpu.VMEM((2048, 640), bf16),
            pltpu.VMEM((4, 7680, 128), bf16),
            pltpu.SemaphoreType.DMA((20,)),
        ],
        compiler_params=params(46),
        cost_estimate=cost(13_400_000_000, 23_000_000, 1_000_000),
    )(place, x, attended, upstream, gains, *shares)


def attend_back_kernel(
    q,
    k,
    v,
    offsets,
    level,
    back_attended,
    q_proj,
    k_proj,
    head_gains,
    cosine,
    sine,
    place,
    kv0,
    kv1,
    kv2,
    kv3,
    back_q,
    back_kv,
    gain_grads,
    back_halo,
    sum_k,
    sum_v,
    wkv,
    semaphores,
):
    t = pl.program_id(0)

    @pl.when(t == 0)
    def _():
        for copy in assemble((kv0, kv1, kv2, kv3), wkv, place[0], semaphores, 0):
            copy.wait()
        sum_k[...] = jnp.zeros_like(sum_k)
        sum_v[...] = jnp.zeros_like(sum_v)
        gain_grads[...] = jnp.zeros_like(gain_grads)

    near = pl.ds(pl.multiple_of(t * 256, 256), 768)
    mine = pl.ds(pl.multiple_of(t * 256 + 512, 256), 256)
    keys, values = k[near, :], v[near, :]
    visible = visible_keys(offsets[...])
    c, s = cosine[mine, :], sine[mine, :]
    for h in range(4):
        cols = slice(256 * h, 256 * h + 256)
        qh, bah = q[:, cols], back_attended[:, cols]
        scores = jnp.where(visible, dot(qh, keys, rows_both) * 0.0625, masked_value)
        probs = jnp.exp(scores - level[h])
        bp = dot(bah, values, rows_both)
        inner = jnp.sum(probs * bp, axis=-1, keepdims=True)
        bs = (probs * (bp - inner)).astype(bf16)
        sum_k[near, :] += dot(bs, qh, cols_both)
        sum_v[near, :] += dot(probs.astype(bf16), bah, cols_both)
        e = turn_back(dot(bs, keys) * 0.0625, c, s)
        qp = q_proj[:, cols]
        r = inverse_rms(qp)
        gain_grads[0:1] += jnp.sum(qp * r * e, axis=0, keepdims=True)
        back_q[:, cols] = norm_back(qp, r, head_gains[4:5], e).astype(bf16)

    @pl.when(t == 1)
    def _():
        e = turn_back(sum_k[...] * 0.0625, cosine[...], sine[...])
        kp = k_proj[...]
        r = inverse_rms(kp)
        gain_grads[1:2] = jnp.sum(kp * r * e, axis=0, keepdims=True)
        back_kv[:, :256] = norm_back(kp, r, head_gains[5:6], e).astype(bf16)
        back_kv[:, 256:] = sum_v[...].astype(bf16)
        back_halo[...] = dot(back_kv[:512, :], wkv[...], rows_both).astype(bf16)


def attend_back(
    q, k, v, offsets, level, back_attended, q_proj, k_proj, head_gains, cosine, sine, place, shares
):
    row = lambda i: (i, 0)
    fixed = lambda i: (0, 0)
    return pl.pallas_call(
        attend_back_kernel,
        name="attend_back",
        grid=(2,),
        in_specs=[
            pl.BlockSpec((256, 1024), row),
            pl.BlockSpec((1024, 256), fixed),
            pl.BlockSpec((1024, 256), fixed),
            pl.BlockSpec((256, 1), row),
            pl.BlockSpec((4, 256, 1), lambda i: (0, i, 0)),
            pl.BlockSpec((256, 1024), row),
            pl.BlockSpec((256, 1024), row),
            pl.BlockSpec((1024, 256), fixed),
            pl.BlockSpec((8, 256), fixed),
            pl.BlockSpec((1024, 128), fixed),
            pl.BlockSpec((1024, 128), fixed),
            pl.BlockSpec(memory_space=pltpu.SMEM),
        ]
        + [pl.BlockSpec(memory_space=pltpu.HBM)] * 4,
        out_specs=[
            pl.BlockSpec((256, 1024), row),
            pl.BlockSpec((1024, 512), fixed),
            pl.BlockSpec((8, 256), fixed),
            pl.BlockSpec((512, 640), fixed),
        ],
        out_shape=[
            spec(512, 1024, bf16),
            spec(1024, 512, bf16),
            spec(8, 256, f32),
            spec(512, 640, bf16),
        ],
        scratch_shapes=[
            pltpu.VMEM((1024, 256), f32),
            pltpu.VMEM((1024, 256), f32),
            pltpu.VMEM((640, 512), bf16),
            pltpu.SemaphoreType.DMA((4,)),
        ],
        compiler_params=params(30),
        cost_estimate=cost(4_300_000_000, 10_000_000, 2_000_000),
    )(
        q, k, v, offsets, level, back_attended, q_proj, k_proj, head_gains, cosine, sine, place, *shares
    )


def weights_kernel(
    place,
    normed,
    back_q,
    back_kv,
    attended,
    back_attn,
    halo,
    own,
    gain_mid,
    gain_head,
    q0,
    q1,
    q2,
    q3,
    kv0,
    kv1,
    kv2,
    kv3,
    back_own,
    kept,
    sent,
    wq,
    wkv,
    grads,
    semaphores,
):
    copies = assemble((kv0, kv1, kv2, kv3), wkv, place[0], semaphores, 0)
    copies += assemble((q0, q1, q2, q3), wq, place[0], semaphores, 4)
    turned = normed[...].astype(f32).T.astype(bf16)
    bq, bkv = back_q[...], back_kv[...]
    part = dot(turned[:, 512:], bq).astype(bf16)
    for b in range(8):
        for f in range(4):
            grads[f, 160 * b : 160 * b + 160, :] = part[
                160 * f : 160 * f + 160, 128 * b : 128 * b + 128
            ]
    part = dot(turned, bkv).astype(bf16)
    for b in range(4):
        for f in range(4):
            grads[f, 1280 + 160 * b : 1440 + 160 * b, :] = part[
                160 * f : 160 * f + 160, 128 * b : 128 * b + 128
            ]
    turned = back_attn[...].astype(f32).T.astype(bf16)
    part = dot(turned, attended[...]).astype(bf16)
    for f in range(4):
        for b in range(2):
            grads[f, 1920 + 640 * b : 2560 + 640 * b, :] = part[
                :, 256 * f + 128 * b : 256 * f + 128 * b + 128
            ]
    for copy in copies:
        copy.wait()
    e = dot(bkv[:512], wkv[...], rows_both)
    x = halo[...].astype(f32)
    grad = jnp.sum(x * inverse_rms(x) * e, axis=0, keepdims=True)
    e = dot(bkv[512:], wkv[...], rows_both) + dot(bq, wq[...], rows_both)
    back_own[...] = e
    x = own[...].astype(f32)
    grad = grad + jnp.sum(x * inverse_rms(x) * e, axis=0, keepdims=True)
    each = jnp.concatenate([grad, gain_mid[0:3]], axis=0)
    heads = gain_head[0:2]
    for f in range(4):
        share = each[:, 160 * f : 160 * f + 160]
        rest = jnp.concatenate([share[:, 128:], jnp.zeros((4, 96), f32)], axis=1)
        ends = jnp.concatenate([heads[:, 64 * f : 64 * f + 64], jnp.zeros((2, 64), f32)], axis=1)
        tile = jnp.concatenate([share[:, :128], rest, ends, jnp.zeros((6, 128), f32)], axis=0)
        grads[f, 3200:3216, :] = tile.astype(bf16)
        grads[f, 3216:, :] = jnp.zeros((368, 128), bf16)
    for copy in split_out(grads, kept, sent, place[0], semaphores, 8):
        copy.wait()


def weights_part(
    place, normed, back_q, back_kv, attended, back_attn, halo, own, gain_mid, gain_head, shares
):
    return pl.pallas_call(
        weights_kernel,
        name="weights_part",
        in_specs=[pl.BlockSpec(memory_space=pltpu.SMEM)]
        + [whole()] * 9
        + [pl.BlockSpec(memory_space=pltpu.HBM)] * 8,
        out_specs=[whole()] + [pl.BlockSpec(memory_space=pltpu.HBM)] * 2,
        out_shape=[
            spec(512, 640, f32),
            spec(2, 3584, 128, bf16),
            spec(2, 3584, 128, bf16),
        ],
        scratch_shapes=[
            pltpu.VMEM((640, 1024), bf16),
            pltpu.VMEM((640, 512), bf16),
            pltpu.VMEM((4, 3584, 128), bf16),
            pltpu.SemaphoreType.DMA((12,)),
        ],
        compiler_params=params(40),
        cost_estimate=cost(3_400_000_000, 14_000_000),
    )(place, normed, back_q, back_kv, attended, back_attn, halo, own, gain_mid, gain_head, *shares)


def finish_kernel(own, back_own, returned, back_middle, gains, grad_in):
    x = own[...].astype(f32)
    e = back_own[...] + returned[...].astype(f32)
    grad_in[...] = (back_middle[...] + norm_back(x, inverse_rms(x), gains[0:1], e)).astype(bf16)


def finish(own, back_own, returned, back_middle, gains):
    row = lambda i: (i, 0)
    return pl.pallas_call(
        finish_kernel,
        name="finish",
        grid=(4,),
        in_specs=[pl.BlockSpec((128, 640), row)] * 4 + [pl.BlockSpec((8, 640), lambda i: (0, 0))],
        out_specs=pl.BlockSpec((128, 640), row),
        out_shape=spec(512, 640, bf16),
        compiler_params=params(10),
        cost_estimate=cost(4_000_000, 5_000_000),
    )(own, back_own, returned, back_middle, gains)


def rope_tables(offsets):
    powers = jnp.arange(128, dtype=f32) * (2.0 / 256)
    row = jnp.arange(512, dtype=jnp.int32)
    every = jnp.concatenate([offsets[0] - 512 + row, offsets])
    angles = every.astype(f32)[:, None] * (rope_base ** (-powers))[None, :]
    return jnp.cos(angles), jnp.sin(angles)


def unpack_kernel(spot, a0, a1, a2, a3, b0, b1, b2, b3, *rest):
    outs, gains, held, (ffn, attn, semaphores) = rest[:7], rest[7], rest[8:15], rest[15:]
    q, k, v, out, gate, up, down = held
    x, y = spot[0], spot[1]
    copies = []
    for half, pieces in enumerate(((a0, a1, a2, a3), (b0, b1, b2, b3))):
        for i in range(4):
            for j in range(4):
                first, second = (x, y) if half == 0 else (y, x)
                block = 16 * half + lax.rem(first - i + 4, 4) * 4 + lax.rem(second - j + 4, 4)
                n = (half * 4 + i) * 4 + j
                for m, (into, start, rows) in enumerate(((ffn, 0, 240), (attn, 240, 112))):
                    copies.append(
                        pltpu.make_async_copy(
                            pieces[i].at[j, pl.ds(start, rows), :],
                            into.at[pl.ds(pl.multiple_of(block * rows, 16), rows), :],
                            semaphores.at[2 * n + m],
                        )
                    )
    for copy in copies:
        copy.start()
    for copy in copies:
        copy.wait()
    outward = []

    def leave(n):
        copy = pltpu.make_async_copy(held[n], outs[n], semaphores.at[64 + n])
        copy.start()
        outward.append(copy)

    for n, into, flat, first, count in (
        (4, gate, ffn, 0, 16),
        (5, up, ffn, 2560, 16),
        (0, q, attn, 0, 8),
        (1, k, attn, 1280, 2),
        (2, v, attn, 1600, 2),
    ):
        for b in range(count):
            at = first + 160 * b
            into[:, 128 * b : 128 * b + 128] = flat[at : at + 160, :].astype(f32)
        leave(n)
    for n, into, flat, first, count in ((6, down, ffn, 5120, 4), (3, out, attn, 1920, 2)):
        for b in range(count):
            at = first + 640 * b
            into[128 * b : 128 * b + 128, :] = flat[at : at + 640, :].astype(f32).T
        leave(n)
    gains[...] = attn[3200:3216, :].astype(f32)
    for copy in outward:
        copy.wait()


def unpack(spot, pieces):
    shapes = [(160, 1024), (160, 256), (160, 256), (256, 640), (160, 2048), (160, 2048), (512, 640)]
    return pl.pallas_call(
        unpack_kernel,
        name="unpack",
        in_specs=[pl.BlockSpec(memory_space=pltpu.SMEM)] + [pl.BlockSpec(memory_space=pltpu.HBM)] * 8,
        out_specs=[pl.BlockSpec(memory_space=pltpu.HBM)] * 7 + [whole()],
        out_shape=[spec(*shape, f32) for shape in shapes] + [spec(16, 128, f32)],
        scratch_shapes=[pltpu.VMEM(shape, f32) for shape in shapes]
        + [
            pltpu.VMEM((7680, 128), bf16),
            pltpu.VMEM((3584, 128), bf16),
            pltpu.SemaphoreType.DMA((71,)),
        ],
        compiler_params=params(20),
        cost_estimate=cost(4_000_000, 11_000_000),
    )(spot, *pieces)


def sum_of(parts):
    whole = parts[0].astype(f32)
    for part in parts[1:]:
        whole = whole + part.astype(f32)
    return whole.astype(bf16)


def turn_around(position, d):
    return lax.rem(position + d, 4)


def first_kernel(spot, kept_ffn, got_ffn, kept_attn, got_attn, *outs):
    for half in range(2):
        for i, d in enumerate((0, 1, 3, 2)):
            at = turn_around(spot[half], d)
            out = outs[4 * half + i]
            for z in range(2):
                for j in range(4):
                    out[z, j, :240] = sum_of([r[z, half, at, j] for r in (kept_ffn, got_ffn)])
                    out[z, j, 240:] = sum_of([r[z, half, at, j] for r in (kept_attn, got_attn)])


def first_sums(spot, kept_ffn, got_ffn, kept_attn, got_attn):
    ins = [p.reshape(2, 2, 4, 4, p.shape[1] // 32, 128) for p in (kept_ffn, got_ffn, kept_attn, got_attn)]
    return pl.pallas_call(
        first_kernel,
        name="first_sums",
        in_specs=[pl.BlockSpec(memory_space=pltpu.SMEM)] + [whole()] * 4,
        out_specs=[whole()] * 8,
        out_shape=[spec(2, 4, 352, 128, bf16)] * 8,
        compiler_params=params(30),
        cost_estimate=cost(3_000_000, 17_000_000),
    )(spot, *ins)


def second_kernel(spot, *refs):
    ins, outs = refs[:8], refs[8:]
    for half in range(2):
        parts = ins[4 * half : 4 * half + 4]
        for i, d in enumerate((0, 1, 3, 2)):
            at = turn_around(spot[1 - half], d)
            for z in range(2):
                outs[4 * half + i][z] = sum_of([r[z, at] for r in parts])


def second_sums(spot, parts):
    return pl.pallas_call(
        second_kernel,
        name="second_sums",
        in_specs=[pl.BlockSpec(memory_space=pltpu.SMEM)] + [whole()] * 8,
        out_specs=[whole()] * 8,
        out_shape=[spec(2, 352, 128, bf16)] * 8,
        compiler_params=params(20),
        cost_estimate=cost(1_000_000, 7_200_000),
    )(spot, *parts)


def third_kernel(place, *refs):
    ins, (mine, other) = refs[:8], refs[8:]
    z = lax.div(place[0], 2)
    for half in range(2):
        parts = ins[4 * half : 4 * half + 4]
        mine[half] = sum_of([r[z] for r in parts])
        other[half] = sum_of([r[1 - z] for r in parts])


def third_sums(place, parts):
    return pl.pallas_call(
        third_kernel,
        name="third_sums",
        in_specs=[pl.BlockSpec(memory_space=pltpu.SMEM)] + [whole()] * 8,
        out_specs=[whole()] * 2,
        out_shape=[spec(2, 352, 128, bf16)] * 2,
        compiler_params=params(10),
        cost_estimate=cost(1_000_000, 1_800_000),
    )(place, *parts)


def fourth_kernel(p0, p1, p2, p3, a, b):
    for half, out in enumerate((a, b)):
        out[...] = sum_of([p0[half], p1[half], p2[half], p3[half]])


def fourth_sums(parts):
    return pl.pallas_call(
        fourth_kernel,
        name="fourth_sums",
        in_specs=[whole()] * 4,
        out_specs=[whole()] * 2,
        out_shape=[spec(352, 128, bf16)] * 2,
        compiler_params=params(10),
        cost_estimate=cost(1_000_000, 900_000),
    )(*parts)


def seq_index(z, x, y):
    return (z % 2 * 4 + x % 4) * 4 + y % 4


def along_xy(dx, dy):
    return [
        (seq_index(z, x, y), seq_index(z, x + dx, y + dy))
        for z in range(2)
        for x in range(4)
        for y in range(4)
    ]


def along_z(step):
    pairs = []
    for s in range(32):
        for f in range(4):
            z = s // 16 * 2 + f // 2
            t = step(z)
            pairs.append((s * 4 + f, (t // 2 * 16 + s % 16) * 4 + t % 2 * 2 + f % 2))
    return pairs


def swap_core(value):
    return lax.ppermute(value, "fsdp", [(0, 1), (1, 0), (2, 3), (3, 2)])


def swap_near(value):
    return lax.ppermute(value, "fsdp", [(0, 2), (1, 3), (2, 0), (3, 1)])


def swap_far(value):
    return lax.ppermute(value, ("seq", "fsdp"), along_z(lambda z: 3 - z))


def swap_hi(value):
    return lax.ppermute(value, "seq", [(s, (s + 16) % 32) for s in range(32)])


def move_x(value, d):
    return lax.ppermute(value, "seq", along_xy(d, 0))


def move_y(value, d):
    return lax.ppermute(value, "seq", along_xy(0, d))


def shifted(value, steps):
    first, last = (max(0, -steps), min(32, 32 - steps))
    return lax.ppermute(value, "seq", [(source, source + steps) for source in range(first, last)])


steps = (1, 3, 2)


def move_first(parts):
    return (
        [parts[0]]
        + [move_x(p, d) for p, d in zip(parts[1:4], steps)]
        + [parts[4]]
        + [move_y(p, d) for p, d in zip(parts[5:8], steps)]
    )


def move_second(parts):
    return (
        [parts[0]]
        + [move_y(p, d) for p, d in zip(parts[1:4], steps)]
        + [parts[4]]
        + [move_x(p, d) for p, d in zip(parts[5:8], steps)]
    )


def together(*groups):
    leaves, tree = jax.tree.flatten(groups)
    return jax.tree.unflatten(tree, lax.optimization_barrier(tuple(leaves)))


def body(
    hidden_in,
    cotangent,
    positions,
    query_weight,
    key_weight,
    value_weight,
    output_weight,
    gate_weight,
    up_weight,
    down_weight,
    norm_in,
    norm_attn,
    norm_ffn_in,
    norm_ffn_out,
    norm_query,
    norm_key,
):
    s = lax.axis_index("seq")
    f = lax.axis_index("fsdp")
    x, y, z_lo, core = s // 4 % 4, s % 4, f // 2, f % 2
    place = f.astype(jnp.int32).reshape(1)
    spot = jnp.stack([x, y]).astype(jnp.int32)
    own = hidden_in[0]
    upstream = cotangent[0]
    offsets = positions[0]

    near = jnp.concatenate([query_weight, gate_weight], axis=1)
    far = jnp.concatenate([key_weight, value_weight, up_weight], axis=1)
    near_partner, far_partner = swap_near(near), swap_far(far)
    halo = shifted(own, 1)
    q_shares = (near, swap_core(near), near_partner, swap_core(near_partner))
    kv_shares = (far, swap_core(far), far_partner, swap_core(far_partner))
    wo_partner, wd_partner = swap_near(output_weight), swap_far(down_weight)
    tile = pack([norm_in, norm_attn, norm_ffn_in, norm_ffn_out, norm_query, norm_key])
    tiles = lax.all_gather(tile, "fsdp")
    gains = jnp.concatenate([tiles[j, :, :160] for j in range(4)], axis=1)
    head_gains = jnp.concatenate([tiles[j, :, :64] for j in range(4)], axis=1)

    cosine, sine = rope_tables(offsets)
    column = offsets[:, None]
    normed, q, k, v, q_proj, k_proj = project(
        place, halo, own, gains, head_gains, q_shares, kv_shares, cosine, sine
    )
    (q, k, v), wo_partner, wd_partner = together((q, k, v), wo_partner, wd_partner)
    wo_shares = (output_weight, swap_core(output_weight), wo_partner, swap_core(wo_partner))
    wd_shares = (down_weight, swap_core(down_weight), wd_partner, swap_core(wd_partner))
    attended, level = attend(q, k, v, column)
    layer_out, back_middle, back_attn, back_attended, gain_mid, kept, sent = middle_part(
        place, own, attended, upstream, gains, wo_shares + q_shares + kv_shares + wd_shares
    )
    got = swap_core(sent)
    back_q, back_kv, gain_head, back_halo = attend_back(
        q,
        k,
        v,
        column,
        level,
        back_attended,
        q_proj,
        k_proj,
        head_gains,
        cosine,
        sine,
        place,
        kv_shares,
    )
    back_own, kept_attn, sent = weights_part(
        place,
        normed,
        back_q,
        back_kv,
        attended,
        back_attn,
        halo,
        own,
        gain_mid,
        gain_head,
        q_shares + kv_shares,
    )
    got_attn = swap_core(sent)
    first = move_first(first_sums(spot, kept, got, kept_attn, got_attn))
    mine, other = third_sums(place, move_second(second_sums(spot, first)))
    returned = shifted(back_halo, -1)
    a, b = fourth_sums([mine, swap_near(other), swap_far(other), swap_hi(mine)])
    a, b, returned = together(a, b, returned)
    a = jnp.stack([a] + [move_y(a, d) for d in (1, 2, 3)])
    b = jnp.stack([b] + [move_x(b, d) for d in (1, 2, 3)])
    a, b = together(a, b)
    pieces = [a] + [move_x(a, d) for d in (1, 2, 3)] + [b] + [move_y(b, d) for d in (1, 2, 3)]
    grad_q, grad_k, grad_v, grad_o, grad_g, grad_u, grad_d, tile = unpack(spot, pieces)
    grad_in = finish(own, back_own, returned, back_middle, gains)
    wide = jnp.concatenate([tile[0:4], tile[4:8, :32]], axis=1)
    return (
        layer_out[None],
        grad_in[None],
        grad_q,
        grad_k,
        grad_v,
        grad_o,
        grad_g,
        grad_u,
        grad_d,
        wide[0],
        wide[1],
        wide[2],
        wide[3],
        tile[8, :64],
        tile[9, :64],
    )


def solution(mesh):
    three = P("fsdp", "seq", None)
    two = P("fsdp", None)
    one = P("fsdp")
    return jax.shard_map(
        body,
        mesh=mesh,
        in_specs=(three, three, P("fsdp", "seq")) + (two,) * 7 + (one,) * 6,
        out_specs=(three, three) + (two,) * 7 + (one,) * 6,
        check_vma=False,
    )
```

```python
import jax
import jax.numpy as jnp
from jax import lax
from jax.experimental import pallas as pl
from jax.experimental.pallas import tpu as pltpu
from jax.sharding import PartitionSpec as P

WINDOW = 512
epsilon = 1e-06
rope_base = 10000.0
masked_value = -1e30
bf16 = jnp.bfloat16
f32 = jnp.float32

rows_out = ((1,), (0,))
rows_both = ((1,), (1,))
cols_both = ((0,), (0,))


def dot(a, b, dims=rows_out):
    return lax.dot_general(a, b, (dims, ((), ())), preferred_element_type=f32)


def spec(*shape):
    return jax.ShapeDtypeStruct(shape[:-1], shape[-1])


def whole():
    return pl.BlockSpec(memory_space=pltpu.VMEM)


def params(mib):
    return pltpu.CompilerParams(vmem_limit_bytes=mib * 1024 * 1024)


def cost(flops, moved, exps=0):
    return pl.CostEstimate(flops=flops, bytes_accessed=moved, transcendentals=exps)


def inverse_rms(v):
    return lax.rsqrt(jnp.mean(v * v, axis=-1, keepdims=True) + epsilon)


def norm_back(v, r, gain, e):
    scaled = gain * e
    return r * scaled - v * (r * r * r * jnp.mean(v * scaled, axis=-1, keepdims=True))


def turn(v, cosine, sine):
    a, b = v[:, :128], v[:, 128:]
    return jnp.concatenate([a * cosine - b * sine, b * cosine + a * sine], axis=1)


def turn_back(v, cosine, sine):
    a, b = v[:, :128], v[:, 128:]
    return jnp.concatenate([a * cosine + b * sine, b * cosine - a * sine], axis=1)


def assemble(pieces, into, place, semaphores, first):
    rows = into.shape[0] // 4
    copies = []
    for r in range(4):
        at = pl.ds(pl.multiple_of((place ^ r) * rows, rows), rows)
        copies.append(
            pltpu.make_async_copy(
                pieces[r],
                into.at[at, :],
                semaphores.at[first + r],
            )
        )
    for copy in copies:
        copy.start()
    return copies


def split_out(grads, kept, sent, place, semaphores, first):
    core = lax.rem(place, 2)
    copies = []
    for z in range(2):
        copies.append(
            pltpu.make_async_copy(
                grads.at[2 * z + 1 - core], sent.at[z], semaphores.at[first + 2 * z]
            )
        )
        copies.append(
            pltpu.make_async_copy(
                grads.at[2 * z + core], kept.at[z], semaphores.at[first + 2 * z + 1]
            )
        )
    for copy in copies:
        copy.start()
    return copies


def pack_kernel(g0, g1, g2, g3, g4, g5, out, *rest):
    held, semaphores = rest[:6], rest[6]
    copies = [
        pltpu.make_async_copy(source, into, semaphores.at[i])
        for i, (source, into) in enumerate(zip((g0, g1, g2, g3, g4, g5), held))
    ]
    for copy in copies:
        copy.start()
    out[...] = jnp.zeros_like(out)
    for copy in copies:
        copy.wait()
    for i, ref in enumerate(held):
        n = ref.shape[0]
        out[i : i + 1, :n] = ref[...].astype(f32).reshape(1, n)


def pack(rows):
    return pl.pallas_call(
        pack_kernel,
        name="pack",
        in_specs=[pl.BlockSpec(memory_space=pltpu.HBM)] * 6,
        out_specs=whole(),
        out_shape=spec(8, 256, f32),
        scratch_shapes=[pltpu.VMEM(row.shape, bf16) for row in rows]
        + [pltpu.SemaphoreType.DMA((6,))],
        compiler_params=params(4),
        cost_estimate=cost(100_000, 20_000),
    )(*rows)


def project_kernel(
    place,
    halo,
    own,
    gains,
    head_gains,
    q0,
    q1,
    q2,
    q3,
    kv0,
    kv1,
    kv2,
    kv3,
    cosine,
    sine,
    normed,
    q,
    k,
    v,
    q_proj,
    k_proj,
    wq,
    wkv,
    semaphores,
):
    i = pl.program_id(0)

    @pl.when(i == 0)
    def _():
        copies = assemble((kv0, kv1, kv2, kv3), wkv, place[0], semaphores, 0)
        copies += assemble((q0, q1, q2, q3), wq, place[0], semaphores, 4)
        for copy in copies:
            copy.wait()

    x = jnp.where(i < 2, halo[...], own[...]).astype(f32)
    n = (x * inverse_rms(x) * gains[0:1]).astype(bf16)
    normed[...] = n
    c, s = cosine[...], sine[...]
    kv = dot(n, wkv[...])
    kp = kv[:, :256]
    k_proj[...] = kp
    v[...] = kv[:, 256:].astype(bf16)
    k[...] = turn(kp * inverse_rms(kp) * head_gains[5:6], c, s).astype(bf16)

    @pl.when(i >= 2)
    def _():
        for h in range(4):
            cols = slice(256 * h, 256 * h + 256)
            qp = dot(n, wq[:, cols])
            q_proj[:, cols] = qp
            q[:, cols] = turn(qp * inverse_rms(qp) * head_gains[4:5], c, s).astype(bf16)


def project(place, halo, own, gains, head_gains, q_shares, kv_shares, cosine, sine):
    late = lambda i: (jnp.maximum(i - 2, 0), 0)
    row = lambda i: (i, 0)
    fixed = lambda i: (0, 0)
    return pl.pallas_call(
        project_kernel,
        name="project",
        grid=(4,),
        in_specs=[
            pl.BlockSpec(memory_space=pltpu.SMEM),
            pl.BlockSpec((256, 640), lambda i: (jnp.minimum(i, 1), 0)),
            pl.BlockSpec((256, 640), late),
            pl.BlockSpec((8, 640), fixed),
            pl.BlockSpec((8, 256), fixed),
        ]
        + [pl.BlockSpec(memory_space=pltpu.HBM)] * 8
        + [pl.BlockSpec((256, 128), row)] * 2,
        out_specs=[
            pl.BlockSpec((256, 640), row),
            pl.BlockSpec((256, 1024), late),
            pl.BlockSpec((256, 256), row),
            pl.BlockSpec((256, 256), row),
            pl.BlockSpec((256, 1024), late),
            pl.BlockSpec((256, 256), row),
        ],
        out_shape=[
            spec(1024, 640, bf16),
            spec(512, 1024, bf16),
            spec(1024, 256, bf16),
            spec(1024, 256, bf16),
            spec(512, 1024, f32),
            spec(1024, 256, f32),
        ],
        scratch_shapes=[
            pltpu.VMEM((640, 1024), bf16),
            pltpu.VMEM((640, 512), bf16),
            pltpu.SemaphoreType.DMA((8,)),
        ],
        compiler_params=params(14),
        cost_estimate=cost(1_350_000_000, 9_000_000),
    )(place, halo, own, gains, head_gains, *q_shares, *kv_shares, cosine, sine)


def visible_keys(offsets):
    distance = (
        lax.broadcasted_iota(jnp.int32, (256, 768), 0)
        + 512
        - lax.broadcasted_iota(jnp.int32, (256, 768), 1)
    )
    return (distance >= 0) & (distance < WINDOW) & (distance <= offsets)


def attend_kernel(q, k, v, offsets, attended, level):
    t = pl.program_id(0)
    near = pl.ds(pl.multiple_of(t * 256, 256), 768)
    keys, values = k[near, :], v[near, :]
    visible = visible_keys(offsets[...])
    for h in range(4):
        cols = slice(256 * h, 256 * h + 256)
        scores = jnp.where(visible, dot(q[:, cols], keys, rows_both) * 0.0625, masked_value)
        top = jnp.max(scores, axis=-1, keepdims=True)
        e = jnp.exp(scores - top)
        total = jnp.sum(e, axis=-1, keepdims=True)
        level[h] = top + jnp.log(total)
        probs = (e * (1.0 / total)).astype(bf16)
        attended[:, cols] = dot(probs, values).astype(bf16)


def attend(q, k, v, offsets):
    row = lambda i: (i, 0)
    fixed = lambda i: (0, 0)
    return pl.pallas_call(
        attend_kernel,
        name="attend",
        grid=(2,),
        in_specs=[
            pl.BlockSpec((256, 1024), row),
            pl.BlockSpec((1024, 256), fixed),
            pl.BlockSpec((1024, 256), fixed),
            pl.BlockSpec((256, 1), row),
        ],
        out_specs=[
            pl.BlockSpec((256, 1024), row),
            pl.BlockSpec((4, 256, 1), lambda i: (0, i, 0)),
        ],
        out_shape=[spec(512, 1024, bf16), spec(4, 512, 1, f32)],
        compiler_params=params(10),
        cost_estimate=cost(1_700_000_000, 4_000_000, 2_000_000),
    )(q, k, v, offsets)


def middle_kernel(
    place,
    x_ref,
    attended,
    upstream,
    gains,
    o0,
    o1,
    o2,
    o3,
    g0,
    g1,
    g2,
    g3,
    u0,
    u1,
    u2,
    u3,
    d0,
    d1,
    d2,
    d3,
    layer_out,
    back_middle,
    back_attn,
    back_attended,
    gain_grads,
    kept,
    sent,
    ffn_in,
    kept_a,
    kept_b,
    hidden,
    back_out,
    in_turned,
    out_turned,
    back_gate,
    back_up,
    wo,
    wg,
    wu,
    wd,
    grads,
    semaphores,
):
    output_copies = assemble((o0, o1, o2, o3), wo, place[0], semaphores, 0)
    gate_copies = assemble((g0, g1, g2, g3), wg, place[0], semaphores, 4)
    up_copies = assemble((u0, u1, u2, u3), wu, place[0], semaphores, 8)
    down_copies = assemble((d0, d1, d2, d3), wd, place[0], semaphores, 12)
    for copy in output_copies:
        copy.wait()
    g_attn, g_in, g_out = gains[1:2], gains[2:3], gains[3:4]
    ao = dot(attended[...], wo[...])
    r1 = inverse_rms(ao)
    mid = x_ref[...].astype(f32) + ao * r1 * g_attn
    r2 = inverse_rms(mid)
    ffn_in[...] = (mid * r2 * g_in).astype(bf16)
    for copy in gate_copies + up_copies:
        copy.wait()

    for j in range(8):
        cols = slice(256 * j, 256 * j + 256)
        u = dot(ffn_in[...], wg[:, cols])
        up = dot(ffn_in[...], wu[:, cols])
        root = 0.7978845608028654
        square = u * u
        t = jnp.tanh(u * (root + (root * 0.044715) * square))
        half = 0.5 + 0.5 * t
        act = u * half
        slope = half + act * (1.0 - t) * (root + (3 * 0.044715 * root) * square)
        hidden[:, cols] = (act * up).astype(bf16)
        kept_a[:, cols] = act
        kept_b[:, cols] = up * slope

    for copy in down_copies:
        copy.wait()
    fo = dot(hidden[...], wd[...])
    r3 = inverse_rms(fo)
    layer_out[...] = (mid + fo * r3 * g_out).astype(bf16)
    g = upstream[...].astype(f32)
    gain_grads[2:3] = jnp.sum(fo * r3 * g, axis=0, keepdims=True)
    bfo = norm_back(fo, r3, g_out, g)
    back_out[...] = bfo.astype(bf16)
    out_turned[...] = back_out[...].T
    in_turned[...] = ffn_in[...].T

    for j in range(8):
        cols = slice(256 * j, 256 * j + 256)
        bh = dot(back_out[...], wd[cols, :], rows_both)
        bu = (bh * kept_a[:, cols]).astype(bf16)
        bg = (bh * kept_b[:, cols]).astype(bf16)
        back_gate[:, cols] = bg
        back_up[:, cols] = bu

    for base, right in ((0, back_gate), (2560, back_up)):
        for j in range(2048 // 512):
            part = dot(in_turned[...], right[:, 512 * j : 512 * j + 512]).astype(bf16)
            for b in range(512 // 128):
                at = base + (512 // 128 * j + b) * 160
                for f in range(4):
                    grads[f, at : at + 160, :] = part[
                        160 * f : 160 * f + 160, 128 * b : 128 * b + 128
                    ]
    for f in range(4):
        part = dot(out_turned[...], hidden[:, 512 * f : 512 * f + 512]).astype(bf16)
        for b in range(4):
            at = 5120 + 640 * b
            grads[f, at : at + 640, :] = part[:, 128 * b : 128 * b + 128]

    outward = split_out(grads, kept, sent, place[0], semaphores, 16)
    e = dot(back_gate[...], wg[...], rows_both) + dot(back_up[...], wu[...], rows_both)
    gain_grads[1:2] = jnp.sum(mid * r2 * e, axis=0, keepdims=True)
    bm = g + norm_back(mid, r2, g_in, e)
    back_middle[...] = bm
    gain_grads[0:1] = jnp.sum(ao * r1 * bm, axis=0, keepdims=True)
    bao = norm_back(ao, r1, g_attn, bm).astype(bf16)
    back_attn[...] = bao
    back_attended[...] = dot(bao, wo[...], rows_both).astype(bf16)
    for copy in outward:
        copy.wait()


def middle_part(place, x, attended, upstream, gains, shares):
    return pl.pallas_call(
        middle_kernel,
        name="middle_part",
        in_specs=[pl.BlockSpec(memory_space=pltpu.SMEM)]
        + [whole()] * 4
        + [pl.BlockSpec(memory_space=pltpu.HBM)] * 16,
        out_specs=[whole()] * 5 + [pl.BlockSpec(memory_space=pltpu.HBM)] * 2,
        out_shape=[
            spec(512, 640, bf16),
            spec(512, 640, f32),
            spec(512, 640, bf16),
            spec(512, 1024, bf16),
            spec(8, 640, f32),
            spec(2, 7680, 128, bf16),
            spec(2, 7680, 128, bf16),
        ],
        scratch_shapes=[
            pltpu.VMEM((512, 640), bf16),
            pltpu.VMEM((512, 2048), f32),
            pltpu.VMEM((512, 2048), f32),
            pltpu.VMEM((512, 2048), bf16),
            pltpu.VMEM((512, 640), bf16),
            pltpu.VMEM((640, 512), bf16),
            pltpu.VMEM((640, 512), bf16),
            pltpu.VMEM((512, 2048), bf16),
            pltpu.VMEM((512, 2048), bf16),
            pltpu.VMEM((1024, 640), bf16),
            pltpu.VMEM((640, 2048), bf16),
            pltpu.VMEM((640, 2048), bf16),
            pltpu.VMEM((2048, 640), bf16),
            pltpu.VMEM((4, 7680, 128), bf16),
            pltpu.SemaphoreType.DMA((20,)),
        ],
        compiler_params=params(44),
        cost_estimate=cost(13_400_000_000, 23_000_000, 1_000_000),
    )(place, x, attended, upstream, gains, *shares)


def attend_back_kernel(
    q,
    k,
    v,
    offsets,
    level,
    back_attended,
    q_proj,
    k_proj,
    head_gains,
    cosine,
    sine,
    place,
    kv0,
    kv1,
    kv2,
    kv3,
    back_q,
    back_kv,
    gain_grads,
    back_halo,
    sum_k,
    sum_v,
    wkv,
    semaphores,
):
    t = pl.program_id(0)

    @pl.when(t == 0)
    def _():
        for copy in assemble((kv0, kv1, kv2, kv3), wkv, place[0], semaphores, 0):
            copy.wait()
        sum_k[...] = jnp.zeros_like(sum_k)
        sum_v[...] = jnp.zeros_like(sum_v)
        gain_grads[...] = jnp.zeros_like(gain_grads)

    near = pl.ds(pl.multiple_of(t * 256, 256), 768)
    mine = pl.ds(pl.multiple_of(t * 256 + 512, 256), 256)
    keys, values = k[near, :], v[near, :]
    visible = visible_keys(offsets[...])
    c, s = cosine[mine, :], sine[mine, :]
    for h in range(4):
        cols = slice(256 * h, 256 * h + 256)
        qh, bah = q[:, cols], back_attended[:, cols]
        scores = jnp.where(visible, dot(qh, keys, rows_both) * 0.0625, masked_value)
        probs = jnp.exp(scores - level[h])
        bp = dot(bah, values, rows_both)
        inner = jnp.sum(probs * bp, axis=-1, keepdims=True)
        bs = (probs * (bp - inner)).astype(bf16)
        sum_k[near, :] += dot(bs, qh, cols_both)
        sum_v[near, :] += dot(probs.astype(bf16), bah, cols_both)
        e = turn_back(dot(bs, keys) * 0.0625, c, s)
        qp = q_proj[:, cols]
        r = inverse_rms(qp)
        gain_grads[0:1] += jnp.sum(qp * r * e, axis=0, keepdims=True)
        back_q[:, cols] = norm_back(qp, r, head_gains[4:5], e).astype(bf16)

    @pl.when(t == 1)
    def _():
        e = turn_back(sum_k[...] * 0.0625, cosine[...], sine[...])
        kp = k_proj[...]
        r = inverse_rms(kp)
        gain_grads[1:2] = jnp.sum(kp * r * e, axis=0, keepdims=True)
        back_kv[:, :256] = norm_back(kp, r, head_gains[5:6], e).astype(bf16)
        back_kv[:, 256:] = sum_v[...].astype(bf16)
        back_halo[...] = dot(back_kv[:512, :], wkv[...], rows_both).astype(bf16)


def attend_back(
    q, k, v, offsets, level, back_attended, q_proj, k_proj, head_gains, cosine, sine, place, shares
):
    row = lambda i: (i, 0)
    fixed = lambda i: (0, 0)
    return pl.pallas_call(
        attend_back_kernel,
        name="attend_back",
        grid=(2,),
        in_specs=[
            pl.BlockSpec((256, 1024), row),
            pl.BlockSpec((1024, 256), fixed),
            pl.BlockSpec((1024, 256), fixed),
            pl.BlockSpec((256, 1), row),
            pl.BlockSpec((4, 256, 1), lambda i: (0, i, 0)),
            pl.BlockSpec((256, 1024), row),
            pl.BlockSpec((256, 1024), row),
            pl.BlockSpec((1024, 256), fixed),
            pl.BlockSpec((8, 256), fixed),
            pl.BlockSpec((1024, 128), fixed),
            pl.BlockSpec((1024, 128), fixed),
            pl.BlockSpec(memory_space=pltpu.SMEM),
        ]
        + [pl.BlockSpec(memory_space=pltpu.HBM)] * 4,
        out_specs=[
            pl.BlockSpec((256, 1024), row),
            pl.BlockSpec((1024, 512), fixed),
            pl.BlockSpec((8, 256), fixed),
            pl.BlockSpec((512, 640), fixed),
        ],
        out_shape=[
            spec(512, 1024, bf16),
            spec(1024, 512, bf16),
            spec(8, 256, f32),
            spec(512, 640, bf16),
        ],
        scratch_shapes=[
            pltpu.VMEM((1024, 256), f32),
            pltpu.VMEM((1024, 256), f32),
            pltpu.VMEM((640, 512), bf16),
            pltpu.SemaphoreType.DMA((4,)),
        ],
        compiler_params=params(16),
        cost_estimate=cost(4_300_000_000, 10_000_000, 2_000_000),
    )(
        q, k, v, offsets, level, back_attended, q_proj, k_proj, head_gains, cosine, sine, place, *shares
    )


def weights_kernel(
    place,
    normed,
    back_q,
    back_kv,
    attended,
    back_attn,
    halo,
    own,
    gain_mid,
    gain_head,
    q0,
    q1,
    q2,
    q3,
    kv0,
    kv1,
    kv2,
    kv3,
    back_own,
    kept,
    sent,
    wq,
    wkv,
    grads,
    semaphores,
):
    copies = assemble((kv0, kv1, kv2, kv3), wkv, place[0], semaphores, 0)
    copies += assemble((q0, q1, q2, q3), wq, place[0], semaphores, 4)
    turned = normed[...].astype(f32).T.astype(bf16)
    bq, bkv = back_q[...], back_kv[...]
    part = dot(turned[:, 512:], bq).astype(bf16)
    for b in range(8):
        for f in range(4):
            grads[f, 160 * b : 160 * b + 160, :] = part[
                160 * f : 160 * f + 160, 128 * b : 128 * b + 128
            ]
    part = dot(turned, bkv).astype(bf16)
    for b in range(4):
        for f in range(4):
            grads[f, 1280 + 160 * b : 1440 + 160 * b, :] = part[
                160 * f : 160 * f + 160, 128 * b : 128 * b + 128
            ]
    turned = back_attn[...].astype(f32).T.astype(bf16)
    part = dot(turned, attended[...]).astype(bf16)
    for f in range(4):
        for b in range(2):
            grads[f, 1920 + 640 * b : 2560 + 640 * b, :] = part[
                :, 256 * f + 128 * b : 256 * f + 128 * b + 128
            ]
    for copy in copies:
        copy.wait()
    e = dot(bkv[:512], wkv[...], rows_both)
    x = halo[...].astype(f32)
    grad = jnp.sum(x * inverse_rms(x) * e, axis=0, keepdims=True)
    e = dot(bkv[512:], wkv[...], rows_both) + dot(bq, wq[...], rows_both)
    back_own[...] = e
    x = own[...].astype(f32)
    grad = grad + jnp.sum(x * inverse_rms(x) * e, axis=0, keepdims=True)
    each = jnp.concatenate([grad, gain_mid[0:3]], axis=0)
    heads = gain_head[0:2]
    for f in range(4):
        share = each[:, 160 * f : 160 * f + 160]
        rest = jnp.concatenate([share[:, 128:], jnp.zeros((4, 96), f32)], axis=1)
        ends = jnp.concatenate([heads[:, 64 * f : 64 * f + 64], jnp.zeros((2, 64), f32)], axis=1)
        tile = jnp.concatenate([share[:, :128], rest, ends, jnp.zeros((6, 128), f32)], axis=0)
        grads[f, 3200:3216, :] = tile.astype(bf16)
        grads[f, 3216:, :] = jnp.zeros((368, 128), bf16)
    for copy in split_out(grads, kept, sent, place[0], semaphores, 8):
        copy.wait()


def weights_part(
    place, normed, back_q, back_kv, attended, back_attn, halo, own, gain_mid, gain_head, shares
):
    return pl.pallas_call(
        weights_kernel,
        name="weights_part",
        in_specs=[pl.BlockSpec(memory_space=pltpu.SMEM)]
        + [whole()] * 9
        + [pl.BlockSpec(memory_space=pltpu.HBM)] * 8,
        out_specs=[whole()] + [pl.BlockSpec(memory_space=pltpu.HBM)] * 2,
        out_shape=[
            spec(512, 640, f32),
            spec(2, 3584, 128, bf16),
            spec(2, 3584, 128, bf16),
        ],
        scratch_shapes=[
            pltpu.VMEM((640, 1024), bf16),
            pltpu.VMEM((640, 512), bf16),
            pltpu.VMEM((4, 3584, 128), bf16),
            pltpu.SemaphoreType.DMA((12,)),
        ],
        compiler_params=params(24),
        cost_estimate=cost(3_400_000_000, 14_000_000),
    )(place, normed, back_q, back_kv, attended, back_attn, halo, own, gain_mid, gain_head, *shares)


def finish_kernel(own, back_own, returned, back_middle, gains, grad_in):
    x = own[...].astype(f32)
    e = back_own[...] + returned[...].astype(f32)
    grad_in[...] = (back_middle[...] + norm_back(x, inverse_rms(x), gains[0:1], e)).astype(bf16)


def finish(own, back_own, returned, back_middle, gains):
    row = lambda i: (i, 0)
    return pl.pallas_call(
        finish_kernel,
        name="finish",
        grid=(4,),
        in_specs=[pl.BlockSpec((128, 640), row)] * 4 + [pl.BlockSpec((8, 640), lambda i: (0, 0))],
        out_specs=pl.BlockSpec((128, 640), row),
        out_shape=spec(512, 640, bf16),
        compiler_params=params(10),
        cost_estimate=cost(4_000_000, 5_000_000),
    )(own, back_own, returned, back_middle, gains)


def rope_tables(offsets):
    powers = jnp.arange(128, dtype=f32) * (2.0 / 256)
    row = jnp.arange(512, dtype=jnp.int32)
    every = jnp.concatenate([offsets[0] - 512 + row, offsets])
    angles = every.astype(f32)[:, None] * (rope_base ** (-powers))[None, :]
    return jnp.cos(angles), jnp.sin(angles)


def unpack_kernel(spot, a0, a1, a2, a3, b0, b1, b2, b3, *rest):
    outs, gains, held, (ffn, attn, semaphores) = rest[:7], rest[7], rest[8:15], rest[15:]
    q, k, v, out, gate, up, down = held
    x, y = spot[0], spot[1]
    copies = []
    for half, pieces in enumerate(((a0, a1, a2, a3), (b0, b1, b2, b3))):
        for i in range(4):
            for j in range(4):
                first, second = (x, y) if half == 0 else (y, x)
                block = 16 * half + lax.rem(first - i + 4, 4) * 4 + lax.rem(second - j + 4, 4)
                n = (half * 4 + i) * 4 + j
                for m, (into, start, rows) in enumerate(((ffn, 0, 240), (attn, 240, 112))):
                    copies.append(
                        pltpu.make_async_copy(
                            pieces[i].at[j, pl.ds(start, rows), :],
                            into.at[pl.ds(pl.multiple_of(block * rows, 16), rows), :],
                            semaphores.at[2 * n + m],
                        )
                    )
    for copy in copies:
        copy.start()
    for copy in copies:
        copy.wait()
    outward = []

    def leave(n):
        copy = pltpu.make_async_copy(held[n], outs[n], semaphores.at[64 + n])
        copy.start()
        outward.append(copy)

    for n, into, flat, first, count in (
        (4, gate, ffn, 0, 16),
        (5, up, ffn, 2560, 16),
        (0, q, attn, 0, 8),
        (1, k, attn, 1280, 2),
        (2, v, attn, 1600, 2),
    ):
        for b in range(count):
            at = first + 160 * b
            into[:, 128 * b : 128 * b + 128] = flat[at : at + 160, :].astype(f32)
        leave(n)
    for n, into, flat, first, count in ((6, down, ffn, 5120, 4), (3, out, attn, 1920, 2)):
        for b in range(count):
            at = first + 640 * b
            into[128 * b : 128 * b + 128, :] = flat[at : at + 640, :].astype(f32).T
        leave(n)
    gains[...] = attn[3200:3216, :].astype(f32)
    for copy in outward:
        copy.wait()


def unpack(spot, pieces):
    shapes = [(160, 1024), (160, 256), (160, 256), (256, 640), (160, 2048), (160, 2048), (512, 640)]
    return pl.pallas_call(
        unpack_kernel,
        name="unpack",
        in_specs=[pl.BlockSpec(memory_space=pltpu.SMEM)] + [pl.BlockSpec(memory_space=pltpu.HBM)] * 8,
        out_specs=[pl.BlockSpec(memory_space=pltpu.HBM)] * 7 + [whole()],
        out_shape=[spec(*shape, f32) for shape in shapes] + [spec(16, 128, f32)],
        scratch_shapes=[pltpu.VMEM(shape, f32) for shape in shapes]
        + [
            pltpu.VMEM((7680, 128), bf16),
            pltpu.VMEM((3584, 128), bf16),
            pltpu.SemaphoreType.DMA((71,)),
        ],
        compiler_params=params(14),
        cost_estimate=cost(4_000_000, 11_000_000),
    )(spot, *pieces)


def sum_of(parts):
    whole = parts[0].astype(f32)
    for part in parts[1:]:
        whole = whole + part.astype(f32)
    return whole.astype(bf16)


def turn_around(position, d):
    return lax.rem(position + d, 4)


def first_kernel(spot, kept_ffn, got_ffn, kept_attn, got_attn, *outs):
    for half in range(2):
        for i, d in enumerate((0, 1, 3, 2)):
            at = turn_around(spot[half], d)
            out = outs[4 * half + i]
            for z in range(2):
                for j in range(4):
                    out[z, j, :240] = sum_of([r[z, half, at, j] for r in (kept_ffn, got_ffn)])
                    out[z, j, 240:] = sum_of([r[z, half, at, j] for r in (kept_attn, got_attn)])


def first_sums(spot, kept_ffn, got_ffn, kept_attn, got_attn):
    ins = [p.reshape(2, 2, 4, 4, p.shape[1] // 32, 128) for p in (kept_ffn, got_ffn, kept_attn, got_attn)]
    return pl.pallas_call(
        first_kernel,
        name="first_sums",
        in_specs=[pl.BlockSpec(memory_space=pltpu.SMEM)] + [whole()] * 4,
        out_specs=[whole()] * 8,
        out_shape=[spec(2, 4, 352, 128, bf16)] * 8,
        compiler_params=params(24),
        cost_estimate=cost(3_000_000, 17_000_000),
    )(spot, *ins)


def second_kernel(spot, *refs):
    ins, outs = refs[:8], refs[8:]
    for half in range(2):
        parts = ins[4 * half : 4 * half + 4]
        for i, d in enumerate((0, 1, 3, 2)):
            at = turn_around(spot[1 - half], d)
            for z in range(2):
                outs[4 * half + i][z] = sum_of([r[z, at] for r in parts])


def second_sums(spot, parts):
    return pl.pallas_call(
        second_kernel,
        name="second_sums",
        in_specs=[pl.BlockSpec(memory_space=pltpu.SMEM)] + [whole()] * 8,
        out_specs=[whole()] * 8,
        out_shape=[spec(2, 352, 128, bf16)] * 8,
        compiler_params=params(12),
        cost_estimate=cost(1_000_000, 7_200_000),
    )(spot, *parts)


def third_kernel(place, *refs):
    ins, (mine, other) = refs[:8], refs[8:]
    z = lax.div(place[0], 2)
    for half in range(2):
        parts = ins[4 * half : 4 * half + 4]
        mine[half] = sum_of([r[z] for r in parts])
        other[half] = sum_of([r[1 - z] for r in parts])


def third_sums(place, parts):
    return pl.pallas_call(
        third_kernel,
        name="third_sums",
        in_specs=[pl.BlockSpec(memory_space=pltpu.SMEM)] + [whole()] * 8,
        out_specs=[whole()] * 2,
        out_shape=[spec(2, 352, 128, bf16)] * 2,
        compiler_params=params(10),
        cost_estimate=cost(1_000_000, 1_800_000),
    )(place, *parts)


def fourth_kernel(p0, p1, p2, p3, a, b):
    for half, out in enumerate((a, b)):
        out[...] = sum_of([p0[half], p1[half], p2[half], p3[half]])


def fourth_sums(parts):
    return pl.pallas_call(
        fourth_kernel,
        name="fourth_sums",
        in_specs=[whole()] * 4,
        out_specs=[whole()] * 2,
        out_shape=[spec(352, 128, bf16)] * 2,
        compiler_params=params(10),
        cost_estimate=cost(1_000_000, 900_000),
    )(*parts)


def seq_index(z, x, y):
    return (z % 2 * 4 + x % 4) * 4 + y % 4


def along_xy(dx, dy):
    return [
        (seq_index(z, x, y), seq_index(z, x + dx, y + dy))
        for z in range(2)
        for x in range(4)
        for y in range(4)
    ]


def along_z(step):
    pairs = []
    for s in range(32):
        for f in range(4):
            z = s // 16 * 2 + f // 2
            t = step(z)
            pairs.append((s * 4 + f, (t // 2 * 16 + s % 16) * 4 + t % 2 * 2 + f % 2))
    return pairs


def swap_core(value):
    return lax.ppermute(value, "fsdp", [(0, 1), (1, 0), (2, 3), (3, 2)])


def swap_near(value):
    return lax.ppermute(value, "fsdp", [(0, 2), (1, 3), (2, 0), (3, 1)])


def swap_across(value):
    return lax.ppermute(value, "fsdp", [(0, 3), (1, 2), (2, 1), (3, 0)])


def swap_far(value):
    return lax.ppermute(value, ("seq", "fsdp"), along_z(lambda z: 3 - z))


def swap_hi(value):
    return lax.ppermute(value, "seq", [(s, (s + 16) % 32) for s in range(32)])


def move_x(value, d):
    return lax.ppermute(value, "seq", along_xy(d, 0))


def move_y(value, d):
    return lax.ppermute(value, "seq", along_xy(0, d))


def shifted(value, steps):
    first, last = (max(0, -steps), min(32, 32 - steps))
    return lax.ppermute(value, "seq", [(source, source + steps) for source in range(first, last)])


steps = (1, 3, 2)


def move_first(parts):
    return (
        [parts[0]]
        + [move_x(p, d) for p, d in zip(parts[1:4], steps)]
        + [parts[4]]
        + [move_y(p, d) for p, d in zip(parts[5:8], steps)]
    )


def move_second(parts):
    return (
        [parts[0]]
        + [move_y(p, d) for p, d in zip(parts[1:4], steps)]
        + [parts[4]]
        + [move_x(p, d) for p, d in zip(parts[5:8], steps)]
    )


def together(*groups):
    leaves, tree = jax.tree.flatten(groups)
    return jax.tree.unflatten(tree, lax.optimization_barrier(tuple(leaves)))


def body(
    hidden_in,
    cotangent,
    positions,
    query_weight,
    key_weight,
    value_weight,
    output_weight,
    gate_weight,
    up_weight,
    down_weight,
    norm_in,
    norm_attn,
    norm_ffn_in,
    norm_ffn_out,
    norm_query,
    norm_key,
):
    s = lax.axis_index("seq")
    f = lax.axis_index("fsdp")
    x, y, z_lo, core = s // 4 % 4, s % 4, f // 2, f % 2
    place = f.astype(jnp.int32).reshape(1)
    spot = jnp.stack([x, y]).astype(jnp.int32)
    own = hidden_in[0]
    upstream = cotangent[0]
    offsets = positions[0]

    q_partner = swap_near(query_weight)
    kv = jnp.concatenate([key_weight, value_weight], axis=1)
    kv_partner = swap_far(kv)
    wg_partner, wu_partner = swap_near(gate_weight), swap_far(up_weight)
    halo = shifted(own, 1)
    rows = (norm_in, norm_attn, norm_ffn_in, norm_ffn_out, norm_query, norm_key)
    q_partner, rows = together(q_partner, rows)
    tile = pack(rows)
    tiles = [tile, swap_core(tile), swap_near(tile), swap_across(tile)]
    tiles = [
        jnp.where(
            j // 2 == z_lo,
            jnp.where(j % 2 == core, tiles[0], tiles[1]),
            jnp.where(j % 2 == core, tiles[2], tiles[3]),
        )
        for j in range(4)
    ]
    gains = jnp.concatenate([t[:, :160] for t in tiles], axis=1)
    head_gains = jnp.concatenate([t[:, :64] for t in tiles], axis=1)
    q_shares = (query_weight, swap_core(query_weight), q_partner, swap_core(q_partner))
    kv_shares = (kv, swap_core(kv), kv_partner, swap_core(kv_partner))
    (q_shares, kv_shares, halo), (wg_partner, wu_partner) = together(
        (q_shares, kv_shares, halo), (wg_partner, wu_partner)
    )
    wo_partner, wd_partner = swap_near(output_weight), swap_far(down_weight)

    cosine, sine = rope_tables(offsets)
    column = offsets[:, None]
    normed, q, k, v, q_proj, k_proj = project(
        place, halo, own, gains, head_gains, q_shares, kv_shares, cosine, sine
    )
    attended, level = attend(q, k, v, column)
    own_weights = (output_weight, gate_weight, up_weight, down_weight)
    partners = (wo_partner, wg_partner, wu_partner, wd_partner)
    attended, own_weights = together(attended, own_weights)
    siblings = [swap_core(w) for w in own_weights]
    shares = []
    for share, sibling, partner in zip(own_weights, siblings, partners):
        attended, partner = together(attended, partner)
        shares += [share, sibling, partner, swap_core(partner)]
    layer_out, back_middle, back_attn, back_attended, gain_mid, kept, sent = middle_part(
        place, own, attended, upstream, gains, shares
    )
    got = swap_core(sent)
    back_q, back_kv, gain_head, back_halo = attend_back(
        q,
        k,
        v,
        column,
        level,
        back_attended,
        q_proj,
        k_proj,
        head_gains,
        cosine,
        sine,
        place,
        kv_shares,
    )
    back_own, kept_attn, sent = weights_part(
        place,
        normed,
        back_q,
        back_kv,
        attended,
        back_attn,
        halo,
        own,
        gain_mid,
        gain_head,
        q_shares + kv_shares,
    )
    got_attn = swap_core(sent)
    first = move_first(first_sums(spot, kept, got, kept_attn, got_attn))
    mine, other = third_sums(place, move_second(second_sums(spot, first)))
    returned = shifted(back_halo, -1)
    a, b = fourth_sums([mine, swap_near(other), swap_far(other), swap_hi(mine)])
    a, b, returned = together(a, b, returned)
    a = jnp.stack([a] + [move_y(a, d) for d in (1, 2, 3)])
    b = jnp.stack([b] + [move_x(b, d) for d in (1, 2, 3)])
    a, b = together(a, b)
    pieces = [a] + [move_x(a, d) for d in (1, 2, 3)] + [b] + [move_y(b, d) for d in (1, 2, 3)]
    grad_q, grad_k, grad_v, grad_o, grad_g, grad_u, grad_d, tile = unpack(spot, pieces)
    grad_in = finish(own, back_own, returned, back_middle, gains)
    wide = jnp.concatenate([tile[0:4], tile[4:8, :32]], axis=1)
    return (
        layer_out[None],
        grad_in[None],
        grad_q,
        grad_k,
        grad_v,
        grad_o,
        grad_g,
        grad_u,
        grad_d,
        wide[0],
        wide[1],
        wide[2],
        wide[3],
        tile[8, :64],
        tile[9, :64],
    )


def solution(mesh):
    three = P("fsdp", "seq", None)
    two = P("fsdp", None)
    one = P("fsdp")
    return jax.shard_map(
        body,
        mesh=mesh,
        in_specs=(three, three, P("fsdp", "seq")) + (two,) * 7 + (one,) * 6,
        out_specs=(three, three) + (two,) * 7 + (one,) * 6,
        check_vma=False,
    )
```

```python
import jax
import jax.numpy as jnp
from jax import lax
from jax.experimental import pallas as pl
from jax.experimental.pallas import tpu as pltpu
from jax.sharding import PartitionSpec as P

WINDOW = 512
epsilon = 1e-06
rope_base = 10000.0
masked_value = -1e30
bf16 = jnp.bfloat16
f32 = jnp.float32

rows_out = ((1,), (0,))
rows_both = ((1,), (1,))
cols_both = ((0,), (0,))


def dot(a, b, dims=rows_out):
    return lax.dot_general(a, b, (dims, ((), ())), preferred_element_type=f32)


def spec(*shape):
    return jax.ShapeDtypeStruct(shape[:-1], shape[-1])


def whole():
    return pl.BlockSpec(memory_space=pltpu.VMEM)


def params(mib):
    return pltpu.CompilerParams(vmem_limit_bytes=mib * 1024 * 1024)


def cost(flops, moved, exps=0):
    return pl.CostEstimate(flops=flops, bytes_accessed=moved, transcendentals=exps)


def inverse_rms(v):
    return lax.rsqrt(jnp.mean(v * v, axis=-1, keepdims=True) + epsilon)


def norm_back(v, r, gain, e):
    scaled = gain * e
    return r * scaled - v * (r * r * r * jnp.mean(v * scaled, axis=-1, keepdims=True))


def turn(v, cosine, sine):
    a, b = v[:, :128], v[:, 128:]
    return jnp.concatenate([a * cosine - b * sine, b * cosine + a * sine], axis=1)


def turn_back(v, cosine, sine):
    a, b = v[:, :128], v[:, 128:]
    return jnp.concatenate([a * cosine + b * sine, b * cosine - a * sine], axis=1)


def assemble(pieces, into, place, semaphores, first):
    rows = into.shape[0] // 4
    copies = []
    for r in range(4):
        at = pl.ds(pl.multiple_of((place ^ r) * rows, rows), rows)
        copies.append(
            pltpu.make_async_copy(
                pieces[r].at[pl.ds(0, rows), :],
                into.at[at, :],
                semaphores.at[first + r],
            )
        )
    for copy in copies:
        copy.start()
    return copies


def split_out(grads, kept, sent, place, semaphores, first):
    core = lax.rem(place, 2)
    copies = []
    for z in range(2):
        copies.append(
            pltpu.make_async_copy(
                grads.at[2 * z + 1 - core], sent.at[z], semaphores.at[first + 2 * z]
            )
        )
        copies.append(
            pltpu.make_async_copy(
                grads.at[2 * z + core], kept.at[z], semaphores.at[first + 2 * z + 1]
            )
        )
    for copy in copies:
        copy.start()
    return copies


def pack_kernel(g0, g1, g2, g3, g4, g5, k, v, kv, *rest):
    held, semaphores = rest[:6], rest[6]
    copies = [
        pltpu.make_async_copy(source, into, semaphores.at[i])
        for i, (source, into) in enumerate(zip((g0, g1, g2, g3, g4, g5), held))
    ]
    for copy in copies:
        copy.start()
    kv[:160, :256] = k[...]
    kv[:160, 256:] = v[...]
    tile = []
    for copy in copies:
        copy.wait()
    for ref in held:
        n = ref.shape[0]
        row = ref[...].astype(f32).reshape(1, n)
        tile.append(jnp.concatenate([row, jnp.zeros((1, 512 - n), f32)], axis=1))
    tile.append(jnp.zeros((10, 512), f32))
    kv[160:, :] = jnp.concatenate(tile, axis=0).astype(bf16)


def pack(rows, key_weight, value_weight):
    return pl.pallas_call(
        pack_kernel,
        name="pack",
        in_specs=[pl.BlockSpec(memory_space=pltpu.HBM)] * 6 + [whole()] * 2,
        out_specs=whole(),
        out_shape=spec(176, 512, bf16),
        scratch_shapes=[pltpu.VMEM(row.shape, bf16) for row in rows]
        + [pltpu.SemaphoreType.DMA((6,))],
        compiler_params=params(4),
        cost_estimate=cost(100_000, 400_000),
    )(*rows, key_weight, value_weight)


def project_kernel(
    place,
    halo,
    own,
    gains,
    head_gains,
    q0,
    q1,
    q2,
    q3,
    kv0,
    kv1,
    kv2,
    kv3,
    cosine,
    sine,
    normed,
    q,
    k,
    v,
    q_proj,
    k_proj,
    wq,
    wkv,
    semaphores,
):
    i = pl.program_id(0)

    @pl.when(i == 0)
    def _():
        copies = assemble((kv0, kv1, kv2, kv3), wkv, place[0], semaphores, 0)
        copies += assemble((q0, q1, q2, q3), wq, place[0], semaphores, 4)
        for copy in copies:
            copy.wait()

    x = jnp.where(i < 2, halo[...], own[...]).astype(f32)
    n = (x * inverse_rms(x) * gains[0:1]).astype(bf16)
    normed[...] = n
    c, s = cosine[...], sine[...]
    kv = dot(n, wkv[...])
    kp = kv[:, :256]
    k_proj[...] = kp
    v[...] = kv[:, 256:].astype(bf16)
    k[...] = turn(kp * inverse_rms(kp) * head_gains[5:6], c, s).astype(bf16)

    @pl.when(i >= 2)
    def _():
        for h in range(4):
            cols = slice(256 * h, 256 * h + 256)
            qp = dot(n, wq[:, cols])
            q_proj[:, cols] = qp
            q[:, cols] = turn(qp * inverse_rms(qp) * head_gains[4:5], c, s).astype(bf16)


def project(place, halo, own, gains, head_gains, q_shares, kv_shares, cosine, sine):
    late = lambda i: (jnp.maximum(i - 2, 0), 0)
    row = lambda i: (i, 0)
    fixed = lambda i: (0, 0)
    return pl.pallas_call(
        project_kernel,
        name="project",
        grid=(4,),
        in_specs=[
            pl.BlockSpec(memory_space=pltpu.SMEM),
            pl.BlockSpec((256, 640), lambda i: (jnp.minimum(i, 1), 0)),
            pl.BlockSpec((256, 640), late),
            pl.BlockSpec((8, 640), fixed),
            pl.BlockSpec((8, 256), fixed),
        ]
        + [pl.BlockSpec(memory_space=pltpu.HBM)] * 8
        + [pl.BlockSpec((256, 128), row)] * 2,
        out_specs=[
            pl.BlockSpec((256, 640), row),
            pl.BlockSpec((256, 1024), late),
            pl.BlockSpec((256, 256), row),
            pl.BlockSpec((256, 256), row),
            pl.BlockSpec((256, 1024), late),
            pl.BlockSpec((256, 256), row),
        ],
        out_shape=[
            spec(1024, 640, bf16),
            spec(512, 1024, bf16),
            spec(1024, 256, bf16),
            spec(1024, 256, bf16),
            spec(512, 1024, f32),
            spec(1024, 256, f32),
        ],
        scratch_shapes=[
            pltpu.VMEM((640, 1024), bf16),
            pltpu.VMEM((640, 512), bf16),
            pltpu.SemaphoreType.DMA((8,)),
        ],
        compiler_params=params(14),
        cost_estimate=cost(1_350_000_000, 9_000_000),
    )(place, halo, own, gains, head_gains, *q_shares, *kv_shares, cosine, sine)


def visible_keys(offsets):
    distance = (
        lax.broadcasted_iota(jnp.int32, (256, 768), 0)
        + 512
        - lax.broadcasted_iota(jnp.int32, (256, 768), 1)
    )
    return (distance >= 0) & (distance < WINDOW) & (distance <= offsets)


def attend_kernel(q, k, v, offsets, attended, level):
    t = pl.program_id(0)
    near = pl.ds(pl.multiple_of(t * 256, 256), 768)
    keys, values = k[near, :], v[near, :]
    visible = visible_keys(offsets[...])
    for h in range(4):
        cols = slice(256 * h, 256 * h + 256)
        scores = jnp.where(visible, dot(q[:, cols], keys, rows_both) * 0.0625, masked_value)
        top = jnp.max(scores, axis=-1, keepdims=True)
        e = jnp.exp(scores - top)
        total = jnp.sum(e, axis=-1, keepdims=True)
        level[h] = top + jnp.log(total)
        probs = (e * (1.0 / total)).astype(bf16)
        attended[:, cols] = dot(probs, values).astype(bf16)


def attend(q, k, v, offsets):
    row = lambda i: (i, 0)
    fixed = lambda i: (0, 0)
    return pl.pallas_call(
        attend_kernel,
        name="attend",
        grid=(2,),
        in_specs=[
            pl.BlockSpec((256, 1024), row),
            pl.BlockSpec((1024, 256), fixed),
            pl.BlockSpec((1024, 256), fixed),
            pl.BlockSpec((256, 1), row),
        ],
        out_specs=[
            pl.BlockSpec((256, 1024), row),
            pl.BlockSpec((4, 256, 1), lambda i: (0, i, 0)),
        ],
        out_shape=[spec(512, 1024, bf16), spec(4, 512, 1, f32)],
        compiler_params=params(10),
        cost_estimate=cost(1_700_000_000, 4_000_000, 2_000_000),
    )(q, k, v, offsets)


def middle_kernel(
    place,
    x_ref,
    attended,
    upstream,
    gains,
    o0,
    o1,
    o2,
    o3,
    g0,
    g1,
    g2,
    g3,
    u0,
    u1,
    u2,
    u3,
    d0,
    d1,
    d2,
    d3,
    layer_out,
    back_middle,
    back_attn,
    back_attended,
    gain_grads,
    kept,
    sent,
    ffn_in,
    kept_a,
    kept_b,
    hidden,
    back_out,
    in_turned,
    out_turned,
    back_gate,
    back_up,
    wo,
    wg,
    wu,
    wd,
    grads,
    semaphores,
):
    output_copies = assemble((o0, o1, o2, o3), wo, place[0], semaphores, 0)
    gate_copies = assemble((g0, g1, g2, g3), wg, place[0], semaphores, 4)
    up_copies = assemble((u0, u1, u2, u3), wu, place[0], semaphores, 8)
    down_copies = assemble((d0, d1, d2, d3), wd, place[0], semaphores, 12)
    for copy in output_copies:
        copy.wait()
    g_attn, g_in, g_out = gains[1:2], gains[2:3], gains[3:4]
    ao = dot(attended[...], wo[...])
    r1 = inverse_rms(ao)
    mid = x_ref[...].astype(f32) + ao * r1 * g_attn
    r2 = inverse_rms(mid)
    ffn_in[...] = (mid * r2 * g_in).astype(bf16)
    for copy in gate_copies + up_copies:
        copy.wait()

    for j in range(8):
        cols = slice(256 * j, 256 * j + 256)
        u = dot(ffn_in[...], wg[:, cols])
        up = dot(ffn_in[...], wu[:, cols])
        root = 0.7978845608028654
        square = u * u
        t = jnp.tanh(u * (root + (root * 0.044715) * square))
        half = 0.5 + 0.5 * t
        act = u * half
        slope = half + act * (1.0 - t) * (root + (3 * 0.044715 * root) * square)
        hidden[:, cols] = (act * up).astype(bf16)
        kept_a[:, cols] = act
        kept_b[:, cols] = up * slope

    for copy in down_copies:
        copy.wait()
    fo = dot(hidden[...], wd[...])
    r3 = inverse_rms(fo)
    layer_out[...] = (mid + fo * r3 * g_out).astype(bf16)
    g = upstream[...].astype(f32)
    gain_grads[2:3] = jnp.sum(fo * r3 * g, axis=0, keepdims=True)
    bfo = norm_back(fo, r3, g_out, g)
    back_out[...] = bfo.astype(bf16)
    out_turned[...] = back_out[...].T
    in_turned[...] = ffn_in[...].T

    for j in range(8):
        cols = slice(256 * j, 256 * j + 256)
        bh = dot(back_out[...], wd[cols, :], rows_both)
        bu = (bh * kept_a[:, cols]).astype(bf16)
        bg = (bh * kept_b[:, cols]).astype(bf16)
        back_gate[:, cols] = bg
        back_up[:, cols] = bu

    for base, right in ((0, back_gate), (2560, back_up)):
        for j in range(2048 // 512):
            part = dot(in_turned[...], right[:, 512 * j : 512 * j + 512]).astype(bf16)
            for b in range(512 // 128):
                at = base + (512 // 128 * j + b) * 160
                for f in range(4):
                    grads[f, at : at + 160, :] = part[
                        160 * f : 160 * f + 160, 128 * b : 128 * b + 128
                    ]
    for f in range(4):
        part = dot(out_turned[...], hidden[:, 512 * f : 512 * f + 512]).astype(bf16)
        for b in range(4):
            at = 5120 + 640 * b
            grads[f, at : at + 640, :] = part[:, 128 * b : 128 * b + 128]

    outward = split_out(grads, kept, sent, place[0], semaphores, 16)
    e = dot(back_gate[...], wg[...], rows_both) + dot(back_up[...], wu[...], rows_both)
    gain_grads[1:2] = jnp.sum(mid * r2 * e, axis=0, keepdims=True)
    bm = g + norm_back(mid, r2, g_in, e)
    back_middle[...] = bm
    gain_grads[0:1] = jnp.sum(ao * r1 * bm, axis=0, keepdims=True)
    bao = norm_back(ao, r1, g_attn, bm).astype(bf16)
    back_attn[...] = bao
    back_attended[...] = dot(bao, wo[...], rows_both).astype(bf16)
    for copy in outward:
        copy.wait()


def middle_part(place, x, attended, upstream, gains, shares):
    return pl.pallas_call(
        middle_kernel,
        name="middle_part",
        in_specs=[pl.BlockSpec(memory_space=pltpu.SMEM)]
        + [whole()] * 4
        + [pl.BlockSpec(memory_space=pltpu.HBM)] * 16,
        out_specs=[whole()] * 5 + [pl.BlockSpec(memory_space=pltpu.HBM)] * 2,
        out_shape=[
            spec(512, 640, bf16),
            spec(512, 640, f32),
            spec(512, 640, bf16),
            spec(512, 1024, bf16),
            spec(8, 640, f32),
            spec(2, 7680, 128, bf16),
            spec(2, 7680, 128, bf16),
        ],
        scratch_shapes=[
            pltpu.VMEM((512, 640), bf16),
            pltpu.VMEM((512, 2048), f32),
            pltpu.VMEM((512, 2048), f32),
            pltpu.VMEM((512, 2048), bf16),
            pltpu.VMEM((512, 640), bf16),
            pltpu.VMEM((640, 512), bf16),
            pltpu.VMEM((640, 512), bf16),
            pltpu.VMEM((512, 2048), bf16),
            pltpu.VMEM((512, 2048), bf16),
            pltpu.VMEM((1024, 640), bf16),
            pltpu.VMEM((640, 2048), bf16),
            pltpu.VMEM((640, 2048), bf16),
            pltpu.VMEM((2048, 640), bf16),
            pltpu.VMEM((4, 7680, 128), bf16),
            pltpu.SemaphoreType.DMA((20,)),
        ],
        compiler_params=params(44),
        cost_estimate=cost(13_400_000_000, 23_000_000, 1_000_000),
    )(place, x, attended, upstream, gains, *shares)


def attend_back_kernel(
    q,
    k,
    v,
    offsets,
    level,
    back_attended,
    q_proj,
    k_proj,
    head_gains,
    cosine,
    sine,
    place,
    kv0,
    kv1,
    kv2,
    kv3,
    back_q,
    back_kv,
    gain_grads,
    back_halo,
    sum_k,
    sum_v,
    wkv,
    semaphores,
):
    t = pl.program_id(0)

    @pl.when(t == 0)
    def _():
        for copy in assemble((kv0, kv1, kv2, kv3), wkv, place[0], semaphores, 0):
            copy.wait()
        sum_k[...] = jnp.zeros_like(sum_k)
        sum_v[...] = jnp.zeros_like(sum_v)
        gain_grads[...] = jnp.zeros_like(gain_grads)

    near = pl.ds(pl.multiple_of(t * 256, 256), 768)
    mine = pl.ds(pl.multiple_of(t * 256 + 512, 256), 256)
    keys, values = k[near, :], v[near, :]
    visible = visible_keys(offsets[...])
    c, s = cosine[mine, :], sine[mine, :]
    for h in range(4):
        cols = slice(256 * h, 256 * h + 256)
        qh, bah = q[:, cols], back_attended[:, cols]
        scores = jnp.where(visible, dot(qh, keys, rows_both) * 0.0625, masked_value)
        probs = jnp.exp(scores - level[h])
        bp = dot(bah, values, rows_both)
        inner = jnp.sum(probs * bp, axis=-1, keepdims=True)
        bs = (probs * (bp - inner)).astype(bf16)
        sum_k[near, :] += dot(bs, qh, cols_both)
        sum_v[near, :] += dot(probs.astype(bf16), bah, cols_both)
        e = turn_back(dot(bs, keys) * 0.0625, c, s)
        qp = q_proj[:, cols]
        r = inverse_rms(qp)
        gain_grads[0:1] += jnp.sum(qp * r * e, axis=0, keepdims=True)
        back_q[:, cols] = norm_back(qp, r, head_gains[4:5], e).astype(bf16)

    @pl.when(t == 1)
    def _():
        e = turn_back(sum_k[...] * 0.0625, cosine[...], sine[...])
        kp = k_proj[...]
        r = inverse_rms(kp)
        gain_grads[1:2] = jnp.sum(kp * r * e, axis=0, keepdims=True)
        back_kv[:, :256] = norm_back(kp, r, head_gains[5:6], e).astype(bf16)
        back_kv[:, 256:] = sum_v[...].astype(bf16)
        back_halo[...] = dot(back_kv[:512, :], wkv[...], rows_both).astype(bf16)


def attend_back(
    q, k, v, offsets, level, back_attended, q_proj, k_proj, head_gains, cosine, sine, place, shares
):
    row = lambda i: (i, 0)
    fixed = lambda i: (0, 0)
    return pl.pallas_call(
        attend_back_kernel,
        name="attend_back",
        grid=(2,),
        in_specs=[
            pl.BlockSpec((256, 1024), row),
            pl.BlockSpec((1024, 256), fixed),
            pl.BlockSpec((1024, 256), fixed),
            pl.BlockSpec((256, 1), row),
            pl.BlockSpec((4, 256, 1), lambda i: (0, i, 0)),
            pl.BlockSpec((256, 1024), row),
            pl.BlockSpec((256, 1024), row),
            pl.BlockSpec((1024, 256), fixed),
            pl.BlockSpec((8, 256), fixed),
            pl.BlockSpec((1024, 128), fixed),
            pl.BlockSpec((1024, 128), fixed),
            pl.BlockSpec(memory_space=pltpu.SMEM),
        ]
        + [pl.BlockSpec(memory_space=pltpu.HBM)] * 4,
        out_specs=[
            pl.BlockSpec((256, 1024), row),
            pl.BlockSpec((1024, 512), fixed),
            pl.BlockSpec((8, 256), fixed),
            pl.BlockSpec((512, 640), fixed),
        ],
        out_shape=[
            spec(512, 1024, bf16),
            spec(1024, 512, bf16),
            spec(8, 256, f32),
            spec(512, 640, bf16),
        ],
        scratch_shapes=[
            pltpu.VMEM((1024, 256), f32),
            pltpu.VMEM((1024, 256), f32),
            pltpu.VMEM((640, 512), bf16),
            pltpu.SemaphoreType.DMA((4,)),
        ],
        compiler_params=params(16),
        cost_estimate=cost(4_300_000_000, 10_000_000, 2_000_000),
    )(
        q, k, v, offsets, level, back_attended, q_proj, k_proj, head_gains, cosine, sine, place, *shares
    )


def weights_kernel(
    place,
    normed,
    back_q,
    back_kv,
    attended,
    back_attn,
    halo,
    own,
    gain_mid,
    gain_head,
    q0,
    q1,
    q2,
    q3,
    kv0,
    kv1,
    kv2,
    kv3,
    back_own,
    kept,
    sent,
    wq,
    wkv,
    grads,
    semaphores,
):
    copies = assemble((kv0, kv1, kv2, kv3), wkv, place[0], semaphores, 0)
    copies += assemble((q0, q1, q2, q3), wq, place[0], semaphores, 4)
    turned = normed[...].astype(f32).T.astype(bf16)
    bq, bkv = back_q[...], back_kv[...]
    part = dot(turned[:, 512:], bq).astype(bf16)
    for b in range(8):
        for f in range(4):
            grads[f, 160 * b : 160 * b + 160, :] = part[
                160 * f : 160 * f + 160, 128 * b : 128 * b + 128
            ]
    part = dot(turned, bkv).astype(bf16)
    for b in range(4):
        for f in range(4):
            grads[f, 1280 + 160 * b : 1440 + 160 * b, :] = part[
                160 * f : 160 * f + 160, 128 * b : 128 * b + 128
            ]
    turned = back_attn[...].astype(f32).T.astype(bf16)
    part = dot(turned, attended[...]).astype(bf16)
    for f in range(4):
        for b in range(2):
            grads[f, 1920 + 640 * b : 2560 + 640 * b, :] = part[
                :, 256 * f + 128 * b : 256 * f + 128 * b + 128
            ]
    for copy in copies:
        copy.wait()
    e = dot(bkv[:512], wkv[...], rows_both)
    x = halo[...].astype(f32)
    grad = jnp.sum(x * inverse_rms(x) * e, axis=0, keepdims=True)
    e = dot(bkv[512:], wkv[...], rows_both) + dot(bq, wq[...], rows_both)
    back_own[...] = e
    x = own[...].astype(f32)
    grad = grad + jnp.sum(x * inverse_rms(x) * e, axis=0, keepdims=True)
    each = jnp.concatenate([grad, gain_mid[0:3]], axis=0)
    heads = gain_head[0:2]
    for f in range(4):
        share = each[:, 160 * f : 160 * f + 160]
        rest = jnp.concatenate([share[:, 128:], jnp.zeros((4, 96), f32)], axis=1)
        ends = jnp.concatenate([heads[:, 64 * f : 64 * f + 64], jnp.zeros((2, 64), f32)], axis=1)
        tile = jnp.concatenate([share[:, :128], rest, ends, jnp.zeros((6, 128), f32)], axis=0)
        grads[f, 3200:3216, :] = tile.astype(bf16)
        grads[f, 3216:, :] = jnp.zeros((368, 128), bf16)
    for copy in split_out(grads, kept, sent, place[0], semaphores, 8):
        copy.wait()


def weights_part(
    place, normed, back_q, back_kv, attended, back_attn, halo, own, gain_mid, gain_head, shares
):
    return pl.pallas_call(
        weights_kernel,
        name="weights_part",
        in_specs=[pl.BlockSpec(memory_space=pltpu.SMEM)]
        + [whole()] * 9
        + [pl.BlockSpec(memory_space=pltpu.HBM)] * 8,
        out_specs=[whole()] + [pl.BlockSpec(memory_space=pltpu.HBM)] * 2,
        out_shape=[
            spec(512, 640, f32),
            spec(2, 3584, 128, bf16),
            spec(2, 3584, 128, bf16),
        ],
        scratch_shapes=[
            pltpu.VMEM((640, 1024), bf16),
            pltpu.VMEM((640, 512), bf16),
            pltpu.VMEM((4, 3584, 128), bf16),
            pltpu.SemaphoreType.DMA((12,)),
        ],
        compiler_params=params(24),
        cost_estimate=cost(3_400_000_000, 14_000_000),
    )(place, normed, back_q, back_kv, attended, back_attn, halo, own, gain_mid, gain_head, *shares)


def finish_kernel(own, back_own, returned, back_middle, gains, grad_in):
    x = own[...].astype(f32)
    e = back_own[...] + returned[...].astype(f32)
    grad_in[...] = (back_middle[...] + norm_back(x, inverse_rms(x), gains[0:1], e)).astype(bf16)


def finish(own, back_own, returned, back_middle, gains):
    row = lambda i: (i, 0)
    return pl.pallas_call(
        finish_kernel,
        name="finish",
        grid=(4,),
        in_specs=[pl.BlockSpec((128, 640), row)] * 4 + [pl.BlockSpec((8, 640), lambda i: (0, 0))],
        out_specs=pl.BlockSpec((128, 640), row),
        out_shape=spec(512, 640, bf16),
        compiler_params=params(10),
        cost_estimate=cost(4_000_000, 5_000_000),
    )(own, back_own, returned, back_middle, gains)


def rope_tables(offsets):
    powers = jnp.arange(128, dtype=f32) * (2.0 / 256)
    row = jnp.arange(512, dtype=jnp.int32)
    every = jnp.concatenate([offsets[0] - 512 + row, offsets])
    angles = every.astype(f32)[:, None] * (rope_base ** (-powers))[None, :]
    return jnp.cos(angles), jnp.sin(angles)


def unpack_kernel(spot, a0, a1, a2, a3, b0, b1, b2, b3, *rest):
    outs, gains, held, (ffn, attn, semaphores) = rest[:7], rest[7], rest[8:15], rest[15:]
    q, k, v, out, gate, up, down = held
    x, y = spot[0], spot[1]
    copies = []
    for half, pieces in enumerate(((a0, a1, a2, a3), (b0, b1, b2, b3))):
        for i in range(4):
            for j in range(4):
                first, second = (x, y) if half == 0 else (y, x)
                block = 16 * half + lax.rem(first - i + 4, 4) * 4 + lax.rem(second - j + 4, 4)
                n = (half * 4 + i) * 4 + j
                for m, (into, start, rows) in enumerate(((ffn, 0, 240), (attn, 240, 112))):
                    copies.append(
                        pltpu.make_async_copy(
                            pieces[i].at[j, pl.ds(start, rows), :],
                            into.at[pl.ds(pl.multiple_of(block * rows, 16), rows), :],
                            semaphores.at[2 * n + m],
                        )
                    )
    for copy in copies:
        copy.start()
    for copy in copies:
        copy.wait()
    outward = []

    def leave(n):
        copy = pltpu.make_async_copy(held[n], outs[n], semaphores.at[64 + n])
        copy.start()
        outward.append(copy)

    for n, into, flat, first, count in (
        (4, gate, ffn, 0, 16),
        (5, up, ffn, 2560, 16),
        (0, q, attn, 0, 8),
        (1, k, attn, 1280, 2),
        (2, v, attn, 1600, 2),
    ):
        for b in range(count):
            at = first + 160 * b
            into[:, 128 * b : 128 * b + 128] = flat[at : at + 160, :].astype(f32)
        leave(n)
    for n, into, flat, first, count in ((6, down, ffn, 5120, 4), (3, out, attn, 1920, 2)):
        for b in range(count):
            at = first + 640 * b
            into[128 * b : 128 * b + 128, :] = flat[at : at + 640, :].astype(f32).T
        leave(n)
    gains[...] = attn[3200:3216, :].astype(f32)
    for copy in outward:
        copy.wait()


def unpack(spot, pieces):
    shapes = [(160, 1024), (160, 256), (160, 256), (256, 640), (160, 2048), (160, 2048), (512, 640)]
    return pl.pallas_call(
        unpack_kernel,
        name="unpack",
        in_specs=[pl.BlockSpec(memory_space=pltpu.SMEM)] + [pl.BlockSpec(memory_space=pltpu.HBM)] * 8,
        out_specs=[pl.BlockSpec(memory_space=pltpu.HBM)] * 7 + [whole()],
        out_shape=[spec(*shape, f32) for shape in shapes] + [spec(16, 128, f32)],
        scratch_shapes=[pltpu.VMEM(shape, f32) for shape in shapes]
        + [
            pltpu.VMEM((7680, 128), bf16),
            pltpu.VMEM((3584, 128), bf16),
            pltpu.SemaphoreType.DMA((71,)),
        ],
        compiler_params=params(14),
        cost_estimate=cost(4_000_000, 11_000_000),
    )(spot, *pieces)


def sum_of(parts):
    whole = parts[0].astype(f32)
    for part in parts[1:]:
        whole = whole + part.astype(f32)
    return whole.astype(bf16)


def turn_around(position, d):
    return lax.rem(position + d, 4)


def first_kernel(spot, kept_ffn, got_ffn, kept_attn, got_attn, *outs):
    for half in range(2):
        for i, d in enumerate((0, 1, 3, 2)):
            at = turn_around(spot[half], d)
            out = outs[4 * half + i]
            for z in range(2):
                for j in range(4):
                    out[z, j, :240] = sum_of([r[z, half, at, j] for r in (kept_ffn, got_ffn)])
                    out[z, j, 240:] = sum_of([r[z, half, at, j] for r in (kept_attn, got_attn)])


def first_sums(spot, kept_ffn, got_ffn, kept_attn, got_attn):
    ins = [p.reshape(2, 2, 4, 4, p.shape[1] // 32, 128) for p in (kept_ffn, got_ffn, kept_attn, got_attn)]
    return pl.pallas_call(
        first_kernel,
        name="first_sums",
        in_specs=[pl.BlockSpec(memory_space=pltpu.SMEM)] + [whole()] * 4,
        out_specs=[whole()] * 8,
        out_shape=[spec(2, 4, 352, 128, bf16)] * 8,
        compiler_params=params(24),
        cost_estimate=cost(3_000_000, 17_000_000),
    )(spot, *ins)


def second_kernel(spot, *refs):
    ins, outs = refs[:8], refs[8:]
    for half in range(2):
        parts = ins[4 * half : 4 * half + 4]
        for i, d in enumerate((0, 1, 3, 2)):
            at = turn_around(spot[1 - half], d)
            for z in range(2):
                outs[4 * half + i][z] = sum_of([r[z, at] for r in parts])


def second_sums(spot, parts):
    return pl.pallas_call(
        second_kernel,
        name="second_sums",
        in_specs=[pl.BlockSpec(memory_space=pltpu.SMEM)] + [whole()] * 8,
        out_specs=[whole()] * 8,
        out_shape=[spec(2, 352, 128, bf16)] * 8,
        compiler_params=params(12),
        cost_estimate=cost(1_000_000, 7_200_000),
    )(spot, *parts)


def third_kernel(place, *refs):
    ins, (mine, other) = refs[:8], refs[8:]
    z = lax.div(place[0], 2)
    for half in range(2):
        parts = ins[4 * half : 4 * half + 4]
        mine[half] = sum_of([r[z] for r in parts])
        other[half] = sum_of([r[1 - z] for r in parts])


def third_sums(place, parts):
    return pl.pallas_call(
        third_kernel,
        name="third_sums",
        in_specs=[pl.BlockSpec(memory_space=pltpu.SMEM)] + [whole()] * 8,
        out_specs=[whole()] * 2,
        out_shape=[spec(2, 352, 128, bf16)] * 2,
        compiler_params=params(10),
        cost_estimate=cost(1_000_000, 1_800_000),
    )(place, *parts)


def fourth_kernel(p0, p1, p2, p3, a, b):
    for half, out in enumerate((a, b)):
        out[...] = sum_of([p0[half], p1[half], p2[half], p3[half]])


def fourth_sums(parts):
    return pl.pallas_call(
        fourth_kernel,
        name="fourth_sums",
        in_specs=[whole()] * 4,
        out_specs=[whole()] * 2,
        out_shape=[spec(352, 128, bf16)] * 2,
        compiler_params=params(10),
        cost_estimate=cost(1_000_000, 900_000),
    )(*parts)


def seq_index(z, x, y):
    return (z % 2 * 4 + x % 4) * 4 + y % 4


def along_xy(dx, dy):
    return [
        (seq_index(z, x, y), seq_index(z, x + dx, y + dy))
        for z in range(2)
        for x in range(4)
        for y in range(4)
    ]


def along_z(step):
    pairs = []
    for s in range(32):
        for f in range(4):
            z = s // 16 * 2 + f // 2
            t = step(z)
            pairs.append((s * 4 + f, (t // 2 * 16 + s % 16) * 4 + t % 2 * 2 + f % 2))
    return pairs


def swap_core(value):
    return lax.ppermute(value, "fsdp", [(0, 1), (1, 0), (2, 3), (3, 2)])


def swap_near(value):
    return lax.ppermute(value, "fsdp", [(0, 2), (1, 3), (2, 0), (3, 1)])


def swap_across(value):
    return lax.ppermute(value, "fsdp", [(0, 3), (1, 2), (2, 1), (3, 0)])


def swap_far(value):
    return lax.ppermute(value, ("seq", "fsdp"), along_z(lambda z: 3 - z))


def swap_hi(value):
    return lax.ppermute(value, "seq", [(s, (s + 16) % 32) for s in range(32)])


def move_x(value, d):
    return lax.ppermute(value, "seq", along_xy(d, 0))


def move_y(value, d):
    return lax.ppermute(value, "seq", along_xy(0, d))


def shifted(value, steps):
    first, last = (max(0, -steps), min(32, 32 - steps))
    return lax.ppermute(value, "seq", [(source, source + steps) for source in range(first, last)])


steps = (1, 3, 2)


def move_first(parts):
    return (
        [parts[0]]
        + [move_x(p, d) for p, d in zip(parts[1:4], steps)]
        + [parts[4]]
        + [move_y(p, d) for p, d in zip(parts[5:8], steps)]
    )


def move_second(parts):
    return (
        [parts[0]]
        + [move_y(p, d) for p, d in zip(parts[1:4], steps)]
        + [parts[4]]
        + [move_x(p, d) for p, d in zip(parts[5:8], steps)]
    )


def together(*groups):
    leaves, tree = jax.tree.flatten(groups)
    return jax.tree.unflatten(tree, lax.optimization_barrier(tuple(leaves)))


def body(
    hidden_in,
    cotangent,
    positions,
    query_weight,
    key_weight,
    value_weight,
    output_weight,
    gate_weight,
    up_weight,
    down_weight,
    norm_in,
    norm_attn,
    norm_ffn_in,
    norm_ffn_out,
    norm_query,
    norm_key,
):
    s = lax.axis_index("seq")
    f = lax.axis_index("fsdp")
    x, y, z_lo, core = s // 4 % 4, s % 4, f // 2, f % 2
    place = f.astype(jnp.int32).reshape(1)
    spot = jnp.stack([x, y]).astype(jnp.int32)
    own = hidden_in[0]
    upstream = cotangent[0]
    offsets = positions[0]

    q_partner = swap_near(query_weight)
    wg_partner, wu_partner = swap_near(gate_weight), swap_far(up_weight)
    kv = pack(
        [norm_in, norm_attn, norm_ffn_in, norm_ffn_out, norm_query, norm_key],
        key_weight,
        value_weight,
    )
    kv_partner = swap_far(kv)
    halo = shifted(own, 1)
    q_shares = (query_weight, swap_core(query_weight), q_partner, swap_core(q_partner))
    kv_shares = (kv, swap_core(kv), kv_partner, swap_core(kv_partner))
    wg_diagonal, wu_diagonal = swap_core(wg_partner), swap_core(wu_partner)
    q_shares, kv_shares, halo, wg_diagonal, wu_diagonal = together(
        q_shares, kv_shares, halo, wg_diagonal, wu_diagonal
    )
    wo, wd, wg_partner, wu_partner = together(
        output_weight, down_weight, wg_partner, wu_partner
    )
    wo_partner, wd_partner = swap_near(wo), swap_far(wd)
    tiles = [share[160:168] for share in kv_shares]
    tiles = [
        jnp.where(
            j // 2 == z_lo,
            jnp.where(j % 2 == core, tiles[0], tiles[1]),
            jnp.where(j % 2 == core, tiles[2], tiles[3]),
        )
        for j in range(4)
    ]
    gains = jnp.concatenate([t[:, :160] for t in tiles], axis=1).astype(f32)
    head_gains = jnp.concatenate([t[:, :64] for t in tiles], axis=1).astype(f32)

    cosine, sine = rope_tables(offsets)
    column = offsets[:, None]
    normed, q, k, v, q_proj, k_proj = project(
        place, halo, own, gains, head_gains, q_shares, kv_shares, cosine, sine
    )
    attended, level = attend(q, k, v, column)
    attended, wo, wg, wu, wd = together(attended, wo, gate_weight, up_weight, wd)
    wg_shares = [wg, swap_core(wg), wg_partner, wg_diagonal]
    wu_shares = [wu, swap_core(wu), wu_partner, wu_diagonal]
    attended, wo_partner = together(attended, wo_partner)
    wo_shares = [wo, swap_core(wo), wo_partner, swap_core(wo_partner)]
    attended, wd_partner = together(attended, wd_partner)
    wd_shares = [wd, swap_core(wd), wd_partner, swap_core(wd_partner)]
    layer_out, back_middle, back_attn, back_attended, gain_mid, kept, sent = middle_part(
        place, own, attended, upstream, gains, wo_shares + wg_shares + wu_shares + wd_shares
    )
    got = swap_core(sent)
    back_q, back_kv, gain_head, back_halo = attend_back(
        q,
        k,
        v,
        column,
        level,
        back_attended,
        q_proj,
        k_proj,
        head_gains,
        cosine,
        sine,
        place,
        kv_shares,
    )
    back_own, kept_attn, sent = weights_part(
        place,
        normed,
        back_q,
        back_kv,
        attended,
        back_attn,
        halo,
        own,
        gain_mid,
        gain_head,
        q_shares + kv_shares,
    )
    got_attn = swap_core(sent)
    first = move_first(first_sums(spot, kept, got, kept_attn, got_attn))
    mine, other = third_sums(place, move_second(second_sums(spot, first)))
    mine, other, back_halo = together(mine, other, back_halo)
    returned = shifted(back_halo, -1)
    a, b = fourth_sums([mine, swap_near(other), swap_far(other), swap_hi(mine)])
    a, b, returned = together(a, b, returned)
    a = jnp.stack([a] + [move_y(a, d) for d in (1, 2, 3)])
    b = jnp.stack([b] + [move_x(b, d) for d in (1, 2, 3)])
    a, b = together(a, b)
    pieces = [a] + [move_x(a, d) for d in (1, 2, 3)] + [b] + [move_y(b, d) for d in (1, 2, 3)]
    grad_q, grad_k, grad_v, grad_o, grad_g, grad_u, grad_d, tile = unpack(spot, pieces)
    grad_in = finish(own, back_own, returned, back_middle, gains)
    wide = jnp.concatenate([tile[0:4], tile[4:8, :32]], axis=1)
    return (
        layer_out[None],
        grad_in[None],
        grad_q,
        grad_k,
        grad_v,
        grad_o,
        grad_g,
        grad_u,
        grad_d,
        wide[0],
        wide[1],
        wide[2],
        wide[3],
        tile[8, :64],
        tile[9, :64],
    )


def solution(mesh):
    three = P("fsdp", "seq", None)
    two = P("fsdp", None)
    one = P("fsdp")
    return jax.shard_map(
        body,
        mesh=mesh,
        in_specs=(three, three, P("fsdp", "seq")) + (two,) * 7 + (one,) * 6,
        out_specs=(three, three) + (two,) * 7 + (one,) * 6,
        check_vma=False,
    )
```

```python
import jax
import jax.numpy as jnp
from jax import lax
from jax.experimental import pallas as pl
from jax.experimental.pallas import tpu as pltpu
from jax.sharding import PartitionSpec as P

WINDOW = 512
epsilon = 1e-06
rope_base = 10000.0
masked_value = -1e30
bf16 = jnp.bfloat16
f32 = jnp.float32

rows_out = ((1,), (0,))
rows_both = ((1,), (1,))
cols_both = ((0,), (0,))


def dot(a, b, dims=rows_out):
    return lax.dot_general(a, b, (dims, ((), ())), preferred_element_type=f32)


def spec(*shape):
    return jax.ShapeDtypeStruct(shape[:-1], shape[-1])


def whole():
    return pl.BlockSpec(memory_space=pltpu.VMEM)


def params(mib):
    return pltpu.CompilerParams(vmem_limit_bytes=mib * 1024 * 1024)


def cost(flops, moved, exps=0):
    return pl.CostEstimate(flops=flops, bytes_accessed=moved, transcendentals=exps)


def inverse_rms(v):
    return lax.rsqrt(jnp.mean(v * v, axis=-1, keepdims=True) + epsilon)


def norm_back(v, r, gain, e):
    scaled = gain * e
    return r * scaled - v * (r * r * r * jnp.mean(v * scaled, axis=-1, keepdims=True))


def turn(v, cosine, sine):
    a, b = v[:, :128], v[:, 128:]
    return jnp.concatenate([a * cosine - b * sine, b * cosine + a * sine], axis=1)


def turn_back(v, cosine, sine):
    a, b = v[:, :128], v[:, 128:]
    return jnp.concatenate([a * cosine + b * sine, b * cosine - a * sine], axis=1)


def assemble(pieces, into, place, semaphores, first, column=0):
    rows = into.shape[0] // 4
    copies = []
    for r in range(4):
        at = pl.ds(pl.multiple_of((place ^ r) * rows, rows), rows)
        copies.append(
            pltpu.make_async_copy(
                pieces[r].at[pl.ds(0, rows), pl.ds(column, into.shape[1])],
                into.at[at, :],
                semaphores.at[first + r],
            )
        )
    for copy in copies:
        copy.start()
    return copies


def split_out(grads, kept, sent, place, semaphores, first):
    core = lax.rem(place, 2)
    copies = []
    for z in range(2):
        copies.append(
            pltpu.make_async_copy(
                grads.at[2 * z + 1 - core], sent.at[z], semaphores.at[first + 2 * z]
            )
        )
        copies.append(
            pltpu.make_async_copy(
                grads.at[2 * z + core], kept.at[z], semaphores.at[first + 2 * z + 1]
            )
        )
    for copy in copies:
        copy.start()
    return copies


def pack_kernel(g0, g1, g2, g3, g4, g5, k, v, up, far, *rest):
    held, semaphores = rest[:6], rest[6]
    copies = [
        pltpu.make_async_copy(source, into, semaphores.at[i])
        for i, (source, into) in enumerate(zip((g0, g1, g2, g3, g4, g5), held))
    ]
    for copy in copies:
        copy.start()
    far[:160, :256] = k[...]
    far[:160, 256:512] = v[...]
    far[:160, 512:] = up[...]
    tile = []
    for copy in copies:
        copy.wait()
    for ref in held:
        n = ref.shape[0]
        row = ref[...].astype(f32).reshape(1, n)
        tile.append(jnp.concatenate([row, jnp.zeros((1, 512 - n), f32)], axis=1))
    tile.append(jnp.zeros((10, 512), f32))
    far[160:, :512] = jnp.concatenate(tile, axis=0).astype(bf16)
    far[160:, 512:] = jnp.zeros((16, 2048), bf16)


def pack(rows, key_weight, value_weight, up_weight):
    return pl.pallas_call(
        pack_kernel,
        name="pack",
        in_specs=[pl.BlockSpec(memory_space=pltpu.HBM)] * 6 + [whole()] * 3,
        out_specs=whole(),
        out_shape=spec(176, 2560, bf16),
        scratch_shapes=[pltpu.VMEM(row.shape, bf16) for row in rows]
        + [pltpu.SemaphoreType.DMA((6,))],
        compiler_params=params(6),
        cost_estimate=cost(100_000, 1_700_000),
    )(*rows, key_weight, value_weight, up_weight)


def project_kernel(
    place,
    halo,
    own,
    gains,
    head_gains,
    q0,
    q1,
    q2,
    q3,
    kv0,
    kv1,
    kv2,
    kv3,
    cosine,
    sine,
    normed,
    q,
    k,
    v,
    q_proj,
    k_proj,
    wq,
    wkv,
    semaphores,
):
    i = pl.program_id(0)

    @pl.when(i == 0)
    def _():
        copies = assemble((kv0, kv1, kv2, kv3), wkv, place[0], semaphores, 0)
        copies += assemble((q0, q1, q2, q3), wq, place[0], semaphores, 4)
        for copy in copies:
            copy.wait()

    x = jnp.where(i < 2, halo[...], own[...]).astype(f32)
    n = (x * inverse_rms(x) * gains[0:1]).astype(bf16)
    normed[...] = n
    c, s = cosine[...], sine[...]
    kv = dot(n, wkv[...])
    kp = kv[:, :256]
    k_proj[...] = kp
    v[...] = kv[:, 256:].astype(bf16)
    k[...] = turn(kp * inverse_rms(kp) * head_gains[5:6], c, s).astype(bf16)

    @pl.when(i >= 2)
    def _():
        for h in range(4):
            cols = slice(256 * h, 256 * h + 256)
            qp = dot(n, wq[:, cols])
            q_proj[:, cols] = qp
            q[:, cols] = turn(qp * inverse_rms(qp) * head_gains[4:5], c, s).astype(bf16)


def project(place, halo, own, gains, head_gains, q_shares, kv_shares, cosine, sine):
    late = lambda i: (jnp.maximum(i - 2, 0), 0)
    row = lambda i: (i, 0)
    fixed = lambda i: (0, 0)
    return pl.pallas_call(
        project_kernel,
        name="project",
        grid=(4,),
        in_specs=[
            pl.BlockSpec(memory_space=pltpu.SMEM),
            pl.BlockSpec((256, 640), lambda i: (jnp.minimum(i, 1), 0)),
            pl.BlockSpec((256, 640), late),
            pl.BlockSpec((8, 640), fixed),
            pl.BlockSpec((8, 256), fixed),
        ]
        + [pl.BlockSpec(memory_space=pltpu.HBM)] * 8
        + [pl.BlockSpec((256, 128), row)] * 2,
        out_specs=[
            pl.BlockSpec((256, 640), row),
            pl.BlockSpec((256, 1024), late),
            pl.BlockSpec((256, 256), row),
            pl.BlockSpec((256, 256), row),
            pl.BlockSpec((256, 1024), late),
            pl.BlockSpec((256, 256), row),
        ],
        out_shape=[
            spec(1024, 640, bf16),
            spec(512, 1024, bf16),
            spec(1024, 256, bf16),
            spec(1024, 256, bf16),
            spec(512, 1024, f32),
            spec(1024, 256, f32),
        ],
        scratch_shapes=[
            pltpu.VMEM((640, 1024), bf16),
            pltpu.VMEM((640, 512), bf16),
            pltpu.SemaphoreType.DMA((8,)),
        ],
        compiler_params=params(14),
        cost_estimate=cost(1_350_000_000, 9_000_000),
    )(place, halo, own, gains, head_gains, *q_shares, *kv_shares, cosine, sine)


def visible_keys(offsets):
    distance = (
        lax.broadcasted_iota(jnp.int32, (256, 768), 0)
        + 512
        - lax.broadcasted_iota(jnp.int32, (256, 768), 1)
    )
    return (distance >= 0) & (distance < WINDOW) & (distance <= offsets)


def attend_kernel(q, k, v, offsets, attended, level):
    t = pl.program_id(0)
    near = pl.ds(pl.multiple_of(t * 256, 256), 768)
    keys, values = k[near, :], v[near, :]
    visible = visible_keys(offsets[...])
    for h in range(4):
        cols = slice(256 * h, 256 * h + 256)
        scores = jnp.where(visible, dot(q[:, cols], keys, rows_both) * 0.0625, masked_value)
        top = jnp.max(scores, axis=-1, keepdims=True)
        e = jnp.exp(scores - top)
        total = jnp.sum(e, axis=-1, keepdims=True)
        level[h] = top + jnp.log(total)
        probs = (e * (1.0 / total)).astype(bf16)
        attended[:, cols] = dot(probs, values).astype(bf16)


def attend(q, k, v, offsets):
    row = lambda i: (i, 0)
    fixed = lambda i: (0, 0)
    return pl.pallas_call(
        attend_kernel,
        name="attend",
        grid=(2,),
        in_specs=[
            pl.BlockSpec((256, 1024), row),
            pl.BlockSpec((1024, 256), fixed),
            pl.BlockSpec((1024, 256), fixed),
            pl.BlockSpec((256, 1), row),
        ],
        out_specs=[
            pl.BlockSpec((256, 1024), row),
            pl.BlockSpec((4, 256, 1), lambda i: (0, i, 0)),
        ],
        out_shape=[spec(512, 1024, bf16), spec(4, 512, 1, f32)],
        compiler_params=params(10),
        cost_estimate=cost(1_700_000_000, 4_000_000, 2_000_000),
    )(q, k, v, offsets)


def middle_kernel(
    place,
    x_ref,
    attended,
    upstream,
    gains,
    o0,
    o1,
    o2,
    o3,
    g0,
    g1,
    g2,
    g3,
    u0,
    u1,
    u2,
    u3,
    d0,
    d1,
    d2,
    d3,
    layer_out,
    back_middle,
    back_attn,
    back_attended,
    gain_grads,
    kept,
    sent,
    ffn_in,
    kept_a,
    kept_b,
    hidden,
    back_out,
    in_turned,
    out_turned,
    back_gate,
    back_up,
    wo,
    wg,
    wu,
    wd,
    grads,
    semaphores,
):
    output_copies = assemble((o0, o1, o2, o3), wo, place[0], semaphores, 0)
    gate_copies = assemble((g0, g1, g2, g3), wg, place[0], semaphores, 4, 1024)
    up_copies = assemble((u0, u1, u2, u3), wu, place[0], semaphores, 8, 512)
    down_copies = assemble((d0, d1, d2, d3), wd, place[0], semaphores, 12)
    for copy in output_copies:
        copy.wait()
    g_attn, g_in, g_out = gains[1:2], gains[2:3], gains[3:4]
    ao = dot(attended[...], wo[...])
    r1 = inverse_rms(ao)
    mid = x_ref[...].astype(f32) + ao * r1 * g_attn
    r2 = inverse_rms(mid)
    ffn_in[...] = (mid * r2 * g_in).astype(bf16)
    for copy in gate_copies + up_copies:
        copy.wait()

    for j in range(8):
        cols = slice(256 * j, 256 * j + 256)
        u = dot(ffn_in[...], wg[:, cols])
        up = dot(ffn_in[...], wu[:, cols])
        root = 0.7978845608028654
        square = u * u
        t = jnp.tanh(u * (root + (root * 0.044715) * square))
        half = 0.5 + 0.5 * t
        act = u * half
        slope = half + act * (1.0 - t) * (root + (3 * 0.044715 * root) * square)
        hidden[:, cols] = (act * up).astype(bf16)
        kept_a[:, cols] = act
        kept_b[:, cols] = up * slope

    for copy in down_copies:
        copy.wait()
    fo = dot(hidden[...], wd[...])
    r3 = inverse_rms(fo)
    layer_out[...] = (mid + fo * r3 * g_out).astype(bf16)
    g = upstream[...].astype(f32)
    gain_grads[2:3] = jnp.sum(fo * r3 * g, axis=0, keepdims=True)
    bfo = norm_back(fo, r3, g_out, g)
    back_out[...] = bfo.astype(bf16)
    out_turned[...] = back_out[...].T
    in_turned[...] = ffn_in[...].T

    for j in range(8):
        cols = slice(256 * j, 256 * j + 256)
        bh = dot(back_out[...], wd[cols, :], rows_both)
        bu = (bh * kept_a[:, cols]).astype(bf16)
        bg = (bh * kept_b[:, cols]).astype(bf16)
        back_gate[:, cols] = bg
        back_up[:, cols] = bu

    for base, right in ((0, back_gate), (2560, back_up)):
        for j in range(2048 // 512):
            part = dot(in_turned[...], right[:, 512 * j : 512 * j + 512]).astype(bf16)
            for b in range(512 // 128):
                at = base + (512 // 128 * j + b) * 160
                for f in range(4):
                    grads[f, at : at + 160, :] = part[
                        160 * f : 160 * f + 160, 128 * b : 128 * b + 128
                    ]
    for f in range(4):
        part = dot(out_turned[...], hidden[:, 512 * f : 512 * f + 512]).astype(bf16)
        for b in range(4):
            at = 5120 + 640 * b
            grads[f, at : at + 640, :] = part[:, 128 * b : 128 * b + 128]

    outward = split_out(grads, kept, sent, place[0], semaphores, 16)
    e = dot(back_gate[...], wg[...], rows_both) + dot(back_up[...], wu[...], rows_both)
    gain_grads[1:2] = jnp.sum(mid * r2 * e, axis=0, keepdims=True)
    bm = g + norm_back(mid, r2, g_in, e)
    back_middle[...] = bm
    gain_grads[0:1] = jnp.sum(ao * r1 * bm, axis=0, keepdims=True)
    bao = norm_back(ao, r1, g_attn, bm).astype(bf16)
    back_attn[...] = bao
    back_attended[...] = dot(bao, wo[...], rows_both).astype(bf16)
    for copy in outward:
        copy.wait()


def middle_part(place, x, attended, upstream, gains, shares):
    return pl.pallas_call(
        middle_kernel,
        name="middle_part",
        in_specs=[pl.BlockSpec(memory_space=pltpu.SMEM)]
        + [whole()] * 4
        + [pl.BlockSpec(memory_space=pltpu.HBM)] * 16,
        out_specs=[whole()] * 5 + [pl.BlockSpec(memory_space=pltpu.HBM)] * 2,
        out_shape=[
            spec(512, 640, bf16),
            spec(512, 640, f32),
            spec(512, 640, bf16),
            spec(512, 1024, bf16),
            spec(8, 640, f32),
            spec(2, 7680, 128, bf16),
            spec(2, 7680, 128, bf16),
        ],
        scratch_shapes=[
            pltpu.VMEM((512, 640), bf16),
            pltpu.VMEM((512, 2048), f32),
            pltpu.VMEM((512, 2048), f32),
            pltpu.VMEM((512, 2048), bf16),
            pltpu.VMEM((512, 640), bf16),
            pltpu.VMEM((640, 512), bf16),
            pltpu.VMEM((640, 512), bf16),
            pltpu.VMEM((512, 2048), bf16),
            pltpu.VMEM((512, 2048), bf16),
            pltpu.VMEM((1024, 640), bf16),
            pltpu.VMEM((640, 2048), bf16),
            pltpu.VMEM((640, 2048), bf16),
            pltpu.VMEM((2048, 640), bf16),
            pltpu.VMEM((4, 7680, 128), bf16),
            pltpu.SemaphoreType.DMA((20,)),
        ],
        compiler_params=params(44),
        cost_estimate=cost(13_400_000_000, 23_000_000, 1_000_000),
    )(place, x, attended, upstream, gains, *shares)


def attend_back_kernel(
    q,
    k,
    v,
    offsets,
    level,
    back_attended,
    q_proj,
    k_proj,
    head_gains,
    cosine,
    sine,
    place,
    kv0,
    kv1,
    kv2,
    kv3,
    back_q,
    back_kv,
    gain_grads,
    back_halo,
    sum_k,
    sum_v,
    wkv,
    semaphores,
):
    t = pl.program_id(0)

    @pl.when(t == 0)
    def _():
        for copy in assemble((kv0, kv1, kv2, kv3), wkv, place[0], semaphores, 0):
            copy.wait()
        sum_k[...] = jnp.zeros_like(sum_k)
        sum_v[...] = jnp.zeros_like(sum_v)
        gain_grads[...] = jnp.zeros_like(gain_grads)

    near = pl.ds(pl.multiple_of(t * 256, 256), 768)
    mine = pl.ds(pl.multiple_of(t * 256 + 512, 256), 256)
    keys, values = k[near, :], v[near, :]
    visible = visible_keys(offsets[...])
    c, s = cosine[mine, :], sine[mine, :]
    for h in range(4):
        cols = slice(256 * h, 256 * h + 256)
        qh, bah = q[:, cols], back_attended[:, cols]
        scores = jnp.where(visible, dot(qh, keys, rows_both) * 0.0625, masked_value)
        probs = jnp.exp(scores - level[h])
        bp = dot(bah, values, rows_both)
        inner = jnp.sum(probs * bp, axis=-1, keepdims=True)
        bs = (probs * (bp - inner)).astype(bf16)
        sum_k[near, :] += dot(bs, qh, cols_both)
        sum_v[near, :] += dot(probs.astype(bf16), bah, cols_both)
        e = turn_back(dot(bs, keys) * 0.0625, c, s)
        qp = q_proj[:, cols]
        r = inverse_rms(qp)
        gain_grads[0:1] += jnp.sum(qp * r * e, axis=0, keepdims=True)
        back_q[:, cols] = norm_back(qp, r, head_gains[4:5], e).astype(bf16)

    @pl.when(t == 1)
    def _():
        e = turn_back(sum_k[...] * 0.0625, cosine[...], sine[...])
        kp = k_proj[...]
        r = inverse_rms(kp)
        gain_grads[1:2] = jnp.sum(kp * r * e, axis=0, keepdims=True)
        back_kv[:, :256] = norm_back(kp, r, head_gains[5:6], e).astype(bf16)
        back_kv[:, 256:] = sum_v[...].astype(bf16)
        back_halo[...] = dot(back_kv[:512, :], wkv[...], rows_both).astype(bf16)


def attend_back(
    q, k, v, offsets, level, back_attended, q_proj, k_proj, head_gains, cosine, sine, place, shares
):
    row = lambda i: (i, 0)
    fixed = lambda i: (0, 0)
    return pl.pallas_call(
        attend_back_kernel,
        name="attend_back",
        grid=(2,),
        in_specs=[
            pl.BlockSpec((256, 1024), row),
            pl.BlockSpec((1024, 256), fixed),
            pl.BlockSpec((1024, 256), fixed),
            pl.BlockSpec((256, 1), row),
            pl.BlockSpec((4, 256, 1), lambda i: (0, i, 0)),
            pl.BlockSpec((256, 1024), row),
            pl.BlockSpec((256, 1024), row),
            pl.BlockSpec((1024, 256), fixed),
            pl.BlockSpec((8, 256), fixed),
            pl.BlockSpec((1024, 128), fixed),
            pl.BlockSpec((1024, 128), fixed),
            pl.BlockSpec(memory_space=pltpu.SMEM),
        ]
        + [pl.BlockSpec(memory_space=pltpu.HBM)] * 4,
        out_specs=[
            pl.BlockSpec((256, 1024), row),
            pl.BlockSpec((1024, 512), fixed),
            pl.BlockSpec((8, 256), fixed),
            pl.BlockSpec((512, 640), fixed),
        ],
        out_shape=[
            spec(512, 1024, bf16),
            spec(1024, 512, bf16),
            spec(8, 256, f32),
            spec(512, 640, bf16),
        ],
        scratch_shapes=[
            pltpu.VMEM((1024, 256), f32),
            pltpu.VMEM((1024, 256), f32),
            pltpu.VMEM((640, 512), bf16),
            pltpu.SemaphoreType.DMA((4,)),
        ],
        compiler_params=params(16),
        cost_estimate=cost(4_300_000_000, 10_000_000, 2_000_000),
    )(
        q, k, v, offsets, level, back_attended, q_proj, k_proj, head_gains, cosine, sine, place, *shares
    )


def weights_kernel(
    place,
    normed,
    back_q,
    back_kv,
    attended,
    back_attn,
    halo,
    own,
    gain_mid,
    gain_head,
    q0,
    q1,
    q2,
    q3,
    kv0,
    kv1,
    kv2,
    kv3,
    back_own,
    kept,
    sent,
    wq,
    wkv,
    grads,
    semaphores,
):
    copies = assemble((kv0, kv1, kv2, kv3), wkv, place[0], semaphores, 0)
    copies += assemble((q0, q1, q2, q3), wq, place[0], semaphores, 4)
    turned = normed[...].astype(f32).T.astype(bf16)
    bq, bkv = back_q[...], back_kv[...]
    part = dot(turned[:, 512:], bq).astype(bf16)
    for b in range(8):
        for f in range(4):
            grads[f, 160 * b : 160 * b + 160, :] = part[
                160 * f : 160 * f + 160, 128 * b : 128 * b + 128
            ]
    part = dot(turned, bkv).astype(bf16)
    for b in range(4):
        for f in range(4):
            grads[f, 1280 + 160 * b : 1440 + 160 * b, :] = part[
                160 * f : 160 * f + 160, 128 * b : 128 * b + 128
            ]
    turned = back_attn[...].astype(f32).T.astype(bf16)
    part = dot(turned, attended[...]).astype(bf16)
    for f in range(4):
        for b in range(2):
            grads[f, 1920 + 640 * b : 2560 + 640 * b, :] = part[
                :, 256 * f + 128 * b : 256 * f + 128 * b + 128
            ]
    for copy in copies:
        copy.wait()
    e = dot(bkv[:512], wkv[...], rows_both)
    x = halo[...].astype(f32)
    grad = jnp.sum(x * inverse_rms(x) * e, axis=0, keepdims=True)
    e = dot(bkv[512:], wkv[...], rows_both) + dot(bq, wq[...], rows_both)
    back_own[...] = e
    x = own[...].astype(f32)
    grad = grad + jnp.sum(x * inverse_rms(x) * e, axis=0, keepdims=True)
    each = jnp.concatenate([grad, gain_mid[0:3]], axis=0)
    heads = gain_head[0:2]
    for f in range(4):
        share = each[:, 160 * f : 160 * f + 160]
        rest = jnp.concatenate([share[:, 128:], jnp.zeros((4, 96), f32)], axis=1)
        ends = jnp.concatenate([heads[:, 64 * f : 64 * f + 64], jnp.zeros((2, 64), f32)], axis=1)
        tile = jnp.concatenate([share[:, :128], rest, ends, jnp.zeros((6, 128), f32)], axis=0)
        grads[f, 3200:3216, :] = tile.astype(bf16)
        grads[f, 3216:, :] = jnp.zeros((368, 128), bf16)
    for copy in split_out(grads, kept, sent, place[0], semaphores, 8):
        copy.wait()


def weights_part(
    place, normed, back_q, back_kv, attended, back_attn, halo, own, gain_mid, gain_head, shares
):
    return pl.pallas_call(
        weights_kernel,
        name="weights_part",
        in_specs=[pl.BlockSpec(memory_space=pltpu.SMEM)]
        + [whole()] * 9
        + [pl.BlockSpec(memory_space=pltpu.HBM)] * 8,
        out_specs=[whole()] + [pl.BlockSpec(memory_space=pltpu.HBM)] * 2,
        out_shape=[
            spec(512, 640, f32),
            spec(2, 3584, 128, bf16),
            spec(2, 3584, 128, bf16),
        ],
        scratch_shapes=[
            pltpu.VMEM((640, 1024), bf16),
            pltpu.VMEM((640, 512), bf16),
            pltpu.VMEM((4, 3584, 128), bf16),
            pltpu.SemaphoreType.DMA((12,)),
        ],
        compiler_params=params(24),
        cost_estimate=cost(3_400_000_000, 14_000_000),
    )(place, normed, back_q, back_kv, attended, back_attn, halo, own, gain_mid, gain_head, *shares)


def finish_kernel(own, back_own, returned, back_middle, gains, grad_in):
    x = own[...].astype(f32)
    e = back_own[...] + returned[...].astype(f32)
    grad_in[...] = (back_middle[...] + norm_back(x, inverse_rms(x), gains[0:1], e)).astype(bf16)


def finish(own, back_own, returned, back_middle, gains):
    row = lambda i: (i, 0)
    return pl.pallas_call(
        finish_kernel,
        name="finish",
        grid=(4,),
        in_specs=[pl.BlockSpec((128, 640), row)] * 4 + [pl.BlockSpec((8, 640), lambda i: (0, 0))],
        out_specs=pl.BlockSpec((128, 640), row),
        out_shape=spec(512, 640, bf16),
        compiler_params=params(10),
        cost_estimate=cost(4_000_000, 5_000_000),
    )(own, back_own, returned, back_middle, gains)


def rope_tables(offsets):
    powers = jnp.arange(128, dtype=f32) * (2.0 / 256)
    row = jnp.arange(512, dtype=jnp.int32)
    every = jnp.concatenate([offsets[0] - 512 + row, offsets])
    angles = every.astype(f32)[:, None] * (rope_base ** (-powers))[None, :]
    return jnp.cos(angles), jnp.sin(angles)


def unpack_kernel(spot, a0, a1, a2, a3, b0, b1, b2, b3, *rest):
    outs, gains, held, (ffn, attn, semaphores) = rest[:7], rest[7], rest[8:15], rest[15:]
    q, k, v, out, gate, up, down = held
    x, y = spot[0], spot[1]
    copies = []
    for half, pieces in enumerate(((a0, a1, a2, a3), (b0, b1, b2, b3))):
        for i in range(4):
            for j in range(4):
                first, second = (x, y) if half == 0 else (y, x)
                block = 16 * half + lax.rem(first - i + 4, 4) * 4 + lax.rem(second - j + 4, 4)
                n = (half * 4 + i) * 4 + j
                for m, (into, start, rows) in enumerate(((ffn, 0, 240), (attn, 240, 112))):
                    copies.append(
                        pltpu.make_async_copy(
                            pieces[i].at[j, pl.ds(start, rows), :],
                            into.at[pl.ds(pl.multiple_of(block * rows, 16), rows), :],
                            semaphores.at[2 * n + m],
                        )
                    )
    for copy in copies:
        copy.start()
    for copy in copies:
        copy.wait()
    outward = []

    def leave(n):
        copy = pltpu.make_async_copy(held[n], outs[n], semaphores.at[64 + n])
        copy.start()
        outward.append(copy)

    for n, into, flat, first, count in (
        (4, gate, ffn, 0, 16),
        (5, up, ffn, 2560, 16),
        (0, q, attn, 0, 8),
        (1, k, attn, 1280, 2),
        (2, v, attn, 1600, 2),
    ):
        for b in range(count):
            at = first + 160 * b
            into[:, 128 * b : 128 * b + 128] = flat[at : at + 160, :].astype(f32)
        leave(n)
    for n, into, flat, first, count in ((6, down, ffn, 5120, 4), (3, out, attn, 1920, 2)):
        for b in range(count):
            at = first + 640 * b
            into[128 * b : 128 * b + 128, :] = flat[at : at + 640, :].astype(f32).T
        leave(n)
    gains[...] = attn[3200:3216, :].astype(f32)
    for copy in outward:
        copy.wait()


def unpack(spot, pieces):
    shapes = [(160, 1024), (160, 256), (160, 256), (256, 640), (160, 2048), (160, 2048), (512, 640)]
    return pl.pallas_call(
        unpack_kernel,
        name="unpack",
        in_specs=[pl.BlockSpec(memory_space=pltpu.SMEM)] + [pl.BlockSpec(memory_space=pltpu.HBM)] * 8,
        out_specs=[pl.BlockSpec(memory_space=pltpu.HBM)] * 7 + [whole()],
        out_shape=[spec(*shape, f32) for shape in shapes] + [spec(16, 128, f32)],
        scratch_shapes=[pltpu.VMEM(shape, f32) for shape in shapes]
        + [
            pltpu.VMEM((7680, 128), bf16),
            pltpu.VMEM((3584, 128), bf16),
            pltpu.SemaphoreType.DMA((71,)),
        ],
        compiler_params=params(14),
        cost_estimate=cost(4_000_000, 11_000_000),
    )(spot, *pieces)


def sum_of(parts):
    whole = parts[0].astype(f32)
    for part in parts[1:]:
        whole = whole + part.astype(f32)
    return whole.astype(bf16)


def turn_around(position, d):
    return lax.rem(position + d, 4)


def first_kernel(spot, kept_ffn, got_ffn, kept_attn, got_attn, *outs):
    for half in range(2):
        for i, d in enumerate((0, 1, 3, 2)):
            at = turn_around(spot[half], d)
            out = outs[4 * half + i]
            for z in range(2):
                for j in range(4):
                    out[z, j, :240] = sum_of([r[z, half, at, j] for r in (kept_ffn, got_ffn)])
                    out[z, j, 240:] = sum_of([r[z, half, at, j] for r in (kept_attn, got_attn)])


def first_sums(spot, kept_ffn, got_ffn, kept_attn, got_attn):
    ins = [p.reshape(2, 2, 4, 4, p.shape[1] // 32, 128) for p in (kept_ffn, got_ffn, kept_attn, got_attn)]
    return pl.pallas_call(
        first_kernel,
        name="first_sums",
        in_specs=[pl.BlockSpec(memory_space=pltpu.SMEM)] + [whole()] * 4,
        out_specs=[whole()] * 8,
        out_shape=[spec(2, 4, 352, 128, bf16)] * 8,
        compiler_params=params(24),
        cost_estimate=cost(3_000_000, 17_000_000),
    )(spot, *ins)


def second_kernel(spot, *refs):
    ins, outs = refs[:8], refs[8:]
    for half in range(2):
        parts = ins[4 * half : 4 * half + 4]
        for i, d in enumerate((0, 1, 3, 2)):
            at = turn_around(spot[1 - half], d)
            for z in range(2):
                outs[4 * half + i][z] = sum_of([r[z, at] for r in parts])


def second_sums(spot, parts):
    return pl.pallas_call(
        second_kernel,
        name="second_sums",
        in_specs=[pl.BlockSpec(memory_space=pltpu.SMEM)] + [whole()] * 8,
        out_specs=[whole()] * 8,
        out_shape=[spec(2, 352, 128, bf16)] * 8,
        compiler_params=params(12),
        cost_estimate=cost(1_000_000, 7_200_000),
    )(spot, *parts)


def third_kernel(place, *refs):
    ins, (mine, other) = refs[:8], refs[8:]
    z = lax.div(place[0], 2)
    for half in range(2):
        parts = ins[4 * half : 4 * half + 4]
        mine[half] = sum_of([r[z] for r in parts])
        other[half] = sum_of([r[1 - z] for r in parts])


def third_sums(place, parts):
    return pl.pallas_call(
        third_kernel,
        name="third_sums",
        in_specs=[pl.BlockSpec(memory_space=pltpu.SMEM)] + [whole()] * 8,
        out_specs=[whole()] * 2,
        out_shape=[spec(2, 352, 128, bf16)] * 2,
        compiler_params=params(10),
        cost_estimate=cost(1_000_000, 1_800_000),
    )(place, *parts)


def fourth_kernel(p0, p1, p2, p3, a, b):
    for half, out in enumerate((a, b)):
        out[...] = sum_of([p0[half], p1[half], p2[half], p3[half]])


def fourth_sums(parts):
    return pl.pallas_call(
        fourth_kernel,
        name="fourth_sums",
        in_specs=[whole()] * 4,
        out_specs=[whole()] * 2,
        out_shape=[spec(352, 128, bf16)] * 2,
        compiler_params=params(10),
        cost_estimate=cost(1_000_000, 900_000),
    )(*parts)


def seq_index(z, x, y):
    return (z % 2 * 4 + x % 4) * 4 + y % 4


def along_xy(dx, dy):
    return [
        (seq_index(z, x, y), seq_index(z, x + dx, y + dy))
        for z in range(2)
        for x in range(4)
        for y in range(4)
    ]


def along_z(step):
    pairs = []
    for s in range(32):
        for f in range(4):
            z = s // 16 * 2 + f // 2
            t = step(z)
            pairs.append((s * 4 + f, (t // 2 * 16 + s % 16) * 4 + t % 2 * 2 + f % 2))
    return pairs


def swap_core(value):
    return lax.ppermute(value, "fsdp", [(0, 1), (1, 0), (2, 3), (3, 2)])


def swap_near(value):
    return lax.ppermute(value, "fsdp", [(0, 2), (1, 3), (2, 0), (3, 1)])


def swap_far(value):
    return lax.ppermute(value, ("seq", "fsdp"), along_z(lambda z: 3 - z))


def swap_hi(value):
    return lax.ppermute(value, "seq", [(s, (s + 16) % 32) for s in range(32)])


def move_x(value, d):
    return lax.ppermute(value, "seq", along_xy(d, 0))


def move_y(value, d):
    return lax.ppermute(value, "seq", along_xy(0, d))


def shifted(value, steps):
    first, last = (max(0, -steps), min(32, 32 - steps))
    return lax.ppermute(value, "seq", [(source, source + steps) for source in range(first, last)])


steps = (1, 3, 2)


def move_first(parts):
    return (
        [parts[0]]
        + [move_x(p, d) for p, d in zip(parts[1:4], steps)]
        + [parts[4]]
        + [move_y(p, d) for p, d in zip(parts[5:8], steps)]
    )


def move_second(parts):
    return (
        [parts[0]]
        + [move_y(p, d) for p, d in zip(parts[1:4], steps)]
        + [parts[4]]
        + [move_x(p, d) for p, d in zip(parts[5:8], steps)]
    )


def together(*groups):
    leaves, tree = jax.tree.flatten(groups)
    return jax.tree.unflatten(tree, lax.optimization_barrier(tuple(leaves)))


def body(
    hidden_in,
    cotangent,
    positions,
    query_weight,
    key_weight,
    value_weight,
    output_weight,
    gate_weight,
    up_weight,
    down_weight,
    norm_in,
    norm_attn,
    norm_ffn_in,
    norm_ffn_out,
    norm_query,
    norm_key,
):
    s = lax.axis_index("seq")
    f = lax.axis_index("fsdp")
    x, y, z_lo, core = s // 4 % 4, s % 4, f // 2, f % 2
    place = f.astype(jnp.int32).reshape(1)
    spot = jnp.stack([x, y]).astype(jnp.int32)
    own = hidden_in[0]
    upstream = cotangent[0]
    offsets = positions[0]

    near = jnp.concatenate([query_weight, gate_weight], axis=1)
    near, key_weight = together(near, key_weight)
    far = pack(
        [norm_in, norm_attn, norm_ffn_in, norm_ffn_out, norm_query, norm_key],
        key_weight,
        value_weight,
        up_weight,
    )
    near_partner, far_partner = swap_near(near), swap_far(far)
    halo = shifted(own, 1)
    near_partner, halo = together(near_partner, halo)
    q_shares = (near, swap_core(near), near_partner, swap_core(near_partner))
    kv_shares = (far, swap_core(far), far_partner, swap_core(far_partner))
    wo_partner, wd_partner = swap_near(output_weight), swap_far(down_weight)
    tiles = [share[160:168, :512] for share in kv_shares]
    tiles = [
        jnp.where(
            j // 2 == z_lo,
            jnp.where(j % 2 == core, tiles[0], tiles[1]),
            jnp.where(j % 2 == core, tiles[2], tiles[3]),
        )
        for j in range(4)
    ]
    gains = jnp.concatenate([t[:, :160] for t in tiles], axis=1).astype(f32)
    head_gains = jnp.concatenate([t[:, :64] for t in tiles], axis=1).astype(f32)

    cosine, sine = rope_tables(offsets)
    column = offsets[:, None]
    normed, q, k, v, q_proj, k_proj = project(
        place, halo, own, gains, head_gains, q_shares, kv_shares, cosine, sine
    )
    (q, k, v), wo_partner, wd_partner = together((q, k, v), wo_partner, wd_partner)
    wo_shares = (output_weight, swap_core(output_weight), wo_partner, swap_core(wo_partner))
    wd_shares = (down_weight, swap_core(down_weight), wd_partner, swap_core(wd_partner))
    attended, level = attend(q, k, v, column)
    layer_out, back_middle, back_attn, back_attended, gain_mid, kept, sent = middle_part(
        place, own, attended, upstream, gains, wo_shares + q_shares + kv_shares + wd_shares
    )
    got = swap_core(sent)
    back_q, back_kv, gain_head, back_halo = attend_back(
        q,
        k,
        v,
        column,
        level,
        back_attended,
        q_proj,
        k_proj,
        head_gains,
        cosine,
        sine,
        place,
        kv_shares,
    )
    returned = shifted(back_halo, -1)
    back_own, kept_attn, sent = weights_part(
        place,
        normed,
        back_q,
        back_kv,
        attended,
        back_attn,
        halo,
        own,
        gain_mid,
        gain_head,
        q_shares + kv_shares,
    )
    sent, returned = together(sent, returned)
    got_attn = swap_core(sent)
    first = move_first(first_sums(spot, kept, got, kept_attn, got_attn))
    mine, other = third_sums(place, move_second(second_sums(spot, first)))
    a, b = fourth_sums([mine, swap_near(other), swap_far(other), swap_hi(mine)])
    a = jnp.stack([a] + [move_y(a, d) for d in (1, 2, 3)])
    b = jnp.stack([b] + [move_x(b, d) for d in (1, 2, 3)])
    a, b = together(a, b)
    pieces = [a] + [move_x(a, d) for d in (1, 2, 3)] + [b] + [move_y(b, d) for d in (1, 2, 3)]
    grad_q, grad_k, grad_v, grad_o, grad_g, grad_u, grad_d, tile = unpack(spot, pieces)
    grad_in = finish(own, back_own, returned, back_middle, gains)
    wide = jnp.concatenate([tile[0:4], tile[4:8, :32]], axis=1)
    return (
        layer_out[None],
        grad_in[None],
        grad_q,
        grad_k,
        grad_v,
        grad_o,
        grad_g,
        grad_u,
        grad_d,
        wide[0],
        wide[1],
        wide[2],
        wide[3],
        tile[8, :64],
        tile[9, :64],
    )


def solution(mesh):
    three = P("fsdp", "seq", None)
    two = P("fsdp", None)
    one = P("fsdp")
    return jax.shard_map(
        body,
        mesh=mesh,
        in_specs=(three, three, P("fsdp", "seq")) + (two,) * 7 + (one,) * 6,
        out_specs=(three, three) + (two,) * 7 + (one,) * 6,
        check_vma=False,
    )
```

```python
import jax
import jax.numpy as jnp
from jax import lax
from jax.experimental import pallas as pl
from jax.experimental.pallas import tpu as pltpu
from jax.sharding import PartitionSpec as P

WINDOW = 512
epsilon = 1e-06
rope_base = 10000.0
masked_value = -1e30
bf16 = jnp.bfloat16
f32 = jnp.float32

rows_out = ((1,), (0,))
rows_both = ((1,), (1,))
cols_both = ((0,), (0,))


def dot(a, b, dims=rows_out):
    return lax.dot_general(a, b, (dims, ((), ())), preferred_element_type=f32)


def spec(*shape):
    return jax.ShapeDtypeStruct(shape[:-1], shape[-1])


def whole():
    return pl.BlockSpec(memory_space=pltpu.VMEM)


def params(mib):
    return pltpu.CompilerParams(vmem_limit_bytes=mib * 1024 * 1024)


def cost(flops, moved, exps=0):
    return pl.CostEstimate(flops=flops, bytes_accessed=moved, transcendentals=exps)


def inverse_rms(v):
    return lax.rsqrt(jnp.mean(v * v, axis=-1, keepdims=True) + epsilon)


def norm_back(v, r, gain, e):
    scaled = gain * e
    return r * scaled - v * (r * r * r * jnp.mean(v * scaled, axis=-1, keepdims=True))


def turn(v, cosine, sine):
    a, b = v[:, :128], v[:, 128:]
    return jnp.concatenate([a * cosine - b * sine, b * cosine + a * sine], axis=1)


def turn_back(v, cosine, sine):
    a, b = v[:, :128], v[:, 128:]
    return jnp.concatenate([a * cosine + b * sine, b * cosine - a * sine], axis=1)


def assemble(pieces, into, place, semaphores, first):
    rows = into.shape[0] // 4
    copies = []
    for r in range(4):
        at = pl.ds(pl.multiple_of((place ^ r) * rows, rows), rows)
        copies.append(
            pltpu.make_async_copy(
                pieces[r],
                into.at[at, :],
                semaphores.at[first + r],
            )
        )
    for copy in copies:
        copy.start()
    return copies


def split_out(grads, kept, sent, place, semaphores, first):
    core = lax.rem(place, 2)
    copies = []
    for z in range(2):
        copies.append(
            pltpu.make_async_copy(
                grads.at[2 * z + 1 - core], sent.at[z], semaphores.at[first + 2 * z]
            )
        )
        copies.append(
            pltpu.make_async_copy(
                grads.at[2 * z + core], kept.at[z], semaphores.at[first + 2 * z + 1]
            )
        )
    for copy in copies:
        copy.start()
    return copies


def pack_kernel(g0, g1, g2, g3, g4, g5, out, *rest):
    held, semaphores = rest[:6], rest[6]
    copies = [
        pltpu.make_async_copy(source, into, semaphores.at[i])
        for i, (source, into) in enumerate(zip((g0, g1, g2, g3, g4, g5), held))
    ]
    for copy in copies:
        copy.start()
    out[...] = jnp.zeros_like(out)
    for copy in copies:
        copy.wait()
    for i, ref in enumerate(held):
        n = ref.shape[0]
        out[i : i + 1, :n] = ref[...].astype(f32).reshape(1, n)


def pack(rows):
    return pl.pallas_call(
        pack_kernel,
        name="pack",
        in_specs=[pl.BlockSpec(memory_space=pltpu.HBM)] * 6,
        out_specs=whole(),
        out_shape=spec(8, 256, f32),
        scratch_shapes=[pltpu.VMEM(row.shape, bf16) for row in rows]
        + [pltpu.SemaphoreType.DMA((6,))],
        compiler_params=params(4),
        cost_estimate=cost(100_000, 20_000),
    )(*rows)


def project_kernel(
    place,
    halo,
    own,
    gains,
    head_gains,
    q0,
    q1,
    q2,
    q3,
    kv0,
    kv1,
    kv2,
    kv3,
    cosine,
    sine,
    normed,
    q,
    k,
    v,
    q_proj,
    k_proj,
    wq,
    wkv,
    semaphores,
):
    i = pl.program_id(0)

    @pl.when(i == 0)
    def _():
        copies = assemble((kv0, kv1, kv2, kv3), wkv, place[0], semaphores, 0)
        copies += assemble((q0, q1, q2, q3), wq, place[0], semaphores, 4)
        for copy in copies:
            copy.wait()

    x = jnp.where(i < 2, halo[...], own[...]).astype(f32)
    n = (x * inverse_rms(x) * gains[0:1]).astype(bf16)
    normed[...] = n
    c, s = cosine[...], sine[...]
    kv = dot(n, wkv[...])
    kp = kv[:, :256]
    k_proj[...] = kp
    v[...] = kv[:, 256:].astype(bf16)
    k[...] = turn(kp * inverse_rms(kp) * head_gains[5:6], c, s).astype(bf16)

    @pl.when(i >= 2)
    def _():
        for h in range(4):
            cols = slice(256 * h, 256 * h + 256)
            qp = dot(n, wq[:, cols])
            q_proj[:, cols] = qp
            q[:, cols] = turn(qp * inverse_rms(qp) * head_gains[4:5], c, s).astype(bf16)


def project(place, halo, own, gains, head_gains, q_shares, kv_shares, cosine, sine):
    late = lambda i: (jnp.maximum(i - 2, 0), 0)
    row = lambda i: (i, 0)
    fixed = lambda i: (0, 0)
    return pl.pallas_call(
        project_kernel,
        name="project",
        grid=(4,),
        in_specs=[
            pl.BlockSpec(memory_space=pltpu.SMEM),
            pl.BlockSpec((256, 640), lambda i: (jnp.minimum(i, 1), 0)),
            pl.BlockSpec((256, 640), late),
            pl.BlockSpec((8, 640), fixed),
            pl.BlockSpec((8, 256), fixed),
        ]
        + [pl.BlockSpec(memory_space=pltpu.HBM)] * 8
        + [pl.BlockSpec((256, 128), row)] * 2,
        out_specs=[
            pl.BlockSpec((256, 640), row),
            pl.BlockSpec((256, 1024), late),
            pl.BlockSpec((256, 256), row),
            pl.BlockSpec((256, 256), row),
            pl.BlockSpec((256, 1024), late),
            pl.BlockSpec((256, 256), row),
        ],
        out_shape=[
            spec(1024, 640, bf16),
            spec(512, 1024, bf16),
            spec(1024, 256, bf16),
            spec(1024, 256, bf16),
            spec(512, 1024, f32),
            spec(1024, 256, f32),
        ],
        scratch_shapes=[
            pltpu.VMEM((640, 1024), bf16),
            pltpu.VMEM((640, 512), bf16),
            pltpu.SemaphoreType.DMA((8,)),
        ],
        compiler_params=params(14),
        cost_estimate=cost(1_350_000_000, 9_000_000),
    )(place, halo, own, gains, head_gains, *q_shares, *kv_shares, cosine, sine)


def visible_keys(offsets):
    distance = (
        lax.broadcasted_iota(jnp.int32, (256, 768), 0)
        + 512
        - lax.broadcasted_iota(jnp.int32, (256, 768), 1)
    )
    return (distance >= 0) & (distance < WINDOW) & (distance <= offsets)


def attend_kernel(q, k, v, offsets, attended, level):
    t = pl.program_id(0)
    near = pl.ds(pl.multiple_of(t * 256, 256), 768)
    keys, values = k[near, :], v[near, :]
    visible = visible_keys(offsets[...])
    for h in range(4):
        cols = slice(256 * h, 256 * h + 256)
        scores = jnp.where(visible, dot(q[:, cols], keys, rows_both) * 0.0625, masked_value)
        top = jnp.max(scores, axis=-1, keepdims=True)
        e = jnp.exp(scores - top)
        total = jnp.sum(e, axis=-1, keepdims=True)
        level[h] = top + jnp.log(total)
        probs = (e * (1.0 / total)).astype(bf16)
        attended[:, cols] = dot(probs, values).astype(bf16)


def attend(q, k, v, offsets):
    row = lambda i: (i, 0)
    fixed = lambda i: (0, 0)
    return pl.pallas_call(
        attend_kernel,
        name="attend",
        grid=(2,),
        in_specs=[
            pl.BlockSpec((256, 1024), row),
            pl.BlockSpec((1024, 256), fixed),
            pl.BlockSpec((1024, 256), fixed),
            pl.BlockSpec((256, 1), row),
        ],
        out_specs=[
            pl.BlockSpec((256, 1024), row),
            pl.BlockSpec((4, 256, 1), lambda i: (0, i, 0)),
        ],
        out_shape=[spec(512, 1024, bf16), spec(4, 512, 1, f32)],
        compiler_params=params(10),
        cost_estimate=cost(1_700_000_000, 4_000_000, 2_000_000),
    )(q, k, v, offsets)


def middle_kernel(
    place,
    x_ref,
    attended,
    upstream,
    gains,
    o0,
    o1,
    o2,
    o3,
    g0,
    g1,
    g2,
    g3,
    u0,
    u1,
    u2,
    u3,
    d0,
    d1,
    d2,
    d3,
    layer_out,
    back_middle,
    back_attn,
    back_attended,
    gain_grads,
    kept,
    sent,
    ffn_in,
    kept_a,
    kept_b,
    hidden,
    back_out,
    in_turned,
    out_turned,
    back_gate,
    back_up,
    wo,
    wg,
    wu,
    wd,
    grads,
    semaphores,
):
    output_copies = assemble((o0, o1, o2, o3), wo, place[0], semaphores, 0)
    gate_copies = assemble((g0, g1, g2, g3), wg, place[0], semaphores, 4)
    up_copies = assemble((u0, u1, u2, u3), wu, place[0], semaphores, 8)
    down_copies = assemble((d0, d1, d2, d3), wd, place[0], semaphores, 12)
    for copy in output_copies:
        copy.wait()
    g_attn, g_in, g_out = gains[1:2], gains[2:3], gains[3:4]
    ao = dot(attended[...], wo[...])
    r1 = inverse_rms(ao)
    mid = x_ref[...].astype(f32) + ao * r1 * g_attn
    r2 = inverse_rms(mid)
    ffn_in[...] = (mid * r2 * g_in).astype(bf16)
    for copy in gate_copies + up_copies:
        copy.wait()

    for j in range(8):
        cols = slice(256 * j, 256 * j + 256)
        u = dot(ffn_in[...], wg[:, cols])
        up = dot(ffn_in[...], wu[:, cols])
        root = 0.7978845608028654
        square = u * u
        t = jnp.tanh(u * (root + (root * 0.044715) * square))
        half = 0.5 + 0.5 * t
        act = u * half
        slope = half + act * (1.0 - t) * (root + (3 * 0.044715 * root) * square)
        hidden[:, cols] = (act * up).astype(bf16)
        kept_a[:, cols] = act
        kept_b[:, cols] = up * slope

    for copy in down_copies:
        copy.wait()
    fo = dot(hidden[...], wd[...])
    r3 = inverse_rms(fo)
    layer_out[...] = (mid + fo * r3 * g_out).astype(bf16)
    g = upstream[...].astype(f32)
    gain_grads[2:3] = jnp.sum(fo * r3 * g, axis=0, keepdims=True)
    bfo = norm_back(fo, r3, g_out, g)
    back_out[...] = bfo.astype(bf16)
    out_turned[...] = back_out[...].T
    in_turned[...] = ffn_in[...].T

    for j in range(8):
        cols = slice(256 * j, 256 * j + 256)
        bh = dot(back_out[...], wd[cols, :], rows_both)
        bu = (bh * kept_a[:, cols]).astype(bf16)
        bg = (bh * kept_b[:, cols]).astype(bf16)
        back_gate[:, cols] = bg
        back_up[:, cols] = bu

    for base, right in ((0, back_gate), (2560, back_up)):
        for j in range(2048 // 512):
            part = dot(in_turned[...], right[:, 512 * j : 512 * j + 512]).astype(bf16)
            for b in range(512 // 128):
                at = base + (512 // 128 * j + b) * 160
                for f in range(4):
                    grads[f, at : at + 160, :] = part[
                        160 * f : 160 * f + 160, 128 * b : 128 * b + 128
                    ]
    for f in range(4):
        part = dot(out_turned[...], hidden[:, 512 * f : 512 * f + 512]).astype(bf16)
        for b in range(4):
            at = 5120 + 640 * b
            grads[f, at : at + 640, :] = part[:, 128 * b : 128 * b + 128]

    outward = split_out(grads, kept, sent, place[0], semaphores, 16)
    e = dot(back_gate[...], wg[...], rows_both) + dot(back_up[...], wu[...], rows_both)
    gain_grads[1:2] = jnp.sum(mid * r2 * e, axis=0, keepdims=True)
    bm = g + norm_back(mid, r2, g_in, e)
    back_middle[...] = bm
    gain_grads[0:1] = jnp.sum(ao * r1 * bm, axis=0, keepdims=True)
    bao = norm_back(ao, r1, g_attn, bm).astype(bf16)
    back_attn[...] = bao
    back_attended[...] = dot(bao, wo[...], rows_both).astype(bf16)
    for copy in outward:
        copy.wait()


def middle_part(place, x, attended, upstream, gains, shares):
    return pl.pallas_call(
        middle_kernel,
        name="middle_part",
        in_specs=[pl.BlockSpec(memory_space=pltpu.SMEM)]
        + [whole()] * 4
        + [pl.BlockSpec(memory_space=pltpu.HBM)] * 16,
        out_specs=[whole()] * 5 + [pl.BlockSpec(memory_space=pltpu.HBM)] * 2,
        out_shape=[
            spec(512, 640, bf16),
            spec(512, 640, f32),
            spec(512, 640, bf16),
            spec(512, 1024, bf16),
            spec(8, 640, f32),
            spec(2, 7680, 128, bf16),
            spec(2, 7680, 128, bf16),
        ],
        scratch_shapes=[
            pltpu.VMEM((512, 640), bf16),
            pltpu.VMEM((512, 2048), f32),
            pltpu.VMEM((512, 2048), f32),
            pltpu.VMEM((512, 2048), bf16),
            pltpu.VMEM((512, 640), bf16),
            pltpu.VMEM((640, 512), bf16),
            pltpu.VMEM((640, 512), bf16),
            pltpu.VMEM((512, 2048), bf16),
            pltpu.VMEM((512, 2048), bf16),
            pltpu.VMEM((1024, 640), bf16),
            pltpu.VMEM((640, 2048), bf16),
            pltpu.VMEM((640, 2048), bf16),
            pltpu.VMEM((2048, 640), bf16),
            pltpu.VMEM((4, 7680, 128), bf16),
            pltpu.SemaphoreType.DMA((20,)),
        ],
        compiler_params=params(44),
        cost_estimate=cost(13_400_000_000, 23_000_000, 1_000_000),
    )(place, x, attended, upstream, gains, *shares)


def attend_back_kernel(
    q,
    k,
    v,
    offsets,
    level,
    back_attended,
    q_proj,
    k_proj,
    head_gains,
    cosine,
    sine,
    place,
    kv0,
    kv1,
    kv2,
    kv3,
    back_q,
    back_kv,
    gain_grads,
    back_halo,
    sum_k,
    sum_v,
    wkv,
    semaphores,
):
    t = pl.program_id(0)

    @pl.when(t == 0)
    def _():
        for copy in assemble((kv0, kv1, kv2, kv3), wkv, place[0], semaphores, 0):
            copy.wait()
        sum_k[...] = jnp.zeros_like(sum_k)
        sum_v[...] = jnp.zeros_like(sum_v)
        gain_grads[...] = jnp.zeros_like(gain_grads)

    near = pl.ds(pl.multiple_of(t * 256, 256), 768)
    mine = pl.ds(pl.multiple_of(t * 256 + 512, 256), 256)
    keys, values = k[near, :], v[near, :]
    visible = visible_keys(offsets[...])
    c, s = cosine[mine, :], sine[mine, :]
    for h in range(4):
        cols = slice(256 * h, 256 * h + 256)
        qh, bah = q[:, cols], back_attended[:, cols]
        scores = jnp.where(visible, dot(qh, keys, rows_both) * 0.0625, masked_value)
        probs = jnp.exp(scores - level[h])
        bp = dot(bah, values, rows_both)
        inner = jnp.sum(probs * bp, axis=-1, keepdims=True)
        bs = (probs * (bp - inner)).astype(bf16)
        sum_k[near, :] += dot(bs, qh, cols_both)
        sum_v[near, :] += dot(probs.astype(bf16), bah, cols_both)
        e = turn_back(dot(bs, keys) * 0.0625, c, s)
        qp = q_proj[:, cols]
        r = inverse_rms(qp)
        gain_grads[0:1] += jnp.sum(qp * r * e, axis=0, keepdims=True)
        back_q[:, cols] = norm_back(qp, r, head_gains[4:5], e).astype(bf16)

    @pl.when(t == 1)
    def _():
        e = turn_back(sum_k[...] * 0.0625, cosine[...], sine[...])
        kp = k_proj[...]
        r = inverse_rms(kp)
        gain_grads[1:2] = jnp.sum(kp * r * e, axis=0, keepdims=True)
        back_kv[:, :256] = norm_back(kp, r, head_gains[5:6], e).astype(bf16)
        back_kv[:, 256:] = sum_v[...].astype(bf16)
        back_halo[...] = dot(back_kv[:512, :], wkv[...], rows_both).astype(bf16)


def attend_back(
    q, k, v, offsets, level, back_attended, q_proj, k_proj, head_gains, cosine, sine, place, shares
):
    row = lambda i: (i, 0)
    fixed = lambda i: (0, 0)
    return pl.pallas_call(
        attend_back_kernel,
        name="attend_back",
        grid=(2,),
        in_specs=[
            pl.BlockSpec((256, 1024), row),
            pl.BlockSpec((1024, 256), fixed),
            pl.BlockSpec((1024, 256), fixed),
            pl.BlockSpec((256, 1), row),
            pl.BlockSpec((4, 256, 1), lambda i: (0, i, 0)),
            pl.BlockSpec((256, 1024), row),
            pl.BlockSpec((256, 1024), row),
            pl.BlockSpec((1024, 256), fixed),
            pl.BlockSpec((8, 256), fixed),
            pl.BlockSpec((1024, 128), fixed),
            pl.BlockSpec((1024, 128), fixed),
            pl.BlockSpec(memory_space=pltpu.SMEM),
        ]
        + [pl.BlockSpec(memory_space=pltpu.HBM)] * 4,
        out_specs=[
            pl.BlockSpec((256, 1024), row),
            pl.BlockSpec((1024, 512), fixed),
            pl.BlockSpec((8, 256), fixed),
            pl.BlockSpec((512, 640), fixed),
        ],
        out_shape=[
            spec(512, 1024, bf16),
            spec(1024, 512, bf16),
            spec(8, 256, f32),
            spec(512, 640, bf16),
        ],
        scratch_shapes=[
            pltpu.VMEM((1024, 256), f32),
            pltpu.VMEM((1024, 256), f32),
            pltpu.VMEM((640, 512), bf16),
            pltpu.SemaphoreType.DMA((4,)),
        ],
        compiler_params=params(16),
        cost_estimate=cost(4_300_000_000, 10_000_000, 2_000_000),
    )(
        q, k, v, offsets, level, back_attended, q_proj, k_proj, head_gains, cosine, sine, place, *shares
    )


def weights_kernel(
    place,
    normed,
    back_q,
    back_kv,
    attended,
    back_attn,
    halo,
    own,
    gain_mid,
    gain_head,
    q0,
    q1,
    q2,
    q3,
    kv0,
    kv1,
    kv2,
    kv3,
    back_own,
    kept,
    sent,
    wq,
    wkv,
    grads,
    semaphores,
):
    copies = assemble((kv0, kv1, kv2, kv3), wkv, place[0], semaphores, 0)
    copies += assemble((q0, q1, q2, q3), wq, place[0], semaphores, 4)
    turned = normed[...].astype(f32).T.astype(bf16)
    bq, bkv = back_q[...], back_kv[...]
    part = dot(turned[:, 512:], bq).astype(bf16)
    for b in range(8):
        for f in range(4):
            grads[f, 160 * b : 160 * b + 160, :] = part[
                160 * f : 160 * f + 160, 128 * b : 128 * b + 128
            ]
    part = dot(turned, bkv).astype(bf16)
    for b in range(4):
        for f in range(4):
            grads[f, 1280 + 160 * b : 1440 + 160 * b, :] = part[
                160 * f : 160 * f + 160, 128 * b : 128 * b + 128
            ]
    turned = back_attn[...].astype(f32).T.astype(bf16)
    part = dot(turned, attended[...]).astype(bf16)
    for f in range(4):
        for b in range(2):
            grads[f, 1920 + 640 * b : 2560 + 640 * b, :] = part[
                :, 256 * f + 128 * b : 256 * f + 128 * b + 128
            ]
    for copy in copies:
        copy.wait()
    e = dot(bkv[:512], wkv[...], rows_both)
    x = halo[...].astype(f32)
    grad = jnp.sum(x * inverse_rms(x) * e, axis=0, keepdims=True)
    e = dot(bkv[512:], wkv[...], rows_both) + dot(bq, wq[...], rows_both)
    back_own[...] = e
    x = own[...].astype(f32)
    grad = grad + jnp.sum(x * inverse_rms(x) * e, axis=0, keepdims=True)
    each = jnp.concatenate([grad, gain_mid[0:3]], axis=0)
    heads = gain_head[0:2]
    for f in range(4):
        share = each[:, 160 * f : 160 * f + 160]
        rest = jnp.concatenate([share[:, 128:], jnp.zeros((4, 96), f32)], axis=1)
        ends = jnp.concatenate([heads[:, 64 * f : 64 * f + 64], jnp.zeros((2, 64), f32)], axis=1)
        tile = jnp.concatenate([share[:, :128], rest, ends, jnp.zeros((6, 128), f32)], axis=0)
        grads[f, 3200:3216, :] = tile.astype(bf16)
        grads[f, 3216:, :] = jnp.zeros((368, 128), bf16)
    for copy in split_out(grads, kept, sent, place[0], semaphores, 8):
        copy.wait()


def weights_part(
    place, normed, back_q, back_kv, attended, back_attn, halo, own, gain_mid, gain_head, shares
):
    return pl.pallas_call(
        weights_kernel,
        name="weights_part",
        in_specs=[pl.BlockSpec(memory_space=pltpu.SMEM)]
        + [whole()] * 9
        + [pl.BlockSpec(memory_space=pltpu.HBM)] * 8,
        out_specs=[whole()] + [pl.BlockSpec(memory_space=pltpu.HBM)] * 2,
        out_shape=[
            spec(512, 640, f32),
            spec(2, 3584, 128, bf16),
            spec(2, 3584, 128, bf16),
        ],
        scratch_shapes=[
            pltpu.VMEM((640, 1024), bf16),
            pltpu.VMEM((640, 512), bf16),
            pltpu.VMEM((4, 3584, 128), bf16),
            pltpu.SemaphoreType.DMA((12,)),
        ],
        compiler_params=params(24),
        cost_estimate=cost(3_400_000_000, 14_000_000),
    )(place, normed, back_q, back_kv, attended, back_attn, halo, own, gain_mid, gain_head, *shares)


def finish_kernel(own, back_own, returned, back_middle, gains, grad_in):
    x = own[...].astype(f32)
    e = back_own[...] + returned[...].astype(f32)
    grad_in[...] = (back_middle[...] + norm_back(x, inverse_rms(x), gains[0:1], e)).astype(bf16)


def finish(own, back_own, returned, back_middle, gains):
    row = lambda i: (i, 0)
    return pl.pallas_call(
        finish_kernel,
        name="finish",
        grid=(4,),
        in_specs=[pl.BlockSpec((128, 640), row)] * 4 + [pl.BlockSpec((8, 640), lambda i: (0, 0))],
        out_specs=pl.BlockSpec((128, 640), row),
        out_shape=spec(512, 640, bf16),
        compiler_params=params(10),
        cost_estimate=cost(4_000_000, 5_000_000),
    )(own, back_own, returned, back_middle, gains)


def rope_tables(offsets):
    powers = jnp.arange(128, dtype=f32) * (2.0 / 256)
    row = jnp.arange(512, dtype=jnp.int32)
    every = jnp.concatenate([offsets[0] - 512 + row, offsets])
    angles = every.astype(f32)[:, None] * (rope_base ** (-powers))[None, :]
    return jnp.cos(angles), jnp.sin(angles)


def unpack_kernel(spot, a0, a1, a2, a3, b0, b1, b2, b3, *rest):
    outs, gains, held, (ffn, attn, semaphores) = rest[:7], rest[7], rest[8:15], rest[15:]
    q, k, v, out, gate, up, down = held
    x, y = spot[0], spot[1]
    copies = []
    for half, pieces in enumerate(((a0, a1, a2, a3), (b0, b1, b2, b3))):
        for i in range(4):
            for j in range(4):
                first, second = (x, y) if half == 0 else (y, x)
                block = 16 * half + lax.rem(first - i + 4, 4) * 4 + lax.rem(second - j + 4, 4)
                n = (half * 4 + i) * 4 + j
                for m, (into, start, rows) in enumerate(((ffn, 0, 240), (attn, 240, 112))):
                    copies.append(
                        pltpu.make_async_copy(
                            pieces[i].at[j, pl.ds(start, rows), :],
                            into.at[pl.ds(pl.multiple_of(block * rows, 16), rows), :],
                            semaphores.at[2 * n + m],
                        )
                    )
    for copy in copies:
        copy.start()
    for copy in copies:
        copy.wait()
    outward = []

    def leave(n):
        copy = pltpu.make_async_copy(held[n], outs[n], semaphores.at[64 + n])
        copy.start()
        outward.append(copy)

    for n, into, flat, first, count in (
        (4, gate, ffn, 0, 16),
        (5, up, ffn, 2560, 16),
        (0, q, attn, 0, 8),
        (1, k, attn, 1280, 2),
        (2, v, attn, 1600, 2),
    ):
        for b in range(count):
            at = first + 160 * b
            into[:, 128 * b : 128 * b + 128] = flat[at : at + 160, :].astype(f32)
        leave(n)
    for n, into, flat, first, count in ((6, down, ffn, 5120, 4), (3, out, attn, 1920, 2)):
        for b in range(count):
            at = first + 640 * b
            into[128 * b : 128 * b + 128, :] = flat[at : at + 640, :].astype(f32).T
        leave(n)
    gains[...] = attn[3200:3216, :].astype(f32)
    for copy in outward:
        copy.wait()


def unpack(spot, pieces):
    shapes = [(160, 1024), (160, 256), (160, 256), (256, 640), (160, 2048), (160, 2048), (512, 640)]
    return pl.pallas_call(
        unpack_kernel,
        name="unpack",
        in_specs=[pl.BlockSpec(memory_space=pltpu.SMEM)] + [pl.BlockSpec(memory_space=pltpu.HBM)] * 8,
        out_specs=[pl.BlockSpec(memory_space=pltpu.HBM)] * 7 + [whole()],
        out_shape=[spec(*shape, f32) for shape in shapes] + [spec(16, 128, f32)],
        scratch_shapes=[pltpu.VMEM(shape, f32) for shape in shapes]
        + [
            pltpu.VMEM((7680, 128), bf16),
            pltpu.VMEM((3584, 128), bf16),
            pltpu.SemaphoreType.DMA((71,)),
        ],
        compiler_params=params(14),
        cost_estimate=cost(4_000_000, 11_000_000),
    )(spot, *pieces)


def sum_of(parts):
    whole = parts[0].astype(f32)
    for part in parts[1:]:
        whole = whole + part.astype(f32)
    return whole.astype(bf16)


def turn_around(position, d):
    return lax.rem(position + d, 4)


def first_kernel(spot, kept_ffn, got_ffn, kept_attn, got_attn, *outs):
    for half in range(2):
        for i, d in enumerate((0, 1, 3, 2)):
            at = turn_around(spot[half], d)
            out = outs[4 * half + i]
            for z in range(2):
                for j in range(4):
                    out[z, j, :240] = sum_of([r[z, half, at, j] for r in (kept_ffn, got_ffn)])
                    out[z, j, 240:] = sum_of([r[z, half, at, j] for r in (kept_attn, got_attn)])


def first_sums(spot, kept_ffn, got_ffn, kept_attn, got_attn):
    ins = [p.reshape(2, 2, 4, 4, p.shape[1] // 32, 128) for p in (kept_ffn, got_ffn, kept_attn, got_attn)]
    return pl.pallas_call(
        first_kernel,
        name="first_sums",
        in_specs=[pl.BlockSpec(memory_space=pltpu.SMEM)] + [whole()] * 4,
        out_specs=[whole()] * 8,
        out_shape=[spec(2, 4, 352, 128, bf16)] * 8,
        compiler_params=params(24),
        cost_estimate=cost(3_000_000, 17_000_000),
    )(spot, *ins)


def second_kernel(spot, *refs):
    ins, outs = refs[:8], refs[8:]
    for half in range(2):
        parts = ins[4 * half : 4 * half + 4]
        for i, d in enumerate((0, 1, 3, 2)):
            at = turn_around(spot[1 - half], d)
            for z in range(2):
                outs[4 * half + i][z] = sum_of([r[z, at] for r in parts])


def second_sums(spot, parts):
    return pl.pallas_call(
        second_kernel,
        name="second_sums",
        in_specs=[pl.BlockSpec(memory_space=pltpu.SMEM)] + [whole()] * 8,
        out_specs=[whole()] * 8,
        out_shape=[spec(2, 352, 128, bf16)] * 8,
        compiler_params=params(12),
        cost_estimate=cost(1_000_000, 7_200_000),
    )(spot, *parts)


def third_kernel(place, *refs):
    ins, (mine, other) = refs[:8], refs[8:]
    z = lax.div(place[0], 2)
    for half in range(2):
        parts = ins[4 * half : 4 * half + 4]
        mine[half] = sum_of([r[z] for r in parts])
        other[half] = sum_of([r[1 - z] for r in parts])


def third_sums(place, parts):
    return pl.pallas_call(
        third_kernel,
        name="third_sums",
        in_specs=[pl.BlockSpec(memory_space=pltpu.SMEM)] + [whole()] * 8,
        out_specs=[whole()] * 2,
        out_shape=[spec(2, 352, 128, bf16)] * 2,
        compiler_params=params(10),
        cost_estimate=cost(1_000_000, 1_800_000),
    )(place, *parts)


def fourth_kernel(p0, p1, p2, p3, a, b):
    for half, out in enumerate((a, b)):
        out[...] = sum_of([p0[half], p1[half], p2[half], p3[half]])


def fourth_sums(parts):
    return pl.pallas_call(
        fourth_kernel,
        name="fourth_sums",
        in_specs=[whole()] * 4,
        out_specs=[whole()] * 2,
        out_shape=[spec(352, 128, bf16)] * 2,
        compiler_params=params(10),
        cost_estimate=cost(1_000_000, 900_000),
    )(*parts)


def seq_index(z, x, y):
    return (z % 2 * 4 + x % 4) * 4 + y % 4


def along_xy(dx, dy):
    return [
        (seq_index(z, x, y), seq_index(z, x + dx, y + dy))
        for z in range(2)
        for x in range(4)
        for y in range(4)
    ]


def along_z(step):
    pairs = []
    for s in range(32):
        for f in range(4):
            z = s // 16 * 2 + f // 2
            t = step(z)
            pairs.append((s * 4 + f, (t // 2 * 16 + s % 16) * 4 + t % 2 * 2 + f % 2))
    return pairs


def swap_core(value):
    return lax.ppermute(value, "fsdp", [(0, 1), (1, 0), (2, 3), (3, 2)])


def swap_near(value):
    return lax.ppermute(value, "fsdp", [(0, 2), (1, 3), (2, 0), (3, 1)])


def swap_across(value):
    return lax.ppermute(value, "fsdp", [(0, 3), (1, 2), (2, 1), (3, 0)])


def swap_far(value):
    return lax.ppermute(value, ("seq", "fsdp"), along_z(lambda z: 3 - z))


def swap_hi(value):
    return lax.ppermute(value, "seq", [(s, (s + 16) % 32) for s in range(32)])


def move_x(value, d):
    return lax.ppermute(value, "seq", along_xy(d, 0))


def move_y(value, d):
    return lax.ppermute(value, "seq", along_xy(0, d))


def shifted(value, steps):
    first, last = (max(0, -steps), min(32, 32 - steps))
    return lax.ppermute(value, "seq", [(source, source + steps) for source in range(first, last)])


steps = (1, 3, 2)


def move_first(parts):
    return (
        [parts[0]]
        + [move_x(p, d) for p, d in zip(parts[1:4], steps)]
        + [parts[4]]
        + [move_y(p, d) for p, d in zip(parts[5:8], steps)]
    )


def move_second(parts):
    return (
        [parts[0]]
        + [move_y(p, d) for p, d in zip(parts[1:4], steps)]
        + [parts[4]]
        + [move_x(p, d) for p, d in zip(parts[5:8], steps)]
    )


def together(*groups):
    leaves, tree = jax.tree.flatten(groups)
    return jax.tree.unflatten(tree, lax.optimization_barrier(tuple(leaves)))


def body(
    hidden_in,
    cotangent,
    positions,
    query_weight,
    key_weight,
    value_weight,
    output_weight,
    gate_weight,
    up_weight,
    down_weight,
    norm_in,
    norm_attn,
    norm_ffn_in,
    norm_ffn_out,
    norm_query,
    norm_key,
):
    s = lax.axis_index("seq")
    f = lax.axis_index("fsdp")
    x, y, z_lo, core = s // 4 % 4, s % 4, f // 2, f % 2
    place = f.astype(jnp.int32).reshape(1)
    spot = jnp.stack([x, y]).astype(jnp.int32)
    own = hidden_in[0]
    upstream = cotangent[0]
    offsets = positions[0]

    q_partner = swap_near(query_weight)
    kv = jnp.concatenate([key_weight, value_weight], axis=1)
    kv_partner = swap_far(kv)
    halo = shifted(own, 1)
    rows = (norm_in, norm_attn, norm_ffn_in, norm_ffn_out, norm_query, norm_key)
    q_partner, rows = together(q_partner, rows)
    tile = pack(rows)
    tiles = [tile, swap_core(tile), swap_near(tile), swap_across(tile)]
    tiles, wg, wu = together(tiles, gate_weight, up_weight)
    wg_partner, wu_partner = swap_near(wg), swap_far(wu)
    tiles = [
        jnp.where(
            j // 2 == z_lo,
            jnp.where(j % 2 == core, tiles[0], tiles[1]),
            jnp.where(j % 2 == core, tiles[2], tiles[3]),
        )
        for j in range(4)
    ]
    gains = jnp.concatenate([t[:, :160] for t in tiles], axis=1)
    head_gains = jnp.concatenate([t[:, :64] for t in tiles], axis=1)
    q_shares = (query_weight, swap_core(query_weight), q_partner, swap_core(q_partner))
    kv_shares = (kv, swap_core(kv), kv_partner, swap_core(kv_partner))
    q_shares, kv_shares, halo, wo, wd = together(
        q_shares, kv_shares, halo, output_weight, down_weight
    )
    wo_partner, wd_partner = swap_near(wo), swap_far(wd)

    cosine, sine = rope_tables(offsets)
    column = offsets[:, None]
    normed, q, k, v, q_proj, k_proj = project(
        place, halo, own, gains, head_gains, q_shares, kv_shares, cosine, sine
    )
    (q, k, v), wg_partner, wu_partner = together((q, k, v), wg_partner, wu_partner)
    attended, level = attend(q, k, v, column)
    own_weights = (wo, wg, wu, wd)
    partners = (wo_partner, wg_partner, wu_partner, wd_partner)
    attended, own_weights = together(attended, own_weights)
    siblings = [swap_core(w) for w in own_weights]
    shares = []
    for share, sibling, partner in zip(own_weights, siblings, partners):
        attended, partner = together(attended, partner)
        shares += [share, sibling, partner, swap_core(partner)]
    layer_out, back_middle, back_attn, back_attended, gain_mid, kept, sent = middle_part(
        place, own, attended, upstream, gains, shares
    )
    got = swap_core(sent)
    back_q, back_kv, gain_head, back_halo = attend_back(
        q,
        k,
        v,
        column,
        level,
        back_attended,
        q_proj,
        k_proj,
        head_gains,
        cosine,
        sine,
        place,
        kv_shares,
    )
    back_own, kept_attn, sent = weights_part(
        place,
        normed,
        back_q,
        back_kv,
        attended,
        back_attn,
        halo,
        own,
        gain_mid,
        gain_head,
        q_shares + kv_shares,
    )
    got_attn = swap_core(sent)
    first = move_first(first_sums(spot, kept, got, kept_attn, got_attn))
    mine, other = third_sums(place, move_second(second_sums(spot, first)))
    returned = shifted(back_halo, -1)
    a, b = fourth_sums([mine, swap_near(other), swap_far(other), swap_hi(mine)])
    a, b, returned = together(a, b, returned)
    a = jnp.stack([a] + [move_y(a, d) for d in (1, 2, 3)])
    b = jnp.stack([b] + [move_x(b, d) for d in (1, 2, 3)])
    a, b = together(a, b)
    pieces = [a] + [move_x(a, d) for d in (1, 2, 3)] + [b] + [move_y(b, d) for d in (1, 2, 3)]
    grad_q, grad_k, grad_v, grad_o, grad_g, grad_u, grad_d, tile = unpack(spot, pieces)
    grad_in = finish(own, back_own, returned, back_middle, gains)
    wide = jnp.concatenate([tile[0:4], tile[4:8, :32]], axis=1)
    return (
        layer_out[None],
        grad_in[None],
        grad_q,
        grad_k,
        grad_v,
        grad_o,
        grad_g,
        grad_u,
        grad_d,
        wide[0],
        wide[1],
        wide[2],
        wide[3],
        tile[8, :64],
        tile[9, :64],
    )


def solution(mesh):
    three = P("fsdp", "seq", None)
    two = P("fsdp", None)
    one = P("fsdp")
    return jax.shard_map(
        body,
        mesh=mesh,
        in_specs=(three, three, P("fsdp", "seq")) + (two,) * 7 + (one,) * 6,
        out_specs=(three, three) + (two,) * 7 + (one,) * 6,
        check_vma=False,
    )
```

```python
import jax
import jax.numpy as jnp
from jax import lax
from jax.experimental import pallas as pl
from jax.experimental.pallas import tpu as pltpu
from jax.sharding import PartitionSpec as P

WINDOW = 512
epsilon = 1e-06
rope_base = 10000.0
masked_value = -1e30
bf16 = jnp.bfloat16
f32 = jnp.float32

rows_out = ((1,), (0,))
rows_both = ((1,), (1,))
cols_both = ((0,), (0,))


def dot(a, b, dims=rows_out):
    return lax.dot_general(a, b, (dims, ((), ())), preferred_element_type=f32)


def spec(*shape):
    return jax.ShapeDtypeStruct(shape[:-1], shape[-1])


def whole():
    return pl.BlockSpec(memory_space=pltpu.VMEM)


def params(mib):
    return pltpu.CompilerParams(vmem_limit_bytes=mib * 1024 * 1024)


def cost(flops, moved, exps=0):
    return pl.CostEstimate(flops=flops, bytes_accessed=moved, transcendentals=exps)


def inverse_rms(v):
    return lax.rsqrt(jnp.mean(v * v, axis=-1, keepdims=True) + epsilon)


def norm_back(v, r, gain, e):
    scaled = gain * e
    return r * scaled - v * (r * r * r * jnp.mean(v * scaled, axis=-1, keepdims=True))


def turn(v, cosine, sine):
    a, b = v[:, :128], v[:, 128:]
    return jnp.concatenate([a * cosine - b * sine, b * cosine + a * sine], axis=1)


def turn_back(v, cosine, sine):
    a, b = v[:, :128], v[:, 128:]
    return jnp.concatenate([a * cosine + b * sine, b * cosine - a * sine], axis=1)


def assemble(pieces, into, place, semaphores, first):
    rows = into.shape[0] // 4
    copies = []
    for r in range(4):
        at = pl.ds(pl.multiple_of((place ^ r) * rows, rows), rows)
        copies.append(
            pltpu.make_async_copy(
                pieces[r],
                into.at[at, :],
                semaphores.at[first + r],
            )
        )
    for copy in copies:
        copy.start()
    return copies


def split_out(grads, kept, sent, place, semaphores, first):
    core = lax.rem(place, 2)
    copies = []
    for z in range(2):
        copies.append(
            pltpu.make_async_copy(
                grads.at[2 * z + 1 - core], sent.at[z], semaphores.at[first + 2 * z]
            )
        )
        copies.append(
            pltpu.make_async_copy(
                grads.at[2 * z + core], kept.at[z], semaphores.at[first + 2 * z + 1]
            )
        )
    for copy in copies:
        copy.start()
    return copies


def pack_kernel(g0, g1, g2, g3, g4, g5, out, *rest):
    held, semaphores = rest[:6], rest[6]
    copies = [
        pltpu.make_async_copy(source, into, semaphores.at[i])
        for i, (source, into) in enumerate(zip((g0, g1, g2, g3, g4, g5), held))
    ]
    for copy in copies:
        copy.start()
    out[...] = jnp.zeros_like(out)
    for copy in copies:
        copy.wait()
    for i, ref in enumerate(held):
        n = ref.shape[0]
        out[i : i + 1, :n] = ref[...].astype(f32).reshape(1, n)


def pack(rows):
    return pl.pallas_call(
        pack_kernel,
        name="pack",
        in_specs=[pl.BlockSpec(memory_space=pltpu.HBM)] * 6,
        out_specs=whole(),
        out_shape=spec(8, 256, f32),
        scratch_shapes=[pltpu.VMEM(row.shape, bf16) for row in rows]
        + [pltpu.SemaphoreType.DMA((6,))],
        compiler_params=params(4),
        cost_estimate=cost(100_000, 20_000),
    )(*rows)


def project_kernel(
    place,
    halo,
    own,
    gains,
    head_gains,
    q0,
    q1,
    q2,
    q3,
    kv0,
    kv1,
    kv2,
    kv3,
    cosine,
    sine,
    normed,
    q,
    k,
    v,
    q_proj,
    k_proj,
    wq,
    wkv,
    semaphores,
):
    i = pl.program_id(0)

    @pl.when(i == 0)
    def _():
        copies = assemble((kv0, kv1, kv2, kv3), wkv, place[0], semaphores, 0)
        copies += assemble((q0, q1, q2, q3), wq, place[0], semaphores, 4)
        for copy in copies:
            copy.wait()

    x = jnp.where(i < 2, halo[...], own[...]).astype(f32)
    n = (x * inverse_rms(x) * gains[0:1]).astype(bf16)
    normed[...] = n
    c, s = cosine[...], sine[...]
    kv = dot(n, wkv[...])
    kp = kv[:, :256]
    k_proj[...] = kp
    v[...] = kv[:, 256:].astype(bf16)
    k[...] = turn(kp * inverse_rms(kp) * head_gains[5:6], c, s).astype(bf16)

    @pl.when(i >= 2)
    def _():
        for h in range(4):
            cols = slice(256 * h, 256 * h + 256)
            qp = dot(n, wq[:, cols])
            q_proj[:, cols] = qp
            q[:, cols] = turn(qp * inverse_rms(qp) * head_gains[4:5], c, s).astype(bf16)


def project(place, halo, own, gains, head_gains, q_shares, kv_shares, cosine, sine):
    late = lambda i: (jnp.maximum(i - 2, 0), 0)
    row = lambda i: (i, 0)
    fixed = lambda i: (0, 0)
    return pl.pallas_call(
        project_kernel,
        name="project",
        grid=(4,),
        in_specs=[
            pl.BlockSpec(memory_space=pltpu.SMEM),
            pl.BlockSpec((256, 640), lambda i: (jnp.minimum(i, 1), 0)),
            pl.BlockSpec((256, 640), late),
            pl.BlockSpec((8, 640), fixed),
            pl.BlockSpec((8, 256), fixed),
        ]
        + [pl.BlockSpec(memory_space=pltpu.HBM)] * 8
        + [pl.BlockSpec((256, 128), row)] * 2,
        out_specs=[
            pl.BlockSpec((256, 640), row),
            pl.BlockSpec((256, 1024), late),
            pl.BlockSpec((256, 256), row),
            pl.BlockSpec((256, 256), row),
            pl.BlockSpec((256, 1024), late),
            pl.BlockSpec((256, 256), row),
        ],
        out_shape=[
            spec(1024, 640, bf16),
            spec(512, 1024, bf16),
            spec(1024, 256, bf16),
            spec(1024, 256, bf16),
            spec(512, 1024, f32),
            spec(1024, 256, f32),
        ],
        scratch_shapes=[
            pltpu.VMEM((640, 1024), bf16),
            pltpu.VMEM((640, 512), bf16),
            pltpu.SemaphoreType.DMA((8,)),
        ],
        compiler_params=params(14),
        cost_estimate=cost(1_350_000_000, 9_000_000),
    )(place, halo, own, gains, head_gains, *q_shares, *kv_shares, cosine, sine)


def visible_keys(offsets):
    distance = (
        lax.broadcasted_iota(jnp.int32, (256, 768), 0)
        + 512
        - lax.broadcasted_iota(jnp.int32, (256, 768), 1)
    )
    return (distance >= 0) & (distance < WINDOW) & (distance <= offsets)


def attend_kernel(q, k, v, offsets, attended, level):
    t = pl.program_id(0)
    near = pl.ds(pl.multiple_of(t * 256, 256), 768)
    keys, values = k[near, :], v[near, :]
    visible = visible_keys(offsets[...])
    for h in range(4):
        cols = slice(256 * h, 256 * h + 256)
        scores = jnp.where(visible, dot(q[:, cols], keys, rows_both) * 0.0625, masked_value)
        top = jnp.max(scores, axis=-1, keepdims=True)
        e = jnp.exp(scores - top)
        total = jnp.sum(e, axis=-1, keepdims=True)
        level[h] = top + jnp.log(total)
        probs = (e * (1.0 / total)).astype(bf16)
        attended[:, cols] = dot(probs, values).astype(bf16)


def attend(q, k, v, offsets):
    row = lambda i: (i, 0)
    fixed = lambda i: (0, 0)
    return pl.pallas_call(
        attend_kernel,
        name="attend",
        grid=(2,),
        in_specs=[
            pl.BlockSpec((256, 1024), row),
            pl.BlockSpec((1024, 256), fixed),
            pl.BlockSpec((1024, 256), fixed),
            pl.BlockSpec((256, 1), row),
        ],
        out_specs=[
            pl.BlockSpec((256, 1024), row),
            pl.BlockSpec((4, 256, 1), lambda i: (0, i, 0)),
        ],
        out_shape=[spec(512, 1024, bf16), spec(4, 512, 1, f32)],
        compiler_params=params(10),
        cost_estimate=cost(1_700_000_000, 4_000_000, 2_000_000),
    )(q, k, v, offsets)


def middle_kernel(
    place,
    x_ref,
    attended,
    upstream,
    gains,
    o0,
    o1,
    o2,
    o3,
    g0,
    g1,
    g2,
    g3,
    u0,
    u1,
    u2,
    u3,
    d0,
    d1,
    d2,
    d3,
    layer_out,
    back_middle,
    back_attn,
    back_attended,
    gain_grads,
    kept,
    sent,
    ffn_in,
    kept_a,
    kept_b,
    hidden,
    back_out,
    in_turned,
    out_turned,
    back_gate,
    back_up,
    wo,
    wg,
    wu,
    wd,
    grads,
    semaphores,
):
    output_copies = assemble((o0, o1, o2, o3), wo, place[0], semaphores, 0)
    gate_copies = assemble((g0, g1, g2, g3), wg, place[0], semaphores, 4)
    up_copies = assemble((u0, u1, u2, u3), wu, place[0], semaphores, 8)
    down_copies = assemble((d0, d1, d2, d3), wd, place[0], semaphores, 12)
    for copy in output_copies:
        copy.wait()
    g_attn, g_in, g_out = gains[1:2], gains[2:3], gains[3:4]
    ao = dot(attended[...], wo[...])
    r1 = inverse_rms(ao)
    mid = x_ref[...].astype(f32) + ao * r1 * g_attn
    r2 = inverse_rms(mid)
    ffn_in[...] = (mid * r2 * g_in).astype(bf16)
    for copy in gate_copies + up_copies:
        copy.wait()

    for j in range(8):
        cols = slice(256 * j, 256 * j + 256)
        u = dot(ffn_in[...], wg[:, cols])
        up = dot(ffn_in[...], wu[:, cols])
        root = 0.7978845608028654
        square = u * u
        t = jnp.tanh(u * (root + (root * 0.044715) * square))
        half = 0.5 + 0.5 * t
        act = u * half
        slope = half + act * (1.0 - t) * (root + (3 * 0.044715 * root) * square)
        hidden[:, cols] = (act * up).astype(bf16)
        kept_a[:, cols] = act
        kept_b[:, cols] = up * slope

    for copy in down_copies:
        copy.wait()
    fo = dot(hidden[...], wd[...])
    r3 = inverse_rms(fo)
    layer_out[...] = (mid + fo * r3 * g_out).astype(bf16)
    g = upstream[...].astype(f32)
    gain_grads[2:3] = jnp.sum(fo * r3 * g, axis=0, keepdims=True)
    bfo = norm_back(fo, r3, g_out, g)
    back_out[...] = bfo.astype(bf16)
    out_turned[...] = back_out[...].T
    in_turned[...] = ffn_in[...].T

    for j in range(8):
        cols = slice(256 * j, 256 * j + 256)
        bh = dot(back_out[...], wd[cols, :], rows_both)
        bu = (bh * kept_a[:, cols]).astype(bf16)
        bg = (bh * kept_b[:, cols]).astype(bf16)
        back_gate[:, cols] = bg
        back_up[:, cols] = bu

    for base, right in ((0, back_gate), (2560, back_up)):
        for j in range(2048 // 512):
            part = dot(in_turned[...], right[:, 512 * j : 512 * j + 512]).astype(bf16)
            for b in range(512 // 128):
                at = base + (512 // 128 * j + b) * 160
                for f in range(4):
                    grads[f, at : at + 160, :] = part[
                        160 * f : 160 * f + 160, 128 * b : 128 * b + 128
                    ]
    for f in range(4):
        part = dot(out_turned[...], hidden[:, 512 * f : 512 * f + 512]).astype(bf16)
        for b in range(4):
            at = 5120 + 640 * b
            grads[f, at : at + 640, :] = part[:, 128 * b : 128 * b + 128]

    outward = split_out(grads, kept, sent, place[0], semaphores, 16)
    e = dot(back_gate[...], wg[...], rows_both) + dot(back_up[...], wu[...], rows_both)
    gain_grads[1:2] = jnp.sum(mid * r2 * e, axis=0, keepdims=True)
    bm = g + norm_back(mid, r2, g_in, e)
    back_middle[...] = bm
    gain_grads[0:1] = jnp.sum(ao * r1 * bm, axis=0, keepdims=True)
    bao = norm_back(ao, r1, g_attn, bm).astype(bf16)
    back_attn[...] = bao
    back_attended[...] = dot(bao, wo[...], rows_both).astype(bf16)
    for copy in outward:
        copy.wait()


def middle_part(place, x, attended, upstream, gains, shares):
    return pl.pallas_call(
        middle_kernel,
        name="middle_part",
        in_specs=[pl.BlockSpec(memory_space=pltpu.SMEM)]
        + [whole()] * 4
        + [pl.BlockSpec(memory_space=pltpu.HBM)] * 16,
        out_specs=[whole()] * 5 + [pl.BlockSpec(memory_space=pltpu.HBM)] * 2,
        out_shape=[
            spec(512, 640, bf16),
            spec(512, 640, f32),
            spec(512, 640, bf16),
            spec(512, 1024, bf16),
            spec(8, 640, f32),
            spec(2, 7680, 128, bf16),
            spec(2, 7680, 128, bf16),
        ],
        scratch_shapes=[
            pltpu.VMEM((512, 640), bf16),
            pltpu.VMEM((512, 2048), f32),
            pltpu.VMEM((512, 2048), f32),
            pltpu.VMEM((512, 2048), bf16),
            pltpu.VMEM((512, 640), bf16),
            pltpu.VMEM((640, 512), bf16),
            pltpu.VMEM((640, 512), bf16),
            pltpu.VMEM((512, 2048), bf16),
            pltpu.VMEM((512, 2048), bf16),
            pltpu.VMEM((1024, 640), bf16),
            pltpu.VMEM((640, 2048), bf16),
            pltpu.VMEM((640, 2048), bf16),
            pltpu.VMEM((2048, 640), bf16),
            pltpu.VMEM((4, 7680, 128), bf16),
            pltpu.SemaphoreType.DMA((20,)),
        ],
        compiler_params=params(44),
        cost_estimate=cost(13_400_000_000, 23_000_000, 1_000_000),
    )(place, x, attended, upstream, gains, *shares)


def attend_back_kernel(
    q,
    k,
    v,
    offsets,
    level,
    back_attended,
    q_proj,
    k_proj,
    head_gains,
    cosine,
    sine,
    place,
    kv0,
    kv1,
    kv2,
    kv3,
    back_q,
    back_kv,
    gain_grads,
    back_halo,
    sum_k,
    sum_v,
    wkv,
    semaphores,
):
    t = pl.program_id(0)

    @pl.when(t == 0)
    def _():
        for copy in assemble((kv0, kv1, kv2, kv3), wkv, place[0], semaphores, 0):
            copy.wait()
        sum_k[...] = jnp.zeros_like(sum_k)
        sum_v[...] = jnp.zeros_like(sum_v)
        gain_grads[...] = jnp.zeros_like(gain_grads)

    near = pl.ds(pl.multiple_of(t * 256, 256), 768)
    mine = pl.ds(pl.multiple_of(t * 256 + 512, 256), 256)
    keys, values = k[near, :], v[near, :]
    visible = visible_keys(offsets[...])
    c, s = cosine[mine, :], sine[mine, :]
    for h in range(4):
        cols = slice(256 * h, 256 * h + 256)
        qh, bah = q[:, cols], back_attended[:, cols]
        scores = jnp.where(visible, dot(qh, keys, rows_both) * 0.0625, masked_value)
        probs = jnp.exp(scores - level[h])
        bp = dot(bah, values, rows_both)
        inner = jnp.sum(probs * bp, axis=-1, keepdims=True)
        bs = (probs * (bp - inner)).astype(bf16)
        sum_k[near, :] += dot(bs, qh, cols_both)
        sum_v[near, :] += dot(probs.astype(bf16), bah, cols_both)
        e = turn_back(dot(bs, keys) * 0.0625, c, s)
        qp = q_proj[:, cols]
        r = inverse_rms(qp)
        gain_grads[0:1] += jnp.sum(qp * r * e, axis=0, keepdims=True)
        back_q[:, cols] = norm_back(qp, r, head_gains[4:5], e).astype(bf16)

    @pl.when(t == 1)
    def _():
        e = turn_back(sum_k[...] * 0.0625, cosine[...], sine[...])
        kp = k_proj[...]
        r = inverse_rms(kp)
        gain_grads[1:2] = jnp.sum(kp * r * e, axis=0, keepdims=True)
        back_kv[:, :256] = norm_back(kp, r, head_gains[5:6], e).astype(bf16)
        back_kv[:, 256:] = sum_v[...].astype(bf16)
        back_halo[...] = dot(back_kv[:512, :], wkv[...], rows_both).astype(bf16)


def attend_back(
    q, k, v, offsets, level, back_attended, q_proj, k_proj, head_gains, cosine, sine, place, shares
):
    row = lambda i: (i, 0)
    fixed = lambda i: (0, 0)
    return pl.pallas_call(
        attend_back_kernel,
        name="attend_back",
        grid=(2,),
        in_specs=[
            pl.BlockSpec((256, 1024), row),
            pl.BlockSpec((1024, 256), fixed),
            pl.BlockSpec((1024, 256), fixed),
            pl.BlockSpec((256, 1), row),
            pl.BlockSpec((4, 256, 1), lambda i: (0, i, 0)),
            pl.BlockSpec((256, 1024), row),
            pl.BlockSpec((256, 1024), row),
            pl.BlockSpec((1024, 256), fixed),
            pl.BlockSpec((8, 256), fixed),
            pl.BlockSpec((1024, 128), fixed),
            pl.BlockSpec((1024, 128), fixed),
            pl.BlockSpec(memory_space=pltpu.SMEM),
        ]
        + [pl.BlockSpec(memory_space=pltpu.HBM)] * 4,
        out_specs=[
            pl.BlockSpec((256, 1024), row),
            pl.BlockSpec((1024, 512), fixed),
            pl.BlockSpec((8, 256), fixed),
            pl.BlockSpec((512, 640), fixed),
        ],
        out_shape=[
            spec(512, 1024, bf16),
            spec(1024, 512, bf16),
            spec(8, 256, f32),
            spec(512, 640, bf16),
        ],
        scratch_shapes=[
            pltpu.VMEM((1024, 256), f32),
            pltpu.VMEM((1024, 256), f32),
            pltpu.VMEM((640, 512), bf16),
            pltpu.SemaphoreType.DMA((4,)),
        ],
        compiler_params=params(16),
        cost_estimate=cost(4_300_000_000, 10_000_000, 2_000_000),
    )(
        q, k, v, offsets, level, back_attended, q_proj, k_proj, head_gains, cosine, sine, place, *shares
    )


def weights_kernel(
    place,
    normed,
    back_q,
    back_kv,
    attended,
    back_attn,
    halo,
    own,
    gain_mid,
    gain_head,
    q0,
    q1,
    q2,
    q3,
    kv0,
    kv1,
    kv2,
    kv3,
    back_own,
    kept,
    sent,
    wq,
    wkv,
    grads,
    semaphores,
):
    copies = assemble((kv0, kv1, kv2, kv3), wkv, place[0], semaphores, 0)
    copies += assemble((q0, q1, q2, q3), wq, place[0], semaphores, 4)
    turned = normed[...].astype(f32).T.astype(bf16)
    bq, bkv = back_q[...], back_kv[...]
    part = dot(turned[:, 512:], bq).astype(bf16)
    for b in range(8):
        for f in range(4):
            grads[f, 160 * b : 160 * b + 160, :] = part[
                160 * f : 160 * f + 160, 128 * b : 128 * b + 128
            ]
    part = dot(turned, bkv).astype(bf16)
    for b in range(4):
        for f in range(4):
            grads[f, 1280 + 160 * b : 1440 + 160 * b, :] = part[
                160 * f : 160 * f + 160, 128 * b : 128 * b + 128
            ]
    turned = back_attn[...].astype(f32).T.astype(bf16)
    part = dot(turned, attended[...]).astype(bf16)
    for f in range(4):
        for b in range(2):
            grads[f, 1920 + 640 * b : 2560 + 640 * b, :] = part[
                :, 256 * f + 128 * b : 256 * f + 128 * b + 128
            ]
    for copy in copies:
        copy.wait()
    e = dot(bkv[:512], wkv[...], rows_both)
    x = halo[...].astype(f32)
    grad = jnp.sum(x * inverse_rms(x) * e, axis=0, keepdims=True)
    e = dot(bkv[512:], wkv[...], rows_both) + dot(bq, wq[...], rows_both)
    back_own[...] = e
    x = own[...].astype(f32)
    grad = grad + jnp.sum(x * inverse_rms(x) * e, axis=0, keepdims=True)
    each = jnp.concatenate([grad, gain_mid[0:3]], axis=0)
    heads = gain_head[0:2]
    for f in range(4):
        share = each[:, 160 * f : 160 * f + 160]
        rest = jnp.concatenate([share[:, 128:], jnp.zeros((4, 96), f32)], axis=1)
        ends = jnp.concatenate([heads[:, 64 * f : 64 * f + 64], jnp.zeros((2, 64), f32)], axis=1)
        tile = jnp.concatenate([share[:, :128], rest, ends, jnp.zeros((6, 128), f32)], axis=0)
        grads[f, 3200:3216, :] = tile.astype(bf16)
        grads[f, 3216:, :] = jnp.zeros((368, 128), bf16)
    for copy in split_out(grads, kept, sent, place[0], semaphores, 8):
        copy.wait()


def weights_part(
    place, normed, back_q, back_kv, attended, back_attn, halo, own, gain_mid, gain_head, shares
):
    return pl.pallas_call(
        weights_kernel,
        name="weights_part",
        in_specs=[pl.BlockSpec(memory_space=pltpu.SMEM)]
        + [whole()] * 9
        + [pl.BlockSpec(memory_space=pltpu.HBM)] * 8,
        out_specs=[whole()] + [pl.BlockSpec(memory_space=pltpu.HBM)] * 2,
        out_shape=[
            spec(512, 640, f32),
            spec(2, 3584, 128, bf16),
            spec(2, 3584, 128, bf16),
        ],
        scratch_shapes=[
            pltpu.VMEM((640, 1024), bf16),
            pltpu.VMEM((640, 512), bf16),
            pltpu.VMEM((4, 3584, 128), bf16),
            pltpu.SemaphoreType.DMA((12,)),
        ],
        compiler_params=params(24),
        cost_estimate=cost(3_400_000_000, 14_000_000),
    )(place, normed, back_q, back_kv, attended, back_attn, halo, own, gain_mid, gain_head, *shares)


def finish_kernel(own, back_own, returned, back_middle, gains, grad_in):
    x = own[...].astype(f32)
    e = back_own[...] + returned[...].astype(f32)
    grad_in[...] = (back_middle[...] + norm_back(x, inverse_rms(x), gains[0:1], e)).astype(bf16)


def finish(own, back_own, returned, back_middle, gains):
    row = lambda i: (i, 0)
    return pl.pallas_call(
        finish_kernel,
        name="finish",
        grid=(4,),
        in_specs=[pl.BlockSpec((128, 640), row)] * 4 + [pl.BlockSpec((8, 640), lambda i: (0, 0))],
        out_specs=pl.BlockSpec((128, 640), row),
        out_shape=spec(512, 640, bf16),
        compiler_params=params(10),
        cost_estimate=cost(4_000_000, 5_000_000),
    )(own, back_own, returned, back_middle, gains)


def rope_tables(offsets):
    powers = jnp.arange(128, dtype=f32) * (2.0 / 256)
    row = jnp.arange(512, dtype=jnp.int32)
    every = jnp.concatenate([offsets[0] - 512 + row, offsets])
    angles = every.astype(f32)[:, None] * (rope_base ** (-powers))[None, :]
    return jnp.cos(angles), jnp.sin(angles)


def unpack_kernel(spot, a0, a1, a2, a3, b0, b1, b2, b3, *rest):
    outs, gains, held, (ffn, attn, semaphores) = rest[:7], rest[7], rest[8:15], rest[15:]
    q, k, v, out, gate, up, down = held
    x, y = spot[0], spot[1]
    copies = []
    for half, pieces in enumerate(((a0, a1, a2, a3), (b0, b1, b2, b3))):
        for i in range(4):
            for j in range(4):
                first, second = (x, y) if half == 0 else (y, x)
                block = 16 * half + lax.rem(first - i + 4, 4) * 4 + lax.rem(second - j + 4, 4)
                n = (half * 4 + i) * 4 + j
                for m, (into, start, rows) in enumerate(((ffn, 0, 240), (attn, 240, 112))):
                    copies.append(
                        pltpu.make_async_copy(
                            pieces[i].at[j, pl.ds(start, rows), :],
                            into.at[pl.ds(pl.multiple_of(block * rows, 16), rows), :],
                            semaphores.at[2 * n + m],
                        )
                    )
    for copy in copies:
        copy.start()
    for copy in copies:
        copy.wait()
    outward = []

    def leave(n):
        copy = pltpu.make_async_copy(held[n], outs[n], semaphores.at[64 + n])
        copy.start()
        outward.append(copy)

    for n, into, flat, first, count in (
        (4, gate, ffn, 0, 16),
        (5, up, ffn, 2560, 16),
        (0, q, attn, 0, 8),
        (1, k, attn, 1280, 2),
        (2, v, attn, 1600, 2),
    ):
        for b in range(count):
            at = first + 160 * b
            into[:, 128 * b : 128 * b + 128] = flat[at : at + 160, :].astype(f32)
        leave(n)
    for n, into, flat, first, count in ((6, down, ffn, 5120, 4), (3, out, attn, 1920, 2)):
        for b in range(count):
            at = first + 640 * b
            into[128 * b : 128 * b + 128, :] = flat[at : at + 640, :].astype(f32).T
        leave(n)
    gains[...] = attn[3200:3216, :].astype(f32)
    for copy in outward:
        copy.wait()


def unpack(spot, pieces):
    shapes = [(160, 1024), (160, 256), (160, 256), (256, 640), (160, 2048), (160, 2048), (512, 640)]
    return pl.pallas_call(
        unpack_kernel,
        name="unpack",
        in_specs=[pl.BlockSpec(memory_space=pltpu.SMEM)] + [pl.BlockSpec(memory_space=pltpu.HBM)] * 8,
        out_specs=[pl.BlockSpec(memory_space=pltpu.HBM)] * 7 + [whole()],
        out_shape=[spec(*shape, f32) for shape in shapes] + [spec(16, 128, f32)],
        scratch_shapes=[pltpu.VMEM(shape, f32) for shape in shapes]
        + [
            pltpu.VMEM((7680, 128), bf16),
            pltpu.VMEM((3584, 128), bf16),
            pltpu.SemaphoreType.DMA((71,)),
        ],
        compiler_params=params(14),
        cost_estimate=cost(4_000_000, 11_000_000),
    )(spot, *pieces)


def sum_of(parts):
    whole = parts[0].astype(f32)
    for part in parts[1:]:
        whole = whole + part.astype(f32)
    return whole.astype(bf16)


def paired(parts):
    return [part for pair in zip(parts[:4], parts[4:]) for part in pair]


def turn_around(position, d):
    return lax.rem(position + d, 4)


def first_kernel(spot, kept_ffn, got_ffn, kept_attn, got_attn, *outs):
    for half in range(2):
        for i, d in enumerate((0, 1, 3, 2)):
            at = turn_around(spot[half], d)
            out = outs[4 * half + i]
            for z in range(2):
                for j in range(4):
                    out[z, j, :240] = sum_of([r[z, half, at, j] for r in (kept_ffn, got_ffn)])
                    out[z, j, 240:] = sum_of([r[z, half, at, j] for r in (kept_attn, got_attn)])


def first_sums(spot, kept_ffn, got_ffn, kept_attn, got_attn):
    ins = [p.reshape(2, 2, 4, 4, p.shape[1] // 32, 128) for p in (kept_ffn, got_ffn, kept_attn, got_attn)]
    return pl.pallas_call(
        first_kernel,
        name="first_sums",
        in_specs=[pl.BlockSpec(memory_space=pltpu.SMEM)] + [whole()] * 4,
        out_specs=[whole()] * 8,
        out_shape=[spec(2, 4, 352, 128, bf16)] * 8,
        compiler_params=params(24),
        cost_estimate=cost(3_000_000, 17_000_000),
    )(spot, *ins)


def second_kernel(spot, *refs):
    ins, outs = refs[:8], refs[8:]
    for half in range(2):
        parts = ins[half::2]
        for i, d in enumerate((0, 1, 3, 2)):
            at = turn_around(spot[1 - half], d)
            for z in range(2):
                outs[4 * half + i][z] = sum_of([r[z, at] for r in parts])


def second_sums(spot, parts):
    return pl.pallas_call(
        second_kernel,
        name="second_sums",
        in_specs=[pl.BlockSpec(memory_space=pltpu.SMEM)] + [whole()] * 8,
        out_specs=[whole()] * 8,
        out_shape=[spec(2, 352, 128, bf16)] * 8,
        compiler_params=params(12),
        cost_estimate=cost(1_000_000, 7_200_000),
    )(spot, *paired(parts))


def third_kernel(place, *refs):
    ins, (mine, other) = refs[:8], refs[8:]
    z = lax.div(place[0], 2)
    for half in range(2):
        parts = ins[half::2]
        mine[half] = sum_of([r[z] for r in parts])
        other[half] = sum_of([r[1 - z] for r in parts])


def third_sums(place, parts):
    return pl.pallas_call(
        third_kernel,
        name="third_sums",
        in_specs=[pl.BlockSpec(memory_space=pltpu.SMEM)] + [whole()] * 8,
        out_specs=[whole()] * 2,
        out_shape=[spec(2, 352, 128, bf16)] * 2,
        compiler_params=params(10),
        cost_estimate=cost(1_000_000, 1_800_000),
    )(place, *paired(parts))


def fourth_kernel(p0, p1, p2, p3, a, b):
    for half, out in enumerate((a, b)):
        out[...] = sum_of([p0[half], p1[half], p2[half], p3[half]])


def fourth_sums(parts):
    return pl.pallas_call(
        fourth_kernel,
        name="fourth_sums",
        in_specs=[whole()] * 4,
        out_specs=[whole()] * 2,
        out_shape=[spec(352, 128, bf16)] * 2,
        compiler_params=params(10),
        cost_estimate=cost(1_000_000, 900_000),
    )(*parts)


def seq_index(z, x, y):
    return (z % 2 * 4 + x % 4) * 4 + y % 4


def along_xy(dx, dy):
    return [
        (seq_index(z, x, y), seq_index(z, x + dx, y + dy))
        for z in range(2)
        for x in range(4)
        for y in range(4)
    ]


def along_z(step):
    pairs = []
    for s in range(32):
        for f in range(4):
            z = s // 16 * 2 + f // 2
            t = step(z)
            pairs.append((s * 4 + f, (t // 2 * 16 + s % 16) * 4 + t % 2 * 2 + f % 2))
    return pairs


def swap_core(value):
    return lax.ppermute(value, "fsdp", [(0, 1), (1, 0), (2, 3), (3, 2)])


def swap_near(value):
    return lax.ppermute(value, "fsdp", [(0, 2), (1, 3), (2, 0), (3, 1)])


def swap_across(value):
    return lax.ppermute(value, "fsdp", [(0, 3), (1, 2), (2, 1), (3, 0)])


def swap_far(value):
    return lax.ppermute(value, ("seq", "fsdp"), along_z(lambda z: 3 - z))


def swap_hi(value):
    return lax.ppermute(value, "seq", [(s, (s + 16) % 32) for s in range(32)])


def move_x(value, d):
    return lax.ppermute(value, "seq", along_xy(d, 0))


def move_y(value, d):
    return lax.ppermute(value, "seq", along_xy(0, d))


def shifted(value, steps):
    first, last = (max(0, -steps), min(32, 32 - steps))
    return lax.ppermute(value, "seq", [(source, source + steps) for source in range(first, last)])


steps = (1, 3, 2)


def move_first(parts):
    moved = list(parts)
    for i, d in zip((1, 2, 3), steps):
        moved[i] = move_x(parts[i], d)
        moved[4 + i] = move_y(parts[4 + i], d)
    return moved


def move_second(parts):
    moved = list(parts)
    for i, d in zip((1, 2, 3), steps):
        moved[i] = move_y(parts[i], d)
        moved[4 + i] = move_x(parts[4 + i], d)
    return moved


def together(*groups):
    leaves, tree = jax.tree.flatten(groups)
    return jax.tree.unflatten(tree, lax.optimization_barrier(tuple(leaves)))


def body(
    hidden_in,
    cotangent,
    positions,
    query_weight,
    key_weight,
    value_weight,
    output_weight,
    gate_weight,
    up_weight,
    down_weight,
    norm_in,
    norm_attn,
    norm_ffn_in,
    norm_ffn_out,
    norm_query,
    norm_key,
):
    s = lax.axis_index("seq")
    f = lax.axis_index("fsdp")
    x, y, z_lo, core = s // 4 % 4, s % 4, f // 2, f % 2
    place = f.astype(jnp.int32).reshape(1)
    spot = jnp.stack([x, y]).astype(jnp.int32)
    own = hidden_in[0]
    upstream = cotangent[0]
    offsets = positions[0]

    q_partner = swap_near(query_weight)
    kv = jnp.concatenate([key_weight, value_weight], axis=1)
    kv_partner = swap_far(kv)
    halo = shifted(own, 1)
    rows = (norm_in, norm_attn, norm_ffn_in, norm_ffn_out, norm_query, norm_key)
    q_partner, rows = together(q_partner, rows)
    tile = pack(rows)
    tiles = [tile, swap_core(tile), swap_near(tile), swap_across(tile)]
    tiles, wg, wu = together(tiles, gate_weight, up_weight)
    wg_partner, wu_partner = swap_near(wg), swap_far(wu)
    tiles = [
        jnp.where(
            j // 2 == z_lo,
            jnp.where(j % 2 == core, tiles[0], tiles[1]),
            jnp.where(j % 2 == core, tiles[2], tiles[3]),
        )
        for j in range(4)
    ]
    gains = jnp.concatenate([t[:, :160] for t in tiles], axis=1)
    head_gains = jnp.concatenate([t[:, :64] for t in tiles], axis=1)
    q_shares = (query_weight, swap_core(query_weight), q_partner, swap_core(q_partner))
    kv_shares = (kv, swap_core(kv), kv_partner, swap_core(kv_partner))
    q_shares, kv_shares, halo, wo, wd = together(
        q_shares, kv_shares, halo, output_weight, down_weight
    )
    wo_partner, wd_partner = swap_near(wo), swap_far(wd)

    cosine, sine = rope_tables(offsets)
    column = offsets[:, None]
    normed, q, k, v, q_proj, k_proj = project(
        place, halo, own, gains, head_gains, q_shares, kv_shares, cosine, sine
    )
    (q, k, v), wg_partner, wu_partner = together((q, k, v), wg_partner, wu_partner)
    attended, level = attend(q, k, v, column)
    own_weights = (wo, wg, wu, wd)
    partners = (wo_partner, wg_partner, wu_partner, wd_partner)
    attended, own_weights = together(attended, own_weights)
    siblings = [swap_core(w) for w in own_weights]
    shares = []
    for share, sibling, partner in zip(own_weights, siblings, partners):
        attended, partner = together(attended, partner)
        shares += [share, sibling, partner, swap_core(partner)]
    layer_out, back_middle, back_attn, back_attended, gain_mid, kept, sent = middle_part(
        place, own, attended, upstream, gains, shares
    )
    got = swap_core(sent)
    back_q, back_kv, gain_head, back_halo = attend_back(
        q,
        k,
        v,
        column,
        level,
        back_attended,
        q_proj,
        k_proj,
        head_gains,
        cosine,
        sine,
        place,
        kv_shares,
    )
    back_own, kept_attn, sent = weights_part(
        place,
        normed,
        back_q,
        back_kv,
        attended,
        back_attn,
        halo,
        own,
        gain_mid,
        gain_head,
        q_shares + kv_shares,
    )
    got_attn = swap_core(sent)
    first = move_first(first_sums(spot, kept, got, kept_attn, got_attn))
    mine, other = third_sums(place, move_second(second_sums(spot, first)))
    returned = shifted(back_halo, -1)
    a, b = fourth_sums([mine, swap_near(other), swap_far(other), swap_hi(mine)])
    a, b, returned = together(a, b, returned)
    a = jnp.stack([a] + [move_y(a, d) for d in (1, 2, 3)])
    b = jnp.stack([b] + [move_x(b, d) for d in (1, 2, 3)])
    a, b = together(a, b)
    pieces = [a] + [move_x(a, d) for d in (1, 2, 3)] + [b] + [move_y(b, d) for d in (1, 2, 3)]
    grad_q, grad_k, grad_v, grad_o, grad_g, grad_u, grad_d, tile = unpack(spot, pieces)
    grad_in = finish(own, back_own, returned, back_middle, gains)
    wide = jnp.concatenate([tile[0:4], tile[4:8, :32]], axis=1)
    return (
        layer_out[None],
        grad_in[None],
        grad_q,
        grad_k,
        grad_v,
        grad_o,
        grad_g,
        grad_u,
        grad_d,
        wide[0],
        wide[1],
        wide[2],
        wide[3],
        tile[8, :64],
        tile[9, :64],
    )


def solution(mesh):
    three = P("fsdp", "seq", None)
    two = P("fsdp", None)
    one = P("fsdp")
    return jax.shard_map(
        body,
        mesh=mesh,
        in_specs=(three, three, P("fsdp", "seq")) + (two,) * 7 + (one,) * 6,
        out_specs=(three, three) + (two,) * 7 + (one,) * 6,
        check_vma=False,
    )
```
